128 devices in a mesh: section: 2 (over core), dp: 16 (over x, y), tensor: 4 (over z).
Axes of the slice: x: 4, y: 4, z: 4, core: 2. Of those that a mesh axis runs over, the one named last changes fastest.
Arguments:
- tokens: bfloat16 [4096, 768], P('dp'), may hold values from -6 to 6
- cotangent: bfloat16 [4096, 768], P('dp'), may hold values from -6 to 6
- norm_gains: bfloat16 [2, 2, 768], P('section'), may hold values from 0.5 to 1.5
- w_qkv: bfloat16 [2, 3, 768, 768], P('section', None, None, 'tensor'), may hold values from -0.21875 to 0.21875
- w_attn_out: bfloat16 [2, 768, 768], P('section', 'tensor'), may hold values from -0.875 to 0.875
- bias_table: bfloat16 [2, 16, 12], P('section', None, 'tensor'), may hold values from -4 to 4
- router: bfloat16 [2, 768, 32], P('section'), may hold values from -0.15625 to 0.15625
- w_in: bfloat16 [2, 32, 768, 3072], P('section', 'dp', None, 'tensor'), may hold values from -0.21875 to 0.21875
- w_out: bfloat16 [2, 32, 3072, 768], P('section', 'dp', 'tensor'), may hold values from -0.21875 to 0.21875
- routes: int32 [2, 4096, 2], P('section', 'dp'), may hold values from 0 to 31, all different within a row; in each aligned block of 128 rows (0 to 127, 128 to 255, ..., all dimensions but the last counted through in order) at most 12 rows name the same one
- segments: int32 [32, 128], P('dp'), may hold values from 0 to 3, never falling along the last dimension, each value on 1 to 64 neighbouring positions
Outputs:
- activations: bfloat16 [2, 4096, 768], P('section', 'dp')
- input_grads: float32 [2, 4096, 768], P('section', 'dp')
- gain_grads: float32 [2, 2, 768], P('section')
- qkv_grads: float32 [2, 3, 768, 768], P('section', None, None, 'tensor')
- attn_out_grads: float32 [2, 768, 768], P('section', 'tensor')
- bias_grads: float32 [2, 16, 12], P('section', None, 'tensor')
- router_grads: float32 [2, 768, 32], P('section')
- w_in_grads: float32 [2, 32, 768, 3072], P('section', 'dp', None, 'tensor')
- w_out_grads: float32 [2, 32, 3072, 768], P('section', 'dp', 'tensor')
The draws below stay inside these ranges and needn't reach their ends.
Inputs may be any that keep to these rules, and one draw needn't show every extreme that they name: `routes`: within each aligned block of 128 rows of one layer (one micro-batch of one data group), no expert is named by more than 12 rows, and in some block an expert is named by exactly 12; a row names two different experts. `segments`: along a row the sequence numbers never fall; each sequence spans 1 to 64 positions, and one spans exactly that many.
All inputs are finite; a program needn't handle non-finite values.
Results may differ from the reference program's by a relative error of at most 0.04.
Values may be sent and summed in bfloat16 or wider, within the bound.
A program may use at most 128 MiB of HBM per device.

```python
import math
import jax
import jax.numpy as jnp
import numpy as np
from jax import lax

D = 768
HEADS = 12
HEAD_DIM = 64
FF = 3072
HDIM = 768
EXPERTS = 32
MB_TOK = 128
MICRO = 2
SEGS = 4
BUCKETS = 16
CAP = 12
TOKENS = 4096
N_DP = 16


def level_of(key, dims, shards, least, high):
    def one(dim, blocks):
        steps = jax.random.uniform(jax.random.fold_in(jax.random.fold_in(key, 6), dim), (blocks,), jnp.float32, least / len(shards), high / len(shards))
        return jnp.repeat(jnp.exp(steps), dims[dim] // blocks).reshape((-1,) + (1,) * (len(dims) - dim - 1))

    gain = one(*shards[0])
    for cut in shards[1:]:
        gain = gain * one(*cut)
    return gain


def length_profile(number_of, total, limit, slope):
    portions = [(1 << 20) // math.isqrt(grade ** slope) + 1 for grade in range(2, number_of + 1)]
    spare, given = total - limit - (number_of - 1), [1] * (number_of - 1)
    while spare > 0:
        movable = [i for i in range(number_of - 1) if given[i] < limit]
        whole, remaining = sum([portions[i] for i in movable]), spare
        for i in movable:
            extra = min(limit - given[i], max(1, remaining * portions[i] // whole), spare)
            given[i] = given[i] + extra
            spare = spare - extra
    return np.array([limit] + given)


def ragged(stream_key, count, total, most, skew):
    if count == 2:
        one = jax.random.randint(stream_key, (), max(1, total - most), min(most, total - 1) + 1)
        return jnp.stack([one, total - one])
    tallies = jnp.asarray(length_profile(count, total, most, skew), jnp.int32)
    twos = (count - 1) // 2
    giver, taker = tallies[1:1 + 2 * twos:2], tallies[2:2 + 2 * twos:2]
    slack = jnp.minimum(giver - 1, most - taker)
    passed = jax.random.randint(jax.random.fold_in(stream_key, 1), (twos,), 0, 1 << 20) % (slack + 1)
    tallies = tallies.at[1:1 + 2 * twos:2].set(giver - passed).at[2:2 + 2 * twos:2].set(taker + passed)
    return tallies[jax.random.permutation(jax.random.fold_in(stream_key, 2), count)]


def deal_out(rng, own, number, rows, count, top, limit, slope):
    order = jax.random.permutation(rng, count)
    packed, common = shares(count, rows * top, limit, slope, True), shares(count, rows * top, limit, slope, False)
    places = jnp.arange(count)

    def named(sizes, turn):
        used = int((sizes > 0).sum())
        fixed = max(1, used // 4)
        moved = fixed + (places - fixed + turn * (used - fixed)) % max(1, count - fixed)
        return jnp.zeros((count,), jnp.int32).at[order[jnp.where(places < fixed, places, moved)]].set(jnp.asarray(sizes, jnp.int32))

    sizes = jnp.where(number % 4 == 0, named(packed, number // 4), named(common, number - number // 4 - 1))
    mixed = jax.random.permutation(jax.random.fold_in(own, 3), count)
    source_of, sink = mixed[0:count // 2 * 2:2], mixed[1:count // 2 * 2:2]
    room = jnp.minimum(sizes[source_of] - 1, limit - sizes[sink]) // 2
    room = jnp.where((source_of == order[0]) | (sink == order[0]) | (sizes[sink] == 0), 0, jnp.maximum(room, 0))
    moved = jax.random.randint(jax.random.fold_in(own, 4), (count // 2,), 0, 1 << 20) % (room + 1)
    sizes = sizes.at[source_of].add(-moved).at[sink].add(moved)
    members = jnp.searchsorted(jnp.cumsum(sizes), jnp.arange(rows * top), side="right").astype(jnp.int32)
    grid = members.reshape(top, rows).T
    grid = grid[jax.random.permutation(jax.random.fold_in(own, 1), rows)]
    turn = jax.random.randint(jax.random.fold_in(own, 2), (rows, 1), 0, top)
    return jnp.take_along_axis(grid, (jnp.arange(top)[None, :] + turn) % top, axis=1)


def shares(amount, total, most, lean, full):
    portions = [(1 << 20) // math.isqrt(rank ** lean) + 1 for rank in range(1, amount + 1)]
    largest = most if full else min(most, max(-(-total // amount), total * portions[0] // sum(portions)))
    least = 1 if total - largest >= amount - 1 else 0
    holding, rest = [largest] + [least] * (amount - 1), total - largest - least * (amount - 1)
    while rest > 0:
        movable = [i for i in range(1, amount) if holding[i] < largest] or [i for i in range(1, amount) if holding[i] < most]
        pool, budget = sum([portions[i] for i in movable]), rest
        for i in movable:
            extra = min(most - holding[i], max(1, budget * portions[i] // pool), rest)
            holding[i] = holding[i] + extra
            rest = rest - extra
    return np.array(holding)


def bell_draw(stream_key, extent, scale, reach, cuts=(), held_as=jnp.bfloat16):
    factor_of = level_of(stream_key, extent, cuts, -0.22, 0.18) if cuts else 1.0
    drawn = jax.random.normal(stream_key, extent, jnp.float32) * scale * factor_of
    return jnp.minimum(jnp.maximum(drawn, -reach), reach).astype(held_as)


def setup_inputs(seed: int = 0) -> dict:
    key_of = jax.random.split(jax.random.key(seed), 12)
    tokens = bell_draw(key_of[0], (TOKENS, D), 1.0, 6.0, ((0, 16),))
    cotangent = bell_draw(key_of[1], (TOKENS, D), 1.0, 6.0, ((0, 16),))
    norm_gains = jnp.clip(1.0 + 0.1 * jax.random.normal(key_of[2], (2, 2, D), jnp.float32), 0.5, 1.5).astype(jnp.bfloat16)
    w_qkv = bell_draw(key_of[3], (2, 3, D, HDIM), D ** -0.5, 0.21875, ((0, 2), (3, 4)))
    w_attn_out = bell_draw(key_of[4], (2, HDIM, D), (HDIM // 16) ** -0.5, 0.875, ((0, 2), (1, 4)))
    bias_table = bell_draw(key_of[5], (2, BUCKETS, HEADS), 1.0, 4.0, ((0, 2), (2, 4)))
    router = bell_draw(key_of[6], (2, D, EXPERTS), (2 * D) ** -0.5, 0.15625, ((0, 2),))
    w_in = bell_draw(key_of[7], (2, EXPERTS, D, FF), D ** -0.5, 0.21875, ((0, 2), (1, 16), (3, 4)))
    w_out = bell_draw(key_of[8], (2, EXPERTS, FF, D), (FF // 4) ** -0.5, 0.21875, ((0, 2), (1, 16), (2, 4)))
    routes_keys = jax.random.split(jax.random.fold_in(key_of[9], 1), 2 * TOKENS // MB_TOK)
    routes_turns = jax.random.permutation(jax.random.fold_in(key_of[9], 3), 2 * TOKENS // MB_TOK)
    routes = jax.vmap(lambda own, number: deal_out(jax.random.fold_in(key_of[9], 2), own, number, MB_TOK, EXPERTS, 2, CAP, 1))(routes_keys, routes_turns).reshape((2, TOKENS, 2))
    segments = jax.vmap(lambda own: jnp.searchsorted(jnp.cumsum(ragged(own, SEGS, MB_TOK, MB_TOK // 2, 2)), jnp.arange(MB_TOK), side="right"))(jax.random.split(key_of[10], (MICRO * N_DP))).reshape((MICRO * N_DP, MB_TOK)).astype(jnp.int32)
    return {"tokens": tokens, "cotangent": cotangent, "norm_gains": norm_gains, "w_qkv": w_qkv, "w_attn_out": w_attn_out, "bias_table": bias_table, "router": router, "w_in": w_in, "w_out": w_out, "routes": routes, "segments": segments}


@jax.custom_vjp
def low(v):
    return lax.optimization_barrier(v.astype(jnp.bfloat16)).astype(jnp.float32)

@jax.custom_vjp
def reduced_precision_return(v):
    return v

def low_keep(v):
    return (low(v), None)

def low_pass(kept, grad):
    return (grad,)

def back_keep(v):
    return (v, None)

def back_low(kept, grad):
    return (low(grad),)
low.defvjp(low_keep, low_pass)
reduced_precision_return.defvjp(back_keep, back_low)
epsilon = 1e-06
masked_score = -1000000000.0
bucket_edges = (1, 2, 3, 4, 5, 6, 7, 8, 10, 13, 16, 20, 25, 32, 40)

def round_both(values):
    return low(reduced_precision_return(values))

def rms_scale(values):
    return lax.rsqrt(lax.optimization_barrier(jnp.mean(values * values, axis=-1, keepdims=True)) + epsilon)

def block_layer(values, gain_pair, qkv_weight, attn_weight, position_bias_rows, router_weight, inner_weight, outer_weight, route_pairs, segment_row):
    highest = lax.Precision.HIGHEST
    row_count = values.shape[0]
    normed = low(values * rms_scale(values) * gain_pair[0])
    qkv_rows = round_both(jnp.einsum('td,jdf->jtf', normed, qkv_weight, precision=highest))
    heads_view = qkv_rows.reshape(3, row_count, HEADS, HEAD_DIM)
    scores = jnp.einsum('qhc,khc->hqk', heads_view[0], heads_view[1], precision=highest) * HEAD_DIM ** (-0.5)
    position = jnp.arange(row_count, dtype=jnp.int32)
    distance = jnp.maximum(position[:, None] - position[None, :], 0)
    bucket = lax.optimization_barrier(jnp.sum((distance[:, :, None] >= jnp.asarray(bucket_edges, jnp.int32)).astype(jnp.int32), axis=-1))
    allowed = (position[:, None] >= position[None, :]) & (segment_row[:, None] == segment_row[None, :])
    relative_bias_value = jnp.transpose(position_bias_rows[bucket], (2, 0, 1))
    scores = reduced_precision_return(jnp.where(allowed[None], scores + relative_bias_value, masked_score))
    attn_probs = jax.nn.softmax(scores, axis=-1)
    context = round_both(jnp.einsum('hqk,khc->qhc', low(attn_probs), heads_view[2], precision=highest))
    context = context.reshape(row_count, HEADS * HEAD_DIM)
    hidden = values + reduced_precision_return(jnp.dot(context, attn_weight, precision=highest))
    normed_ffn = low(hidden * rms_scale(hidden) * gain_pair[1])
    logits = reduced_precision_return(jnp.dot(normed_ffn, router_weight, precision=highest))
    gate_values = jax.nn.softmax(jnp.take_along_axis(logits, route_pairs, axis=1), axis=-1)
    expert_ids = route_pairs.reshape(-1)
    expert_hits = (expert_ids[:, None] == jnp.arange(EXPERTS, dtype=jnp.int32)[None, :]).astype(jnp.int32)
    slot_rank = lax.optimization_barrier(jnp.sum((jnp.cumsum(expert_hits, axis=0) - expert_hits) * expert_hits, axis=1)).astype(jnp.int32)
    copies = reduced_precision_return(jnp.repeat(normed_ffn, 2, axis=0))
    buffer = jnp.zeros((EXPERTS, CAP, D), jnp.float32).at[expert_ids, slot_rank].set(copies)
    pre_act = reduced_precision_return(jnp.einsum('ecd,edf->ecf', buffer, inner_weight, precision=highest))
    activation = low(jax.nn.gelu(pre_act, approximate=True))
    expert_out = round_both(jnp.einsum('ecf,efd->ecd', activation, outer_weight, precision=highest))
    returned = expert_out[expert_ids, slot_rank].reshape(row_count, 2, D)
    moe_out = lax.optimization_barrier(jnp.sum(returned * gate_values[:, :, None], axis=1))
    return round_both(hidden + moe_out)

def reference(tokens, cotangent, norm_gains, w_qkv, w_attn_out, bias_table, router, w_in, w_out, routes, segments):
    blocks = segments.shape[0]
    pair_blocks = jnp.transpose(routes.reshape(2, blocks, MB_TOK, 2), (1, 0, 2, 3))

    def forward(token_rows, middle_rows, gain_set, qkv_set, attn_set, bias_set, router_set, inner_set, outer_set):

        def one_block(items_in):
            block_in, block_mid, block_pairs, segment_row = items_in
            first_out = block_layer(block_in, gain_set[0], qkv_set[0], attn_set[0], bias_set[0], router_set[0], inner_set[0], outer_set[0], block_pairs[0], segment_row)
            second_out = block_layer(first_out + block_mid, gain_set[1], qkv_set[1], attn_set[1], bias_set[1], router_set[1], inner_set[1], outer_set[1], block_pairs[1], segment_row)
            return jnp.stack([first_out, second_out])
        stacked = lax.map(jax.checkpoint(one_block), (token_rows.reshape(blocks, MB_TOK, D), middle_rows.reshape(blocks, MB_TOK, D), pair_blocks, segments))
        return jnp.transpose(stacked, (1, 0, 2, 3)).reshape(2, blocks * MB_TOK, D)
    token_rows = tokens.astype(jnp.float32)
    middle_rows = jnp.zeros((TOKENS, D), jnp.float32)
    outputs, pull_back = jax.vjp(forward, token_rows, middle_rows, norm_gains.astype(jnp.float32), w_qkv.astype(jnp.float32), w_attn_out.astype(jnp.float32), bias_table.astype(jnp.float32), router.astype(jnp.float32), w_in.astype(jnp.float32), w_out.astype(jnp.float32))
    seed_grad = jnp.stack([jnp.zeros((TOKENS, D), jnp.float32), cotangent.astype(jnp.float32)])
    gradients = pull_back(seed_grad)
    input_grads = jnp.stack([gradients[0], gradients[1]])
    return (outputs.astype(jnp.bfloat16), input_grads, gradients[2], gradients[3], gradients[4], gradients[5], gradients[6], gradients[7], gradients[8])
```

```python
import jax
import jax.numpy as jnp
from jax import lax
from jax.experimental import pallas as pl
from jax.experimental.pallas import tpu as pltpu
from jax.sharding import PartitionSpec as P

epsilon = 1e-06
masked_score = -1000000000.0
bucket_edges = (1, 2, 3, 4, 5, 6, 7, 8, 10, 13, 16, 20, 25, 32, 40)
MESH = pl.DeviceIdType.MESH
f32 = jnp.float32
bf16 = jnp.bfloat16

DP = 16
TZ = 4
ROWS = 256
BLOCK = 128
OWN = ROWS // TZ
D = 768
HF = 192
HEADS = 3
CAP = 12
MSG = 48
SLOTS = DP * MSG
ER = SLOTS // 2
SMALL = 128
GAIN0, GAIN1, BIAS = 33, 32, 34


def nn(a, b):
    return lax.dot_general(a, b, (((1,), (0,)), ((), ())), preferred_element_type=f32)


def nt(a, b):
    return lax.dot_general(a, b, (((1,), (1,)), ((), ())), preferred_element_type=f32)


def tn(a, b):
    return lax.dot_general(a, b, (((0,), (0,)), ((), ())), preferred_element_type=f32)


def iota(shape, dim):
    return lax.broadcasted_iota(jnp.int32, shape, dim)


def rms_scale(values):
    return lax.rsqrt(jnp.mean(values * values, axis=-1, keepdims=True) + epsilon)


def kernel(
    tokens, cotangent, gains, w_qkv, w_att, bias_tab, router, w_in_hbm, w_out_hbm, routes, segments,
    act_out, grad_out, dense_out, small_out, xe_out, u_out, dpre_out, de_out,
    xin, gin, w_in, w_out, wall, call, normed, qkv, probs, hidden, hid_scale, normed2, rpad,
    gate, slots, ptg, send_b, recv_b, send_e, recv_e, send_d, recv_d, send_x, recv_x,
    xe, act, dact, de, dpre, yf, part_y, rs_y, part_h, rs_h, dh_full, part_a, rs_a, in_full,
    dq_all, gact, dense_s, dense_r, dense_f, small_z, small_f,
    ld_sem, out_sem, w_ss, w_rs, c_ss, c_rs, b_ss, b_rs, e_ss, e_rs, d_ss, d_rs, x_ss, x_rs,
    ry_ss, ry_rs, ay_ss, ay_rs, rh_ss, rh_rs, ah_ss, ah_rs, ra_ss, ra_rs, aa_ss, aa_rs,
    hand_ss, hand_rs, back_ss, back_rs, dn_ss, dn_rs, df_ss, df_rs, sz_ss, sz_rs, sf_ss, sf_rs,
    turn_sem,
):
    sec = lax.axis_index("section")
    me = lax.axis_index("dp")
    mz = lax.axis_index("tensor")
    first = sec == 0

    load_in = pltpu.make_async_copy(w_in_hbm, w_in, ld_sem.at[0])
    load_out = pltpu.make_async_copy(w_out_hbm, w_out, ld_sem.at[1])
    load_in.start()
    load_out.start()

    barrier = pltpu.get_barrier_semaphore()

    def greet(i, carry):
        pl.semaphore_signal(
            barrier, inc=1, device_id={"dp": lax.rem(me + i, DP)}, device_id_type=MESH
        )
        return carry

    lax.fori_loop(1, DP, greet, 0)
    for i in range(1, TZ):
        pl.semaphore_signal(
            barrier, inc=1, device_id={"tensor": lax.rem(mz + i, TZ)}, device_id_type=MESH
        )
    pl.semaphore_signal(barrier, inc=1, device_id={"section": 1 - sec}, device_id_type=MESH)
    pl.semaphore_wait(barrier, DP + TZ - 1)

    def z_copy(src, dst, ss, rs, peer, slot):
        return pltpu.make_async_remote_copy(
            src_ref=src, dst_ref=dst, send_sem=ss.at[peer], recv_sem=rs.at[slot],
            device_id={"tensor": peer}, device_id_type=MESH,
        )

    def gather_start(buf, ss, rs):
        for i in range(1, TZ):
            z_copy(buf.at[mz], buf.at[mz], ss, rs, lax.rem(mz + i, TZ), mz).start()

    def gather_recv(buf, ss, rs, i):
        src = lax.rem(mz + i, TZ)
        z_copy(buf.at[src], buf.at[src], ss, rs, src, src).wait_recv()

    def gather_sent(buf, ss, rs):
        for i in range(1, TZ):
            z_copy(buf.at[mz], buf.at[mz], ss, rs, lax.rem(mz + i, TZ), mz).wait_send()

    def scatter_start(part, rcv, ss, rs):
        for i in range(1, TZ):
            peer = lax.rem(mz + i, TZ)
            z_copy(part.at[peer], rcv.at[mz], ss, rs, peer, mz).start()

    def scatter_sum(part, rcv, ss, rs):
        total = part[mz].astype(f32)
        for i in range(1, TZ):
            src = lax.rem(mz + i, TZ)
            z_copy(part.at[src], rcv.at[src], ss, rs, src, src).wait_recv()
            total += rcv[src].astype(f32)
        return total

    def scatter_sent(part, rcv, ss, rs):
        for i in range(1, TZ):
            peer = lax.rem(mz + i, TZ)
            z_copy(part.at[peer], rcv.at[mz], ss, rs, peer, mz).wait_send()

    def dp_copy(src, dst, ss, rs, peer, slot):
        return pltpu.make_async_remote_copy(
            src_ref=src, dst_ref=dst, send_sem=ss.at[peer], recv_sem=rs.at[slot],
            device_id={"dp": peer}, device_id_type=MESH,
        )

    def swap_one(snd, rcv, ss, rs, peer):
        @pl.when(peer != me)
        def _():
            dp_copy(snd.at[peer], rcv.at[me], ss, rs, peer, me).start()

    def swap_start(snd, rcv, ss, rs):
        rcv[me] = snd[me]

        def step(i, carry):
            swap_one(snd, rcv, ss, rs, lax.rem(me + i, DP))
            return carry

        lax.fori_loop(1, DP, step, 0)

    def swap_recv(snd, rcv, ss, rs, src):
        @pl.when(src != me)
        def _():
            dp_copy(snd.at[src], rcv.at[src], ss, rs, src, src).wait_recv()

    def swap_recv_all(snd, rcv, ss, rs):
        def step(i, carry):
            swap_recv(snd, rcv, ss, rs, lax.rem(me + DP - i, DP))
            return carry

        lax.fori_loop(1, DP, step, 0)

    def swap_sent(snd, rcv, ss, rs):
        def step(i, carry):
            peer = lax.rem(me + i, DP)
            dp_copy(snd.at[peer], rcv.at[me], ss, rs, peer, me).wait_send()
            return carry

        lax.fori_loop(1, DP, step, 0)

    def unpack(snd, rcv, ss, rs, rows):
        def step(i, carry):
            pair = lax.rem(me // 2 + DP // 2 - i, DP // 2)
            swap_recv(snd, rcv, ss, rs, 2 * pair)
            swap_recv(snd, rcv, ss, rs, 2 * pair + 1)
            one = rcv[2 * pair].astype(f32)
            two = rcv[2 * pair + 1].astype(f32)
            at = pl.ds(pl.multiple_of(pair * MSG, MSG), MSG)
            half = MSG // 2
            rows[0, at, :] = jnp.concatenate([one[:half], two[:half]], axis=0).astype(bf16)
            rows[1, at, :] = jnp.concatenate([one[half:], two[half:]], axis=0).astype(bf16)
            return carry

        lax.fori_loop(0, DP // 2, step, 0)

    def pack(snd, rcv, ss, rs):
        def step(i, carry):
            pair = lax.rem(me // 2 + i, DP // 2)
            at = pl.ds(pl.multiple_of(pair * MSG, MSG), MSG)
            half = MSG // 2
            one = yf[0, at, :]
            two = yf[1, at, :]
            snd[2 * pair] = jnp.concatenate([one[:half], two[:half]], axis=0).astype(bf16)
            snd[2 * pair + 1] = jnp.concatenate([one[half:], two[half:]], axis=0).astype(bf16)
            swap_one(snd, rcv, ss, rs, 2 * pair)
            swap_one(snd, rcv, ss, rs, 2 * pair + 1)
            return carry

        lax.fori_loop(0, DP // 2, step, 0)
        rcv[me] = snd[me]

    @pl.when(first)
    def _():
        wall[mz] = w_att[0]
        gather_start(wall, w_ss, w_rs)
        xin[...] = tokens[...].reshape(TZ, OWN, D)

    @pl.when(jnp.logical_not(first))
    def _():
        gin[...] = cotangent[...].reshape(TZ, OWN, D)
        pl.semaphore_wait(turn_sem, 1)
        wall[mz] = w_att[0]
        gather_start(wall, w_ss, w_rs)

    tok = iota((ROWS, ROWS), 0)
    oth = iota((ROWS, ROWS), 1)
    same = (tok // BLOCK) == (oth // BLOCK)
    earlier = (same & (tok > oth)).astype(f32).astype(bf16)
    within = same.astype(f32).astype(bf16)
    lane = iota((ROWS, SMALL), 1)
    e0 = routes[0][:, 0:1]
    e1 = routes[0][:, 1:2]
    hit0 = (lane == e0).astype(f32)
    hit1 = (lane == e1).astype(f32)
    rank0 = jnp.sum(nn(earlier, hit0.astype(bf16)) * hit0, axis=1, keepdims=True)
    rank1 = jnp.sum(
        (nn(earlier, hit1.astype(bf16)) + nn(within, hit0.astype(bf16))) * hit1,
        axis=1, keepdims=True,
    )
    base = (iota((ROWS, 1), 0) // BLOCK) * CAP
    slot0 = (e0 // 2) * MSG + (e0 % 2) * (MSG // 2) + base + rank0.astype(jnp.int32)
    slot1 = (e1 // 2) * MSG + (e1 % 2) * (MSG // 2) + base + rank1.astype(jnp.int32)
    slots[:, 0:1] = slot0
    slots[:, 1:2] = slot1
    rpad[...] = jnp.zeros((D, SMALL), bf16)
    rpad[:, 0:32] = router[0]

    @pl.when(jnp.logical_not(first))
    def _():
        for t in range(TZ):
            pltpu.make_async_remote_copy(
                src_ref=in_full.at[t], dst_ref=xin.at[t], send_sem=hand_ss.at[t],
                recv_sem=hand_rs.at[t], device_id={"section": 1 - sec}, device_id_type=MESH,
            ).wait_recv()

    x = xin[...].reshape(ROWS, D).astype(f32)
    gain0 = gains[0, 0:1, :].astype(f32)
    gain1 = gains[0, 1:2, :].astype(f32)
    normed[...] = (x * rms_scale(x) * gain0).astype(bf16)
    for j in range(3):
        qkv[j] = nn(normed[...], w_qkv[0, j]).astype(bf16)

    row = iota((BLOCK, BLOCK), 0)
    col = iota((BLOCK, BLOCK), 1)
    gap = row - col
    head_of = iota((BLOCK, HF), 1) // (HF // HEADS)
    bias_now = []
    for h in range(HEADS):
        value = jnp.broadcast_to(bias_tab[0, 0:1, h : h + 1].astype(f32), (BLOCK, BLOCK))
        for b, edge in enumerate(bucket_edges):
            value = jnp.where(gap >= edge, bias_tab[0, b + 1 : b + 2, h : h + 1].astype(f32), value)
        bias_now.append(value)
    for b in range(2):
        rows = slice(b * BLOCK, (b + 1) * BLOCK)
        seg_row = segments[b : b + 1, :].astype(f32)
        seg_col = jnp.sum(jnp.where(row == col, seg_row, 0.0), axis=1, keepdims=True)
        allowed = (gap >= 0) & (seg_row == seg_col)
        q = qkv[0, rows, :]
        k = qkv[1, rows, :]
        v = qkv[2, rows, :]
        context = jnp.zeros((BLOCK, HF), f32)
        for h in range(HEADS):
            score = nt(jnp.where(head_of == h, q, jnp.zeros_like(q)), k) * 0.125 + bias_now[h]
            score = jnp.where(allowed, score, masked_score)
            score = jnp.exp(score - jnp.max(score, axis=-1, keepdims=True))
            prob = score / jnp.sum(score, axis=-1, keepdims=True)
            probs[b * HEADS + h] = prob
            context = jnp.where(head_of == h, nn(prob.astype(bf16), v), context)
        call[mz, rows, :] = context.astype(bf16)
    gather_start(call, c_ss, c_rs)

    slot_lane = iota((ROWS, SLOTS), 1)
    eye = tok == oth
    row0 = jnp.sum(jnp.where(eye, slots[:, 0:1], 0), axis=0, keepdims=True)
    row1 = jnp.sum(jnp.where(eye, slots[:, 1:2], 0), axis=0, keepdims=True)
    slot_sub = iota((SLOTS, ROWS), 0)
    pick = ((slot_sub == row0) | (slot_sub == row1)).astype(f32).astype(bf16)

    for i in range(1, TZ):
        gather_recv(call, c_ss, c_rs, i)
        gather_recv(wall, w_ss, w_rs, i)

    @pl.when(first)
    def _():
        pl.semaphore_signal(turn_sem, inc=1, device_id={"section": 1 - sec}, device_id_type=MESH)

    h = xin[...].reshape(ROWS, D).astype(f32)
    for t in range(TZ):
        h += nn(call[t], wall[t])
    hidden[...] = h
    scale = rms_scale(h)
    hid_scale[...] = scale
    normed2[...] = (h * scale * gain1).astype(bf16)

    sent = nn(pick, normed2[...]).astype(bf16)
    send_b[...] = sent.reshape(DP, MSG, D)
    swap_start(send_b, recv_b, b_ss, b_rs)

    z = nn(normed2[...], rpad[...])
    z0 = jnp.sum(z * hit0, axis=1, keepdims=True)
    z1 = jnp.sum(z * hit1, axis=1, keepdims=True)
    g0 = 1.0 / (1.0 + jnp.exp(z1 - z0))
    g1 = 1.0 / (1.0 + jnp.exp(z0 - z1))
    gate[:, 0:1] = g0
    gate[:, 1:2] = g1
    ptg[...] = (
        jnp.where(slot_lane == slot0, g0, 0.0) + jnp.where(slot_lane == slot1, g1, 0.0)
    ).astype(bf16)

    def dispatch_grad():
        grow0 = jnp.sum(jnp.where(eye, gate[:, 0:1], 0.0), axis=0, keepdims=True)
        grow1 = jnp.sum(jnp.where(eye, gate[:, 1:2], 0.0), axis=0, keepdims=True)
        crow0 = jnp.sum(jnp.where(eye, slots[:, 0:1], 0), axis=0, keepdims=True)
        crow1 = jnp.sum(jnp.where(eye, slots[:, 1:2], 0), axis=0, keepdims=True)
        pick_g = jnp.where(slot_sub == crow0, grow0, 0.0) + jnp.where(slot_sub == crow1, grow1, 0.0)
        out = nn(pick_g.astype(bf16), gin[...].reshape(ROWS, D)).astype(bf16)
        send_d[...] = out.reshape(DP, MSG, D)
        swap_start(send_d, recv_d, d_ss, d_rs)

    @pl.when(jnp.logical_not(first))
    def _():
        dispatch_grad()

    unpack(send_b, recv_b, b_ss, b_rs, xe)
    load_in.wait()
    load_out.wait()
    save_xe = pltpu.make_async_copy(xe, xe_out, out_sem.at[0])
    save_xe.start()
    root = 0.7978845608028654

    def expert_forward(e, carry):
        for n in range(3):
            cols = slice(256 * n, 256 * (n + 1))
            pre = nn(xe[e], w_in[e, :, cols])
            square = pre * pre
            wave = jnp.tanh(root * pre * (1.0 + 0.044715 * square))
            lift = 0.5 * (1.0 + wave)
            act[e, :, cols] = (pre * lift).astype(bf16)
            slope = lift + 0.5 * root * pre * (1.0 - wave * wave) * (1.0 + 0.134145 * square)
            dact[e, :, cols] = slope.astype(bf16)
        yf[e] = nn(act[e], w_out[e])
        return carry

    lax.fori_loop(0, 2, expert_forward, 0)
    save_u = pltpu.make_async_copy(act, u_out, out_sem.at[1])
    save_u.start()
    pack(send_e, recv_e, e_ss, e_rs)

    def finish_forward():
        swap_recv_all(send_e, recv_e, e_ss, e_rs)
        part_y[...] = nn(ptg[...], recv_e[...].reshape(SLOTS, D)).astype(bf16).reshape(TZ, OWN, D)
        scatter_start(part_y, rs_y, ry_ss, ry_rs)
        own = pl.ds(pl.multiple_of(mz * OWN, OWN), OWN)
        total = scatter_sum(part_y, rs_y, ry_ss, ry_rs) + hidden[own, :]
        act_all = gact
        act_all[mz] = total.astype(bf16)
        gather_start(act_all, ay_ss, ay_rs)

    def hand(t, ss, rs, src, dst):
        return pltpu.make_async_remote_copy(
            src_ref=src.at[t], dst_ref=dst.at[t], send_sem=ss.at[t], recv_sem=rs.at[t],
            device_id={"section": 1 - sec}, device_id_type=MESH,
        )

    @pl.when(first)
    def _():
        finish_forward()
        hand(mz, hand_ss, hand_rs, gact, xin).start()
        for i in range(1, TZ):
            gather_recv(gact, ay_ss, ay_rs, i)
            hand(lax.rem(mz + i, TZ), hand_ss, hand_rs, gact, xin).start()
        for t in range(TZ):
            hand(t, back_ss, back_rs, in_full, gin).wait_recv()
        dispatch_grad()

    unpack(send_d, recv_d, d_ss, d_rs, de)
    save_de = pltpu.make_async_copy(de, de_out, out_sem.at[2])
    save_de.start()

    def expert_backward(e, carry):
        for n in range(3):
            cols = slice(256 * n, 256 * (n + 1))
            grad = nt(de[e], w_out[e, cols, :])
            dpre[e, :, cols] = (grad * dact[e, :, cols].astype(f32)).astype(bf16)
        yf[e] = nt(dpre[e], w_in[e])
        return carry

    lax.fori_loop(0, 2, expert_backward, 0)
    save_dpre = pltpu.make_async_copy(dpre, dpre_out, out_sem.at[3])
    save_dpre.start()
    pack(send_x, recv_x, x_ss, x_rs)

    @pl.when(jnp.logical_not(first))
    def _():
        finish_forward()
        for i in range(1, TZ):
            gather_recv(gact, ay_ss, ay_rs, i)

    act_out[...] = gact[...].reshape(ROWS, D)

    c0 = slots[:, 0:1]
    c1 = slots[:, 1:2]
    w0 = gate[:, 0:1]
    w1 = gate[:, 1:2]
    marks = nt(gin[...].reshape(ROWS, D), recv_e[...].reshape(SLOTS, D))
    dg0 = jnp.sum(jnp.where(slot_lane == c0, marks, 0.0), axis=1, keepdims=True)
    dg1 = jnp.sum(jnp.where(slot_lane == c1, marks, 0.0), axis=1, keepdims=True)
    mean = w0 * dg0 + w1 * dg1
    dz = (
        jnp.where(lane == routes[0][:, 0:1], w0 * (dg0 - mean), 0.0)
        + jnp.where(lane == routes[0][:, 1:2], w1 * (dg1 - mean), 0.0)
    ).astype(bf16)
    pick_t = ((slot_lane == c0) | (slot_lane == c1)).astype(f32).astype(bf16)

    swap_recv_all(send_x, recv_x, x_ss, x_rs)
    db = nn(pick_t, recv_x[...].reshape(SLOTS, D)) + nt(dz, rpad[...])
    part_h[...] = db.astype(bf16).reshape(TZ, OWN, D)
    scatter_start(part_h, rs_h, rh_ss, rh_rs)
    small = tn(normed2[...], dz)
    unit1 = (lane == GAIN1).astype(f32).astype(bf16)
    unit0 = (lane == GAIN0).astype(f32).astype(bf16)
    small += tn((db * hidden[...] * hid_scale[...]).astype(bf16), unit1)

    own = pl.ds(pl.multiple_of(mz * OWN, OWN), OWN)
    db_own = scatter_sum(part_h, rs_h, rh_ss, rh_rs)
    h_own = hidden[own, :]
    s_own = hid_scale[own, :]
    lifted = db_own * gain1
    hat = h_own * s_own
    dh_own = gin[mz].astype(f32) + s_own * (
        lifted - hat * jnp.mean(lifted * hat, axis=-1, keepdims=True)
    )
    dh_full[mz] = dh_own.astype(bf16)
    gather_start(dh_full, ah_ss, ah_rs)
    for i in range(1, TZ):
        gather_recv(dh_full, ah_ss, ah_rs, i)

    do = dh_full[...].reshape(ROWS, D)
    dc_all = nt(do, w_att[0]).astype(bf16)
    score_grads = [jnp.zeros((BLOCK, BLOCK), f32) for _ in range(HEADS)]
    for b in range(2):
        rows = slice(b * BLOCK, (b + 1) * BLOCK)
        q = qkv[0, rows, :]
        k = qkv[1, rows, :]
        v = qkv[2, rows, :]
        dc = dc_all[rows, :]
        dq = jnp.zeros((BLOCK, HF), f32)
        dk = jnp.zeros((BLOCK, HF), f32)
        dv = jnp.zeros((BLOCK, HF), f32)
        for h in range(HEADS):
            mine = head_of == h
            prob = probs[b * HEADS + h]
            dp = nt(jnp.where(mine, dc, jnp.zeros_like(dc)), v)
            ds = (prob * (dp - jnp.sum(prob * dp, axis=-1, keepdims=True))).astype(bf16)
            score_grads[h] += ds.astype(f32)
            dq = jnp.where(mine, nn(ds, k), dq)
            dk = jnp.where(mine, tn(ds, q), dk)
            dv = jnp.where(mine, tn(prob.astype(bf16), dc), dv)
        dq_all[0, rows, :] = (dq * 0.125).astype(bf16)
        dq_all[1, rows, :] = (dk * 0.125).astype(bf16)
        dq_all[2, rows, :] = dv.astype(bf16)
    da = nt(dq_all[0], w_qkv[0, 0]) + nt(dq_all[1], w_qkv[0, 1]) + nt(dq_all[2], w_qkv[0, 2])
    part_a[...] = da.astype(bf16).reshape(TZ, OWN, D)
    scatter_start(part_a, rs_a, ra_ss, ra_rs)

    xs = xin[...].reshape(ROWS, D).astype(f32)
    small += tn((da * xs * rms_scale(xs)).astype(bf16), unit0)
    bias_rows = []
    edges = (0,) + bucket_edges
    for b in range(len(edges)):
        hit = gap >= edges[b]
        if b + 1 < len(edges):
            hit = hit & (gap < edges[b + 1])
        for h in range(HEADS):
            bias_rows.append(jnp.sum(jnp.where(hit, score_grads[h], 0.0), axis=0, keepdims=True))
    bias_col = jnp.sum(jnp.concatenate(bias_rows, axis=0), axis=1, keepdims=True)
    lane48 = iota((MSG, SMALL), 1)
    bias_part = jnp.where(lane48 == BIAS + mz, bias_col, 0.0)

    a_own = scatter_sum(part_a, rs_a, ra_ss, ra_rs)
    x_own = xin[mz].astype(f32)
    r_own = rms_scale(x_own)
    lifted = a_own * gain0
    hat = x_own * r_own
    grad_own = dh_own + r_own * (lifted - hat * jnp.mean(lifted * hat, axis=-1, keepdims=True))
    in_full[mz] = grad_own.astype(bf16)
    gather_start(in_full, aa_ss, aa_rs)

    for j in range(3):
        dense_s[:, :, HF * j : HF * (j + 1)] = (
            tn(normed[...], dq_all[j]).astype(bf16).reshape(DP, MSG, HF)
        )
    dense_s[:, :, 3 * HF : D] = tn(do, call[mz]).astype(bf16).reshape(DP, MSG, HF)
    dense_s[:, :, D:] = small.astype(bf16).reshape(DP, MSG, SMALL)
    dense_s[0, :, D:] = (small[0:MSG, :] + bias_part).astype(bf16)

    @pl.when(jnp.logical_not(first))
    def _():
        hand(mz, back_ss, back_rs, in_full, gin).start()
        for i in range(1, TZ):
            gather_recv(in_full, aa_ss, aa_rs, i)
            hand(lax.rem(mz + i, TZ), back_ss, back_rs, in_full, gin).start()

    swap_start(dense_s, dense_r, dn_ss, dn_rs)

    @pl.when(first)
    def _():
        for i in range(1, TZ):
            gather_recv(in_full, aa_ss, aa_rs, i)

    grad_out[...] = in_full[...].reshape(ROWS, D)

    swap_recv_all(dense_s, dense_r, dn_ss, dn_rs)
    total = dense_r[0].astype(f32)
    for p in range(1, DP):
        total += dense_r[p].astype(f32)
    dense_f[me] = total[:, 0:D].astype(bf16)
    small_z[mz] = total[:, D:].astype(bf16)
    gather_start(small_z, sz_ss, sz_rs)

    def spread(buf, ss, rs):
        def step(i, carry):
            dp_copy(buf.at[me], buf.at[me], ss, rs, lax.rem(me + i, DP), me).start()
            return carry

        lax.fori_loop(1, DP, step, 0)

    def spread_recv(buf, ss, rs):
        def step(i, carry):
            src = lax.rem(me + DP - i, DP)
            dp_copy(buf.at[src], buf.at[src], ss, rs, src, src).wait_recv()
            return carry

        lax.fori_loop(1, DP, step, 0)

    def spread_sent(buf, ss, rs):
        def step(i, carry):
            dp_copy(buf.at[me], buf.at[me], ss, rs, lax.rem(me + i, DP), me).wait_send()
            return carry

        lax.fori_loop(1, DP, step, 0)

    spread(dense_f, df_ss, df_rs)
    for i in range(1, TZ):
        gather_recv(small_z, sz_ss, sz_rs, i)
    small_total = small_z[0].astype(f32)
    for t in range(1, TZ):
        small_total += small_z[t].astype(f32)
    small_f[me] = small_total.astype(bf16)
    spread(small_f, sf_ss, sf_rs)

    gather_sent(wall, w_ss, w_rs)
    gather_sent(call, c_ss, c_rs)
    swap_sent(send_b, recv_b, b_ss, b_rs)
    swap_sent(send_e, recv_e, e_ss, e_rs)
    swap_sent(send_d, recv_d, d_ss, d_rs)
    swap_sent(send_x, recv_x, x_ss, x_rs)
    scatter_sent(part_y, rs_y, ry_ss, ry_rs)
    gather_sent(gact, ay_ss, ay_rs)
    scatter_sent(part_h, rs_h, rh_ss, rh_rs)
    gather_sent(dh_full, ah_ss, ah_rs)
    scatter_sent(part_a, rs_a, ra_ss, ra_rs)
    gather_sent(in_full, aa_ss, aa_rs)
    swap_sent(dense_s, dense_r, dn_ss, dn_rs)
    gather_sent(small_z, sz_ss, sz_rs)

    @pl.when(first)
    def _():
        for t in range(TZ):
            hand(t, hand_ss, hand_rs, gact, xin).wait_send()

    @pl.when(jnp.logical_not(first))
    def _():
        for t in range(TZ):
            hand(t, back_ss, back_rs, in_full, gin).wait_send()

    spread_recv(dense_f, df_ss, df_rs)
    dense_out[...] = dense_f[...].reshape(D, D)
    spread_recv(small_f, sf_ss, sf_rs)
    small_out[...] = small_f[...].reshape(D, SMALL)
    spread_sent(dense_f, df_ss, df_rs)
    spread_sent(small_f, sf_ss, sf_rs)
    save_xe.wait()
    save_u.wait()
    save_de.wait()
    save_dpre.wait()


def body(
    tokens, cotangent, norm_gains, w_qkv, w_attn_out, bias_table, router, w_in, w_out, routes, segments
):
    vmem = pl.BlockSpec(memory_space=pltpu.VMEM)
    hbm = pl.BlockSpec(memory_space=pl.ANY)
    dma = pltpu.SemaphoreType.DMA
    rows3 = pltpu.VMEM((TZ, OWN, D), bf16)
    messages = pltpu.VMEM((DP, MSG, D), bf16)
    expert_rows = pltpu.VMEM((2, ER, D), bf16)
    scratch = dict(
        xin=rows3,
        gin=rows3,
        w_in=pltpu.VMEM((2, D, D), bf16),
        w_out=pltpu.VMEM((2, D, D), bf16),
        wall=pltpu.VMEM((TZ, HF, D), bf16),
        call=pltpu.VMEM((TZ, ROWS, HF), bf16),
        normed=pltpu.VMEM((ROWS, D), bf16),
        qkv=pltpu.VMEM((3, ROWS, HF), bf16),
        probs=pltpu.VMEM((2 * HEADS, BLOCK, BLOCK), f32),
        hidden=pltpu.VMEM((ROWS, D), f32),
        hid_scale=pltpu.VMEM((ROWS, 1), f32),
        normed2=pltpu.VMEM((ROWS, D), bf16),
        rpad=pltpu.VMEM((D, SMALL), bf16),
        gate=pltpu.VMEM((ROWS, 2), f32),
        slots=pltpu.VMEM((ROWS, 2), jnp.int32),
        ptg=pltpu.VMEM((ROWS, SLOTS), bf16),
        send_b=messages, recv_b=messages, send_e=messages, recv_e=messages,
        send_d=messages, recv_d=messages, send_x=messages, recv_x=messages,
        xe=expert_rows, act=expert_rows, dact=expert_rows, de=expert_rows, dpre=expert_rows,
        yf=pltpu.VMEM((2, ER, D), f32),
        part_y=rows3, rs_y=rows3, part_h=rows3, rs_h=rows3, dh_full=rows3,
        part_a=rows3, rs_a=rows3, in_full=rows3,
        dq_all=pltpu.VMEM((3, ROWS, HF), bf16),
        gact=rows3,
        dense_s=pltpu.VMEM((DP, MSG, D + SMALL), bf16),
        dense_r=pltpu.VMEM((DP, MSG, D + SMALL), bf16),
        dense_f=messages,
        small_z=pltpu.VMEM((TZ, MSG, SMALL), bf16),
        small_f=pltpu.VMEM((DP, MSG, SMALL), bf16),
        ld_sem=dma((2,)),
        out_sem=dma((4,)),
    )
    for name in ("w", "c"):
        scratch[name + "_ss"] = dma((TZ,))
        scratch[name + "_rs"] = dma((TZ,))
    for name in ("b", "e", "d", "x"):
        scratch[name + "_ss"] = dma((DP,))
        scratch[name + "_rs"] = dma((DP,))
    for name in ("ry", "ay", "rh", "ah", "ra", "aa", "hand", "back"):
        scratch[name + "_ss"] = dma((TZ,))
        scratch[name + "_rs"] = dma((TZ,))
    for name in ("dn", "df"):
        scratch[name + "_ss"] = dma((DP,))
        scratch[name + "_rs"] = dma((DP,))
    scratch["sz_ss"] = dma((TZ,))
    scratch["sz_rs"] = dma((TZ,))
    scratch["sf_ss"] = dma((DP,))
    scratch["sf_rs"] = dma((DP,))
    scratch["turn_sem"] = pltpu.SemaphoreType.REGULAR

    shape = jax.ShapeDtypeStruct
    act, grads, dense, small, xe, act_u, dpre, de = pl.pallas_call(
        kernel,
        out_shape=(
            shape((ROWS, D), bf16),
            shape((ROWS, D), bf16),
            shape((D, D), bf16),
            shape((D, SMALL), bf16),
            shape((2, ER, D), bf16),
            shape((2, ER, D), bf16),
            shape((2, ER, D), bf16),
            shape((2, ER, D), bf16),
        ),
        in_specs=[vmem] * 7 + [hbm] * 2 + [vmem] * 2,
        out_specs=(vmem,) * 4 + (hbm,) * 4,
        scratch_shapes=list(scratch.values()),
        compiler_params=pltpu.CompilerParams(
            collective_id=0, has_side_effects=True, vmem_limit_bytes=58 * 1024 * 1024
        ),
        name="layers",
    )(
        tokens, cotangent, norm_gains, w_qkv, w_attn_out, bias_table, router,
        w_in[0], w_out[0], routes, segments,
    )
    inner = jnp.einsum("erd,erf->edf", xe, dpre, preferred_element_type=f32)
    outer = jnp.einsum("erf,erd->efd", act_u, de, preferred_element_type=f32)
    dense = dense.astype(f32)
    small = small.astype(f32)
    qkv_grad = jnp.stack([dense[:, HF * j : HF * (j + 1)] for j in range(3)])
    attn_grad = dense[:, 3 * HF :].T
    gain_grad = jnp.stack([small[:, GAIN0], small[:, GAIN1]])
    bias_all = lax.dynamic_slice_in_dim(small[0:MSG], BIAS + lax.axis_index("tensor"), 1, axis=1)
    return (
        act[None],
        grads.astype(f32)[None],
        gain_grad[None],
        qkv_grad[None],
        attn_grad[None],
        bias_all.reshape(1, 16, HEADS),
        small[:, 0:32][None],
        inner[None],
        outer[None],
    )


def solution(mesh):
    in_specs = (
        P("dp", None),
        P("dp", None),
        P("section", None, None),
        P("section", None, None, "tensor"),
        P("section", "tensor", None),
        P("section", None, "tensor"),
        P("section", None, None),
        P("section", "dp", None, "tensor"),
        P("section", "dp", "tensor", None),
        P("section", "dp", None),
        P("dp", None),
    )
    out_specs = (
        P("section", "dp", None),
        P("section", "dp", None),
        P("section", None, None),
        P("section", None, None, "tensor"),
        P("section", "tensor", None),
        P("section", None, "tensor"),
        P("section", None, None),
        P("section", "dp", None, "tensor"),
        P("section", "dp", "tensor", None),
    )
    return jax.shard_map(body, mesh=mesh, in_specs=in_specs, out_specs=out_specs, check_vma=False)
```

```python
import jax
import jax.numpy as jnp
from jax import lax
from jax.experimental import pallas as pl
from jax.experimental.pallas import tpu as pltpu
from jax.sharding import PartitionSpec as P

epsilon = 1e-06
masked_score = -1000000000.0
bucket_edges = (1, 2, 3, 4, 5, 6, 7, 8, 10, 13, 16, 20, 25, 32, 40)
MESH = pl.DeviceIdType.MESH
f32 = jnp.float32
bf16 = jnp.bfloat16

DP = 16
TZ = 4
ROWS = 256
BLOCK = 128
OWN = BLOCK // TZ
D = 768
HF = 192
HEADS = 3
PAD = 16
ER = DP * PAD
SLOTS = 2 * ER
WIDE = D + 128
CUT = D // DP
SMALL = 48
GAIN0, GAIN1, BIAS = 32, 33, 34
HALF = D // 2
PARTS = D // 128
EDGES = (0,) + bucket_edges


def nn(a, b):
    return lax.dot_general(a, b, (((1,), (0,)), ((), ())), preferred_element_type=f32)


def nt(a, b):
    return lax.dot_general(a, b, (((1,), (1,)), ((), ())), preferred_element_type=f32)


def tn(a, b):
    return lax.dot_general(a, b, (((0,), (0,)), ((), ())), preferred_element_type=f32)


def iota(shape, dim):
    return lax.broadcasted_iota(jnp.int32, shape, dim)


def rms_scale(values):
    return lax.rsqrt(jnp.mean(values * values, axis=-1, keepdims=True) + epsilon)


def kernel(
    tokens, cotangent, gains, w_qkv, w_att, bias_tab, router, w_in_hbm, w_out_hbm, routes, segments,
    act_out, grad_out, dense_out, small_out, xe_out, u_out, dpre_out, de_out,
    xin, gin, w_in, w_out, wall, call, normed, qkv, probs, hidden, hid_scale, normed2, rpad,
    gate, slots, hits, ptg, pick, pick_g, send_b, recv_b, send_e, recv_e, send_d, recv_d, send_x,
    recv_x, act, dact, dpre, part_y, rs_y, part_h, rs_h, dh_own, dh_full, part_a, rs_a, in_full,
    dq_all, score_sum, gact, dense_s, dense_r, dense_f, small_acc, small_s, small_r, small_z, small_f,
    ld_sem, out_sem, w_ss, w_rs, c_ss, c_rs, b_ss, b_rs, e_ss, e_rs, d_ss, d_rs, x_ss, x_rs,
    ry_ss, ry_rs, ay_ss, ay_rs, rh_ss, rh_rs, ah_ss, ah_rs, ra_ss, ra_rs, aa_ss, aa_rs,
    hand_ss, hand_rs, back_ss, back_rs, dn_ss, dn_rs, df_ss, df_rs, sm_ss, sm_rs, sz_ss, sz_rs,
    sf_ss, sf_rs, turn_sem,
):
    sec = lax.axis_index("section")
    me = lax.axis_index("dp")
    mz = lax.axis_index("tensor")
    first = sec == 0
    second = sec == 1

    load_in = pltpu.make_async_copy(w_in_hbm, w_in, ld_sem.at[0])
    load_out = pltpu.make_async_copy(w_out_hbm, w_out, ld_sem.at[1])
    load_in.start()
    load_out.start()

    barrier = pltpu.get_barrier_semaphore()

    def greet(i, carry):
        pl.semaphore_signal(
            barrier, inc=1, device_id={"dp": lax.rem(me + i, DP)}, device_id_type=MESH
        )
        return carry

    lax.fori_loop(1, DP, greet, 0)
    for i in range(1, TZ):
        pl.semaphore_signal(
            barrier, inc=1, device_id={"tensor": lax.rem(mz + i, TZ)}, device_id_type=MESH
        )
    pl.semaphore_signal(barrier, inc=1, device_id={"section": 1 - sec}, device_id_type=MESH)

    def z_copy(src, dst, ss, rs, peer, slot):
        return pltpu.make_async_remote_copy(
            src_ref=src, dst_ref=dst, send_sem=ss.at[peer], recv_sem=rs.at[slot],
            device_id={"tensor": peer}, device_id_type=MESH,
        )

    def gather_start(buf, ss, rs):
        for i in range(1, TZ):
            z_copy(buf.at[mz], buf.at[mz], ss, rs, lax.rem(mz + i, TZ), mz).start()

    def gather_recv(buf, ss, rs, i):
        src = lax.rem(mz + i, TZ)
        z_copy(buf.at[src], buf.at[src], ss, rs, src, src).wait_recv()

    def gather_sent(buf, ss, rs):
        for i in range(1, TZ):
            z_copy(buf.at[mz], buf.at[mz], ss, rs, lax.rem(mz + i, TZ), mz).wait_send()

    def scatter_start(part, rcv, ss, rs):
        for i in range(1, TZ):
            peer = lax.rem(mz + i, TZ)
            z_copy(part.at[peer], rcv.at[mz], ss, rs, peer, mz).start()

    def scatter_sum(part, rcv, ss, rs):
        total = part[mz].astype(f32)
        for i in range(1, TZ):
            src = lax.rem(mz + i, TZ)
            z_copy(part.at[src], rcv.at[src], ss, rs, src, src).wait_recv()
            total += rcv[src].astype(f32)
        return total

    def scatter_sent(part, rcv, ss, rs):
        for i in range(1, TZ):
            peer = lax.rem(mz + i, TZ)
            z_copy(part.at[peer], rcv.at[mz], ss, rs, peer, mz).wait_send()

    def dp_copy(src, dst, ss, rs, peer, slot):
        return pltpu.make_async_remote_copy(
            src_ref=src, dst_ref=dst, send_sem=ss.at[peer], recv_sem=rs.at[slot],
            device_id={"dp": peer}, device_id_type=MESH,
        )

    def others(step):
        def one(i, carry):
            step(lax.rem(me + i, DP))
            return carry

        lax.fori_loop(1, DP, one, 0)

    def others_back(step):
        def one(i, carry):
            step(lax.rem(me + DP - i, DP))
            return carry

        lax.fori_loop(1, DP, one, 0)

    def swap_start(snd, rcv, ss, rs):
        others(lambda peer: dp_copy(snd.at[peer], rcv.at[me], ss, rs, peer, me).start())
        rcv[me] = snd[me]

    def swap_recv(snd, rcv, ss, rs):
        others_back(lambda src: dp_copy(snd.at[src], rcv.at[src], ss, rs, src, src).wait_recv())

    def swap_sent(snd, rcv, ss, rs):
        others(lambda peer: dp_copy(snd.at[peer], rcv.at[me], ss, rs, peer, me).wait_send())

    def spread(buf, ss, rs):
        others(lambda peer: dp_copy(buf.at[me], buf.at[me], ss, rs, peer, me).start())

    def spread_recv(buf, ss, rs):
        others_back(lambda src: dp_copy(buf.at[src], buf.at[src], ss, rs, src, src).wait_recv())

    def spread_sent(buf, ss, rs):
        others(lambda peer: dp_copy(buf.at[me], buf.at[me], ss, rs, peer, me).wait_send())

    def hand(b, t, ss, rs, src, dst):
        return pltpu.make_async_remote_copy(
            src_ref=src.at[b, t], dst_ref=dst.at[b, t], send_sem=ss.at[b, t],
            recv_sem=rs.at[b, t], device_id={"section": 1 - sec}, device_id_type=MESH,
        )

    def both(sems, b):
        return sems[0].at[b], sems[1].at[b]

    c_sem, b_sem, d_sem = (c_ss, c_rs), (b_ss, b_rs), (d_ss, d_rs)
    ry, ay, rh = (ry_ss, ry_rs), (ay_ss, ay_rs), (rh_ss, rh_rs)
    ah, ra, aa = (ah_ss, ah_rs), (ra_ss, ra_rs), (aa_ss, aa_rs)
    dn, df = (dn_ss, dn_rs), (df_ss, df_rs)

    row = iota((BLOCK, BLOCK), 0)
    col = iota((BLOCK, BLOCK), 1)
    eye = row == col
    earlier = (row > col).astype(f32).astype(bf16)
    every = jnp.ones((BLOCK, BLOCK), bf16)
    lane = iota((BLOCK, SMALL), 1)
    slot_lane = iota((BLOCK, SLOTS), 1)
    slot_sub = iota((SLOTS, BLOCK), 0)

    def to_col(values):
        return jnp.sum(jnp.where(eye, values, 0.0), axis=1, keepdims=True)

    def to_row(values):
        return jnp.sum(jnp.where(eye, values, 0.0), axis=0, keepdims=True)

    rpad[...] = jnp.zeros((SMALL, D), bf16)
    rpad[0:32, :] = router[0]
    for b in range(2):
        named = routes[0, :, b * BLOCK : (b + 1) * BLOCK].astype(f32)
        e0 = to_col(named[0:1, :]).astype(jnp.int32)
        e1 = to_col(named[1:2, :]).astype(jnp.int32)
        hit0 = (lane == e0).astype(f32)
        hit1 = (lane == e1).astype(f32)
        rank0 = jnp.sum(nn(earlier, hit0.astype(bf16)) * hit0, axis=1, keepdims=True)
        rank1 = jnp.sum(
            (nn(earlier, hit1.astype(bf16)) + nn(every, hit0.astype(bf16))) * hit1,
            axis=1, keepdims=True,
        )
        slot0 = (e0 % 2) * ER + (e0 // 2) * PAD + rank0.astype(jnp.int32)
        slot1 = (e1 % 2) * ER + (e1 // 2) * PAD + rank1.astype(jnp.int32)
        slots[b, :, 0:1] = slot0
        slots[b, :, 1:2] = slot1
        hits[b, 0] = hit0
        hits[b, 1] = hit1
        row0 = to_row(slot0.astype(f32)).astype(jnp.int32)
        row1 = to_row(slot1.astype(f32)).astype(jnp.int32)
        pick[b] = ((slot_sub == row0) | (slot_sub == row1)).astype(f32).astype(bf16)

    @pl.when(first)
    def _():
        xin[...] = tokens[...].reshape(2, TZ, OWN, D)

    @pl.when(second)
    def _():
        gin[...] = cotangent[...].reshape(2, TZ, OWN, D)

    wall[mz] = w_att[0]
    gain0 = gains[0, 0:1, :].astype(f32)
    gain1 = gains[0, 1:2, :].astype(f32)
    gap = row - col
    head_of = iota((BLOCK, HF), 1) // (HF // HEADS)

    pl.semaphore_wait(barrier, DP + TZ - 1)

    @pl.when(second)
    def _():
        pl.semaphore_wait(turn_sem, 1)

    gather_start(wall, w_ss, w_rs)

    for b in range(2):
        rows = slice(b * BLOCK, (b + 1) * BLOCK)

        @pl.when(second)
        def _():
            for t in range(TZ):
                hand(b, t, hand_ss, hand_rs, gact, xin).wait_recv()

        x = xin[b].reshape(BLOCK, D).astype(f32)
        normed[rows, :] = (x * rms_scale(x) * gain0).astype(bf16)
        for j in range(3):
            qkv[j, rows, :] = nt(normed[rows, :], w_qkv[0, j]).astype(bf16)
        seg_row = segments[b : b + 1, :].astype(f32)
        allowed = (gap >= 0) & (seg_row == to_col(seg_row))
        q = qkv[0, rows, :]
        k = qkv[1, rows, :]
        v = qkv[2, rows, :]
        context = jnp.zeros((BLOCK, HF), f32)
        for h in range(HEADS):
            bias = jnp.broadcast_to(bias_tab[0, h : h + 1, 0:1].astype(f32), (BLOCK, BLOCK))
            for n, edge in enumerate(bucket_edges):
                bias = jnp.where(
                    gap >= edge, bias_tab[0, h : h + 1, n + 1 : n + 2].astype(f32), bias
                )
            score = nt(jnp.where(head_of == h, q, jnp.zeros_like(q)), k) * 0.125 + bias
            score = jnp.where(allowed, score, masked_score)
            score = jnp.exp(score - jnp.max(score, axis=-1, keepdims=True))
            prob = score / jnp.sum(score, axis=-1, keepdims=True)
            probs[b * HEADS + h] = prob
            context = jnp.where(head_of == h, nn(prob.astype(bf16), v), context)
        call[b, mz] = context.astype(bf16)
        gather_start(call.at[b], *both(c_sem, b))

    def dispatch(chosen, values, snd, rcv, sems, b):
        for e in range(2):
            out = nn(chosen[b, ER * e : ER * (e + 1), :], values).astype(bf16)
            snd[b, e] = out.reshape(DP, PAD, D)
            swap_start(snd.at[b, e], rcv.at[b, e], sems[0].at[b, e], sems[1].at[b, e])

    def dispatch_grad(b):
        dispatch(pick_g, gin[b].reshape(BLOCK, D), send_d, recv_d, d_sem, b)

    for b in range(2):
        for i in range(1, TZ):
            gather_recv(call.at[b], *both(c_sem, b), i)
        if b == 0:
            for i in range(1, TZ):
                gather_recv(wall, w_ss, w_rs, i)

            @pl.when(first)
            def _():
                pl.semaphore_signal(
                    turn_sem, inc=1, device_id={"section": 1 - sec}, device_id_type=MESH
                )

        h = xin[b].reshape(BLOCK, D).astype(f32)
        for t in range(TZ):
            h += nn(call[b, t], wall[t])
        hidden[b] = h
        scale = rms_scale(h)
        hid_scale[b] = scale
        normed2[b] = (h * scale * gain1).astype(bf16)
        dispatch(pick, normed2[b], send_b, recv_b, b_sem, b)

        z = nt(normed2[b], rpad[...])
        z0 = jnp.sum(z * hits[b, 0], axis=1, keepdims=True)
        z1 = jnp.sum(z * hits[b, 1], axis=1, keepdims=True)
        g0 = 1.0 / (1.0 + jnp.exp(z1 - z0))
        g1 = 1.0 / (1.0 + jnp.exp(z0 - z1))
        gate[b, :, 0:1] = g0
        gate[b, :, 1:2] = g1
        slot0 = slots[b, :, 0:1]
        slot1 = slots[b, :, 1:2]
        row0 = to_row(slot0.astype(f32)).astype(jnp.int32)
        row1 = to_row(slot1.astype(f32)).astype(jnp.int32)
        pick_g[b] = (
            jnp.where(slot_sub == row0, to_row(g0), 0.0)
            + jnp.where(slot_sub == row1, to_row(g1), 0.0)
        ).astype(bf16)

        @pl.when(second)
        def _():
            dispatch_grad(b)

        ptg[b] = (
            jnp.where(slot_lane == slot0, g0, 0.0) + jnp.where(slot_lane == slot1, g1, 0.0)
        ).astype(bf16)

    root = 0.7978845608028654
    saved = []

    def save(b, n, src, dst):
        copy = pltpu.make_async_copy(src.at[b], dst.at[b], out_sem.at[b, n])
        copy.start()
        saved.append(copy)

    def expert_forward(b, e):
        swap_recv(send_b.at[b, e], recv_b.at[b, e], b_ss.at[b, e], b_rs.at[b, e])
        x = recv_b[b, e].reshape(ER, D)
        for n in range(3):
            cols = slice(256 * n, 256 * (n + 1))
            pre = nn(x, w_in[e, :, cols])
            square = pre * pre
            wave = jnp.tanh(root * pre * (1.0 + 0.044715 * square))
            lift = 0.5 * (1.0 + wave)
            act[b, e, :, cols] = (pre * lift).astype(bf16)
            slope = lift + 0.5 * root * pre * (1.0 - wave * wave) * (1.0 + 0.134145 * square)
            dact[b, e, :, cols] = slope.astype(bf16)
        out = nn(act[b, e], w_out[e])
        send_e[b, e] = out.astype(bf16).reshape(DP, PAD, D)

    def return_rows(b, e):
        swap_start(send_e.at[b, e], recv_e.at[b, e], e_ss.at[b, e], e_rs.at[b, e])

    def expert_backward(b, e):
        swap_recv(send_d.at[b, e], recv_d.at[b, e], d_ss.at[b, e], d_rs.at[b, e])
        de = recv_d[b, e].reshape(ER, D)
        for n in range(3):
            cols = slice(256 * n, 256 * (n + 1))
            grad = nt(de, w_out[e, cols, :])
            dpre[b, e, :, cols] = (grad * dact[b, e, :, cols].astype(f32)).astype(bf16)
        out = nt(dpre[b, e], w_in[e])
        send_x[b, e, :, :, 0:D] = out.astype(bf16).reshape(DP, PAD, D)
        rows = send_e[b, e].reshape(ER, D).astype(f32)
        weight = jnp.sum(rows * de.astype(f32), axis=1, keepdims=True)
        coarse = weight.astype(bf16).astype(f32)
        place = iota((ER, 128), 1)
        pair = jnp.where(place == 0, coarse, jnp.where(place == 1, weight - coarse, 0.0))
        send_x[b, e, :, :, D:] = pair.astype(bf16).reshape(DP, PAD, 128)
        swap_start(send_x.at[b, e], recv_x.at[b, e], x_ss.at[b, e], x_rs.at[b, e])

    def each_expert(step):
        def one(e, carry):
            step(e)
            return carry

        lax.fori_loop(0, 2, one, 0)

    def each_part(step):
        def one(i, carry):
            step(i // 2, i % 2)
            return carry

        lax.fori_loop(0, 4, one, 0)

    def combine(b):
        for e in range(2):
            swap_recv(send_e.at[b, e], recv_e.at[b, e], e_ss.at[b, e], e_rs.at[b, e])
        out = nn(ptg[b], recv_e[b].reshape(SLOTS, D))
        part_y[b] = out.astype(bf16).reshape(TZ, OWN, D)
        scatter_start(part_y.at[b], rs_y.at[b], *both(ry, b))

    def settle(b):
        own = pl.ds(pl.multiple_of(mz * OWN, OWN), OWN)
        total = scatter_sum(part_y.at[b], rs_y.at[b], *both(ry, b)) + hidden[b, own, :]
        gact[b, mz] = total.astype(bf16)
        gather_start(gact.at[b], *both(ay, b))

    load_in.wait()
    load_out.wait()

    @pl.when(first)
    def _():
        def part(b, e):
            expert_forward(b, e)
            return_rows(b, e)

        each_part(part)

    @pl.when(second)
    def _():
        def block(b, carry):
            each_expert(lambda e: expert_forward(b, e))
            each_expert(lambda e: expert_backward(b, e))
            return carry

        lax.fori_loop(0, 2, block, 0)
        each_part(return_rows)

    for b in range(2):
        save(b, 0, recv_b, xe_out)
        save(b, 1, act, u_out)

    @pl.when(first)
    def _():
        combine(0)
        combine(1)
        for b in range(2):
            settle(b)
            hand(b, mz, hand_ss, hand_rs, gact, xin).start()
        for b in range(2):
            for i in range(1, TZ):
                gather_recv(gact.at[b], *both(ay, b), i)
                hand(b, lax.rem(mz + i, TZ), hand_ss, hand_rs, gact, xin).start()
        for b in range(2):
            for t in range(TZ):
                hand(b, t, back_ss, back_rs, in_full, gin).wait_recv()
            dispatch_grad(b)
        each_part(expert_backward)

    for b in range(2):
        save(b, 2, recv_d, de_out)
        save(b, 3, dpre, dpre_out)

    for b in range(2):
        pt0 = (slot_lane == slots[b, :, 0:1]).astype(f32).astype(bf16)
        pt1 = (slot_lane == slots[b, :, 1:2]).astype(f32).astype(bf16)
        for e in range(2):
            swap_recv(send_x.at[b, e], recv_x.at[b, e], x_ss.at[b, e], x_rs.at[b, e])
        back = recv_x[b].reshape(SLOTS, WIDE)
        q0 = jnp.sum(nn(pt0, back[:, D:]), axis=1, keepdims=True)
        q1 = jnp.sum(nn(pt1, back[:, D:]), axis=1, keepdims=True)
        dc = gate[b, :, 1:2] * q0 - gate[b, :, 0:1] * q1
        dz = ((hits[b, 0] - hits[b, 1]) * dc).astype(bf16)
        db = nn(pt0 + pt1, back[:, 0:D]) + nn(dz, rpad[...])
        part_h[b] = db.astype(bf16).reshape(TZ, OWN, D)
        scatter_start(part_h.at[b], rs_h.at[b], *both(rh, b))
        unit = (lane == GAIN1).astype(f32).astype(bf16)
        small = tn(dz, normed2[b])
        small += tn(unit, (db * hidden[b] * hid_scale[b]).astype(bf16))
        if b == 0:
            small_acc[...] = small
        else:
            small_acc[...] += small

    for b in range(2):
        own = pl.ds(pl.multiple_of(mz * OWN, OWN), OWN)
        s_own = hid_scale[b, own, :]
        hat = hidden[b, own, :] * s_own
        lifted = scatter_sum(part_h.at[b], rs_h.at[b], *both(rh, b)) * gain1
        total = gin[b, mz].astype(f32) + s_own * (
            lifted - hat * jnp.mean(lifted * hat, axis=-1, keepdims=True)
        )
        dh_own[b] = total
        dh_full[b, mz] = total.astype(bf16)
        gather_start(dh_full.at[b], *both(ah, b))

    for b in range(2):
        rows = slice(b * BLOCK, (b + 1) * BLOCK)
        for i in range(1, TZ):
            gather_recv(dh_full.at[b], *both(ah, b), i)
        dc = nt(dh_full[b].reshape(BLOCK, D), w_att[0]).astype(bf16)
        q = qkv[0, rows, :]
        k = qkv[1, rows, :]
        v = qkv[2, rows, :]
        dq = jnp.zeros((BLOCK, HF), f32)
        dk = jnp.zeros((BLOCK, HF), f32)
        dv = jnp.zeros((BLOCK, HF), f32)
        for h in range(HEADS):
            mine = head_of == h
            prob = probs[b * HEADS + h]
            dp = nt(jnp.where(mine, dc, jnp.zeros_like(dc)), v)
            ds = (prob * (dp - jnp.sum(prob * dp, axis=-1, keepdims=True))).astype(bf16)
            if b == 0:
                score_sum[h] = ds.astype(f32)
            else:
                score_sum[h] += ds.astype(f32)
            dq = jnp.where(mine, nn(ds, k), dq)
            dk = jnp.where(mine, tn(ds, q), dk)
            dv = jnp.where(mine, tn(prob.astype(bf16), dc), dv)
        dq_all[0, rows, :] = (dq * 0.125).astype(bf16)
        dq_all[1, rows, :] = (dk * 0.125).astype(bf16)
        dq_all[2, rows, :] = dv.astype(bf16)
        da = nn(dq_all[0, rows, :], w_qkv[0, 0])
        da += nn(dq_all[1, rows, :], w_qkv[0, 1])
        da += nn(dq_all[2, rows, :], w_qkv[0, 2])
        part_a[b] = da.astype(bf16).reshape(TZ, OWN, D)
        scatter_start(part_a.at[b], rs_a.at[b], *both(ra, b))

    def dense_part():
        own_context = jnp.concatenate([call[0, mz], call[1, mz]], axis=0)
        for n in range(2):
            cols = slice(HALF * n, HALF * (n + 1))
            for j in range(3):
                out = tn(dq_all[j], normed[:, cols]).astype(bf16)
                dense_s[n, 4 * j : 4 * j + 4] = out.reshape(4, CUT, HALF)
            grad = dh_full[:, :, :, cols].reshape(ROWS, HALF)
            dense_s[n, 12:16] = tn(own_context, grad).astype(bf16).reshape(4, CUT, HALF)
            swap_start(dense_s.at[n], dense_r.at[n], *both(dn, n))
        small = small_acc[...]
        unit = (lane == GAIN0).astype(f32).astype(bf16)
        for b in range(2):
            x = xin[b].reshape(BLOCK, D).astype(f32)
            da = part_a[b].reshape(BLOCK, D).astype(f32)
            small += tn(unit, (da * x * rms_scale(x)).astype(bf16))
        bias_rows = []
        for h in range(HEADS):
            for n in range(len(EDGES)):
                hit = gap >= EDGES[n]
                if n + 1 < len(EDGES):
                    hit = hit & (gap < EDGES[n + 1])
                bias_rows.append(jnp.sum(jnp.where(hit, score_sum[h], 0.0), axis=0, keepdims=True))
        bias_col = jnp.sum(jnp.concatenate(bias_rows, axis=0), axis=1, keepdims=True)
        diagonal = iota((SMALL, 128), 0) == iota((SMALL, 128), 1)
        bias_row = jnp.sum(jnp.where(diagonal, bias_col, 0.0), axis=0, keepdims=True)
        mine = iota((SMALL, 128), 0) == BIAS + mz
        for j in range(PARTS):
            piece = small[:, 128 * j : 128 * (j + 1)]
            if j == 0:
                piece += jnp.where(mine, bias_row, 0.0)
            small_s[j] = piece.astype(bf16)

            @pl.when(me != j)
            def _():
                dp_copy(small_s.at[j], small_r.at[me], sm_ss, sm_rs, j, me).start()

    @pl.when(first)
    def _():
        dense_part()

    for b in range(2):
        x_own = xin[b, mz].astype(f32)
        r_own = rms_scale(x_own)
        hat = x_own * r_own
        lifted = scatter_sum(part_a.at[b], rs_a.at[b], *both(ra, b)) * gain0
        total = dh_own[b] + r_own * (lifted - hat * jnp.mean(lifted * hat, axis=-1, keepdims=True))
        in_full[b, mz] = total.astype(bf16)
        gather_start(in_full.at[b], *both(aa, b))

        @pl.when(second)
        def _():
            hand(b, mz, back_ss, back_rs, in_full, gin).start()

    for b in range(2):
        for i in range(1, TZ):
            gather_recv(in_full.at[b], *both(aa, b), i)

            @pl.when(second)
            def _():
                hand(b, lax.rem(mz + i, TZ), back_ss, back_rs, in_full, gin).start()

    grad_out[...] = in_full[...].reshape(ROWS, D)

    @pl.when(second)
    def _():
        dense_part()
        for b in range(2):
            combine(b)
        for b in range(2):
            settle(b)
        for b in range(2):
            for i in range(1, TZ):
                gather_recv(gact.at[b], *both(ay, b), i)

    act_out[...] = gact[...].reshape(ROWS, D)

    holds = me < PARTS

    for n in range(2):
        swap_recv(dense_s.at[n], dense_r.at[n], *both(dn, n))
        total = dense_r[n, 0].astype(f32)
        for p in range(1, DP):
            total += dense_r[n, p].astype(f32)
        dense_f[n, me] = total.astype(bf16)
        spread(dense_f.at[n], *both(df, n))

    @pl.when(holds)
    def _():
        small_r[me] = small_s[me]
        others_back(
            lambda src: dp_copy(small_s.at[src], small_r.at[src], sm_ss, sm_rs, src, src).wait_recv()
        )
        total = small_r[0].astype(f32)
        for p in range(1, DP):
            total += small_r[p].astype(f32)
        small_z[mz] = total.astype(bf16)
        gather_start(small_z, sz_ss, sz_rs)
        for i in range(1, TZ):
            gather_recv(small_z, sz_ss, sz_rs, i)
        total = small_z[0].astype(f32)
        for t in range(1, TZ):
            total += small_z[t].astype(f32)
        small_f[me] = total.astype(bf16)
        spread(small_f, sf_ss, sf_rs)

    gather_sent(wall, w_ss, w_rs)
    for b in range(2):
        gather_sent(call.at[b], *both(c_sem, b))
        for e in range(2):
            swap_sent(send_b.at[b, e], recv_b.at[b, e], b_ss.at[b, e], b_rs.at[b, e])
            swap_sent(send_e.at[b, e], recv_e.at[b, e], e_ss.at[b, e], e_rs.at[b, e])
            swap_sent(send_d.at[b, e], recv_d.at[b, e], d_ss.at[b, e], d_rs.at[b, e])
            swap_sent(send_x.at[b, e], recv_x.at[b, e], x_ss.at[b, e], x_rs.at[b, e])
        scatter_sent(part_y.at[b], rs_y.at[b], *both(ry, b))
        gather_sent(gact.at[b], *both(ay, b))
        scatter_sent(part_h.at[b], rs_h.at[b], *both(rh, b))
        gather_sent(dh_full.at[b], *both(ah, b))
        scatter_sent(part_a.at[b], rs_a.at[b], *both(ra, b))
        gather_sent(in_full.at[b], *both(aa, b))

        @pl.when(first)
        def _():
            for t in range(TZ):
                hand(b, t, hand_ss, hand_rs, gact, xin).wait_send()

        @pl.when(second)
        def _():
            for t in range(TZ):
                hand(b, t, back_ss, back_rs, in_full, gin).wait_send()

    for n in range(2):
        swap_sent(dense_s.at[n], dense_r.at[n], *both(dn, n))
    for j in range(PARTS):
        @pl.when(me != j)
        def _():
            dp_copy(small_s.at[j], small_r.at[me], sm_ss, sm_rs, j, me).wait_send()

    @pl.when(holds)
    def _():
        gather_sent(small_z, sz_ss, sz_rs)
        spread_sent(small_f, sf_ss, sf_rs)

    for copy in saved:
        copy.wait()
    for n in range(2):
        spread_recv(dense_f.at[n], *both(df, n))
        dense_out[:, HALF * n : HALF * (n + 1)] = dense_f[n].reshape(D, HALF)
    for j in range(PARTS):
        @pl.when(me != j)
        def _():
            dp_copy(small_f.at[j], small_f.at[j], sf_ss, sf_rs, j, j).wait_recv()

        small_out[:, 128 * j : 128 * (j + 1)] = small_f[j].astype(f32)
    held = small_f[0].astype(f32)
    mine = iota((SMALL, 128), 0) == BIAS + mz
    small_out[BIAS : BIAS + 1, 0:128] = jnp.sum(jnp.where(mine, held, 0.0), axis=0, keepdims=True)
    for n in range(2):
        spread_sent(dense_f.at[n], *both(df, n))


def last_outputs(
    xe, dpre, u, de, act, grads, dense, small,
    inner, outer, act_out, grads_out, qkv_out, attn_out, gain_out, router_out, bias_out,
):
    inner[0] = tn(xe[...].reshape(SLOTS, 256), dpre[...].reshape(SLOTS, D))
    outer[0] = tn(u[...].reshape(SLOTS, 256), de[...].reshape(SLOTS, D))
    act_out[...] = act[...]
    grads_out[...] = grads[...].astype(f32)
    qkv_out[...] = dense[0 : 3 * HF, :].astype(f32).reshape(3, HF, 128)
    attn_out[...] = dense[3 * HF :, :].astype(f32)
    router_out[...] = small[0:32, :]
    gain_out[...] = small[GAIN0 : GAIN1 + 1, :]

    @pl.when((pl.program_id(0) == 0) & (pl.program_id(1) == 0))
    def _():
        for h in range(HEADS):
            bias_out[h] = small[BIAS : BIAS + 1, 16 * h : 16 * (h + 1)]


def body(
    tokens, cotangent, norm_gains, w_qkv, w_attn_out, bias_table, router, w_in, w_out, routes, segments
):
    vmem = pl.BlockSpec(memory_space=pltpu.VMEM)
    hbm = pl.BlockSpec(memory_space=pl.ANY)
    dma = pltpu.SemaphoreType.DMA
    rows4 = pltpu.VMEM((2, TZ, OWN, D), bf16)
    messages = pltpu.VMEM((2, 2, DP, PAD, D), bf16)
    wide = pltpu.VMEM((2, 2, DP, PAD, WIDE), bf16)
    expert_rows = pltpu.VMEM((2, 2, ER, D), bf16)
    cuts = pltpu.VMEM((2, DP, CUT, HALF), bf16)
    pieces = pltpu.VMEM((DP, SMALL, 128), bf16)
    scratch = dict(
        xin=rows4,
        gin=rows4,
        w_in=pltpu.VMEM((2, D, D), bf16),
        w_out=pltpu.VMEM((2, D, D), bf16),
        wall=pltpu.VMEM((TZ, HF, D), bf16),
        call=pltpu.VMEM((2, TZ, BLOCK, HF), bf16),
        normed=pltpu.VMEM((ROWS, D), bf16),
        qkv=pltpu.VMEM((3, ROWS, HF), bf16),
        probs=pltpu.VMEM((2 * HEADS, BLOCK, BLOCK), f32),
        hidden=pltpu.VMEM((2, BLOCK, D), f32),
        hid_scale=pltpu.VMEM((2, BLOCK, 1), f32),
        normed2=pltpu.VMEM((2, BLOCK, D), bf16),
        rpad=pltpu.VMEM((SMALL, D), bf16),
        gate=pltpu.VMEM((2, BLOCK, 2), f32),
        slots=pltpu.VMEM((2, BLOCK, 2), jnp.int32),
        hits=pltpu.VMEM((2, 2, BLOCK, SMALL), f32),
        ptg=pltpu.VMEM((2, BLOCK, SLOTS), bf16),
        pick=pltpu.VMEM((2, SLOTS, BLOCK), bf16),
        pick_g=pltpu.VMEM((2, SLOTS, BLOCK), bf16),
        send_b=messages, recv_b=messages, send_e=messages, recv_e=messages,
        send_d=messages, recv_d=messages, send_x=wide, recv_x=wide,
        act=expert_rows, dact=expert_rows, dpre=expert_rows,
        part_y=rows4, rs_y=rows4, part_h=rows4, rs_h=rows4,
        dh_own=pltpu.VMEM((2, OWN, D), f32),
        dh_full=rows4, part_a=rows4, rs_a=rows4, in_full=rows4,
        dq_all=pltpu.VMEM((3, ROWS, HF), bf16),
        score_sum=pltpu.VMEM((HEADS, BLOCK, BLOCK), f32),
        gact=rows4,
        dense_s=cuts, dense_r=cuts, dense_f=cuts,
        small_acc=pltpu.VMEM((SMALL, D), f32),
        small_s=pieces, small_r=pieces,
        small_z=pltpu.VMEM((TZ, SMALL, 128), bf16),
        small_f=pieces,
        ld_sem=dma((2,)),
        out_sem=dma((2, 4)),
        w_ss=dma((TZ,)), w_rs=dma((TZ,)),
        c_ss=dma((2, TZ)), c_rs=dma((2, TZ)),
    )
    for name in ("b", "e", "d", "x"):
        scratch[name + "_ss"] = dma((2, 2, DP))
        scratch[name + "_rs"] = dma((2, 2, DP))
    for name in ("ry", "ay", "rh", "ah", "ra", "aa", "hand", "back"):
        scratch[name + "_ss"] = dma((2, TZ))
        scratch[name + "_rs"] = dma((2, TZ))
    for name in ("dn", "df"):
        scratch[name + "_ss"] = dma((2, DP))
        scratch[name + "_rs"] = dma((2, DP))
    for name, count in (("sm", DP), ("sz", TZ), ("sf", DP)):
        scratch[name + "_ss"] = dma((count,))
        scratch[name + "_rs"] = dma((count,))
    scratch["turn_sem"] = pltpu.SemaphoreType.REGULAR

    shape = jax.ShapeDtypeStruct
    rows = shape((2, 2, DP, PAD, D), bf16)
    kept = shape((2, 2, ER, D), bf16)
    act, grads, dense, small, xe, u, dpre, de = pl.pallas_call(
        kernel,
        out_shape=(
            shape((ROWS, D), bf16),
            shape((ROWS, D), bf16),
            shape((D, D), bf16),
            shape((SMALL, D), f32),
            rows, kept, kept, rows,
        ),
        in_specs=[vmem] * 7 + [hbm] * 2 + [vmem] * 2,
        out_specs=(vmem,) * 4 + (hbm,) * 4,
        scratch_shapes=list(scratch.values()),
        compiler_params=pltpu.CompilerParams(
            collective_id=0, has_side_effects=True, vmem_limit_bytes=58 * 1024 * 1024
        ),
        name="layers",
    )(
        tokens, cotangent, norm_gains, w_qkv.swapaxes(2, 3), w_attn_out, bias_table.swapaxes(1, 2),
        router.swapaxes(1, 2), w_in[0], w_out[0], routes.swapaxes(1, 2), segments,
    )

    cut = pl.BlockSpec((2, None, ER, 256), lambda e, i: (0, e, 0, i))
    full = pl.BlockSpec((2, None, ER, D), lambda e, i: (0, e, 0, 0))
    out = pl.BlockSpec((1, 256, D), lambda e, i: (e, i, 0))

    def lanes(*lead):
        return pl.BlockSpec(lead + (128,), lambda e, i: (0,) * len(lead) + (3 * e + i,))

    inner, outer, act, grads, qkv_grad, attn_grad, gain_grad, router_grad, bias_grad = pl.pallas_call(
        last_outputs,
        grid=(2, 3),
        out_shape=(
            shape((2, D, D), f32),
            shape((2, D, D), f32),
            shape((ROWS, D), bf16),
            shape((ROWS, D), f32),
            shape((3, HF, D), f32),
            shape((HF, D), f32),
            shape((2, D), f32),
            shape((32, D), f32),
            shape((HEADS, 1, 16), f32),
        ),
        in_specs=[
            cut, full, cut, full, lanes(ROWS), lanes(ROWS), lanes(D), lanes(SMALL),
        ],
        out_specs=(
            out, out, lanes(ROWS), lanes(ROWS), lanes(3, HF), lanes(HF), lanes(2), lanes(32),
            pl.BlockSpec((HEADS, 1, 16), lambda e, i: (0, 0, 0)),
        ),
        compiler_params=pltpu.CompilerParams(vmem_limit_bytes=58 * 1024 * 1024),
        name="last_outputs",
    )(xe.reshape(2, 2, ER, D), dpre, u, de.reshape(2, 2, ER, D), act, grads, dense, small)

    return (
        act[None],
        grads[None],
        gain_grad[None],
        qkv_grad.swapaxes(1, 2)[None],
        attn_grad[None],
        bias_grad.transpose(1, 2, 0),
        router_grad.T[None],
        inner[None],
        outer[None],
    )


def solution(mesh):
    in_specs = (
        P("dp", None),
        P("dp", None),
        P("section", None, None),
        P("section", None, None, "tensor"),
        P("section", "tensor", None),
        P("section", None, "tensor"),
        P("section", None, None),
        P("section", "dp", None, "tensor"),
        P("section", "dp", "tensor", None),
        P("section", "dp", None),
        P("dp", None),
    )
    out_specs = (
        P("section", "dp", None),
        P("section", "dp", None),
        P("section", None, None),
        P("section", None, None, "tensor"),
        P("section", "tensor", None),
        P("section", None, "tensor"),
        P("section", None, None),
        P("section", "dp", None, "tensor"),
        P("section", "dp", "tensor", None),
    )
    return jax.shard_map(body, mesh=mesh, in_specs=in_specs, out_specs=out_specs, check_vma=False)
```

```python
import jax
import jax.numpy as jnp
from jax import lax
from jax.experimental import pallas as pl
from jax.experimental.pallas import tpu as pltpu
from jax.sharding import PartitionSpec as P

epsilon = 1e-06
masked_score = -1000000000.0
bucket_edges = (1, 2, 3, 4, 5, 6, 7, 8, 10, 13, 16, 20, 25, 32, 40)
MESH = pl.DeviceIdType.MESH
f32 = jnp.float32
bf16 = jnp.bfloat16

DP = 16
TZ = 4
ROWS = 256
BLOCK = 128
OWN = BLOCK // TZ
D = 768
HF = 192
HEADS = 3
PAD = 16
ER = DP * PAD
SLOTS = 2 * ER
WIDE = D + 128
CUT = D // DP
SMALL = 48
GAIN0, GAIN1, BIAS = 32, 33, 34
HALF = D // 2
PARTS = D // 128
EDGES = (0,) + bucket_edges


def nn(a, b):
    return lax.dot_general(a, b, (((1,), (0,)), ((), ())), preferred_element_type=f32)


def nt(a, b):
    return lax.dot_general(a, b, (((1,), (1,)), ((), ())), preferred_element_type=f32)


def tn(a, b):
    return lax.dot_general(a, b, (((0,), (0,)), ((), ())), preferred_element_type=f32)


def iota(shape, dim):
    return lax.broadcasted_iota(jnp.int32, shape, dim)


def rms_scale(values):
    return lax.rsqrt(jnp.mean(values * values, axis=-1, keepdims=True) + epsilon)


def kernel(
    tokens, cotangent, gains, w_qkv_hbm, w_att, bias_tab, router, w_in_hbm, w_out_hbm, routes, segments,
    act_out, grad_out, dense_out, small_out, xe_out, act, dpre, de_out,
    xin, gin, w_qkv, w_in, w_out, wall, part_o, rs_o, o_full, call, normed, qkv, probs, hidden, hid_scale, normed2, rpad,
    gate, slots, hits, ptg, pick, pick_g, send_b, recv_b, send_e, recv_e, send_d, recv_d, send_x,
    recv_x, dact, part_y, rs_y, part_h, rs_h, dh_own, dh_full, part_a, rs_a, in_full,
    dq_all, score_sum, gact, dense_s, dense_r, dense_f, small_acc, small_s, small_r, small_z, small_f,
    ld_sem, out_sem, end_sem, w_ss, w_rs, c_ss, c_rs, b_ss, b_rs, e_ss, e_rs, d_ss, d_rs, x_ss, x_rs,
    ro_ss, ro_rs, ao_ss, ao_rs, ry_ss, ry_rs, ay_ss, ay_rs, rh_ss, rh_rs, ah_ss, ah_rs, ra_ss, ra_rs, aa_ss, aa_rs,
    hand_ss, hand_rs, back_ss, back_rs, dn_ss, dn_rs, df_ss, df_rs, sm_ss, sm_rs, sz_ss, sz_rs,
    sf_ss, sf_rs, turn_sem,
):
    sec = lax.axis_index("section")
    me = lax.axis_index("dp")
    mz = lax.axis_index("tensor")
    first = sec == 0
    second = sec == 1

    load_in = pltpu.make_async_copy(w_in_hbm, w_in, ld_sem.at[0])
    load_out = pltpu.make_async_copy(w_out_hbm, w_out, ld_sem.at[1])
    load_qkv = pltpu.make_async_copy(w_qkv_hbm, w_qkv, ld_sem.at[2])
    load_att = pltpu.make_async_copy(w_att, wall.at[mz], ld_sem.at[3])
    load_x = pltpu.make_async_copy(tokens, xin, ld_sem.at[4])
    load_g = pltpu.make_async_copy(cotangent, gin, ld_sem.at[4])

    @pl.when(first)
    def _():
        load_x.start()

    @pl.when(second)
    def _():
        load_g.start()

    load_qkv.start()
    load_att.start()

    barrier = pltpu.get_barrier_semaphore()

    def greet(i, carry):
        pl.semaphore_signal(
            barrier, inc=1, device_id={"dp": lax.rem(me + i, DP)}, device_id_type=MESH
        )
        return carry

    lax.fori_loop(1, DP, greet, 0)
    for i in range(1, TZ):
        pl.semaphore_signal(
            barrier, inc=1, device_id={"tensor": lax.rem(mz + i, TZ)}, device_id_type=MESH
        )
    pl.semaphore_signal(barrier, inc=1, device_id={"section": 1 - sec}, device_id_type=MESH)

    def z_copy(src, dst, ss, rs, peer, slot):
        return pltpu.make_async_remote_copy(
            src_ref=src, dst_ref=dst, send_sem=ss.at[peer], recv_sem=rs.at[slot],
            device_id={"tensor": peer}, device_id_type=MESH,
        )

    def gather_start(buf, ss, rs):
        for i in range(1, TZ):
            z_copy(buf.at[mz], buf.at[mz], ss, rs, lax.rem(mz + i, TZ), mz).start()

    def gather_recv(buf, ss, rs, i):
        src = lax.rem(mz + i, TZ)
        z_copy(buf.at[src], buf.at[src], ss, rs, src, src).wait_recv()

    def gather_sent(buf, ss, rs):
        for i in range(1, TZ):
            z_copy(buf.at[mz], buf.at[mz], ss, rs, lax.rem(mz + i, TZ), mz).wait_send()

    def scatter_start(part, rcv, ss, rs):
        for i in range(1, TZ):
            peer = lax.rem(mz + i, TZ)
            z_copy(part.at[peer], rcv.at[mz], ss, rs, peer, mz).start()

    def scatter_sum(part, rcv, ss, rs):
        total = part[mz].astype(f32)
        for i in range(1, TZ):
            src = lax.rem(mz + i, TZ)
            z_copy(part.at[src], rcv.at[src], ss, rs, src, src).wait_recv()
            total += rcv[src].astype(f32)
        return total

    def scatter_sent(part, rcv, ss, rs):
        for i in range(1, TZ):
            peer = lax.rem(mz + i, TZ)
            z_copy(part.at[peer], rcv.at[mz], ss, rs, peer, mz).wait_send()

    def dp_copy(src, dst, ss, rs, peer, slot):
        return pltpu.make_async_remote_copy(
            src_ref=src, dst_ref=dst, send_sem=ss.at[peer], recv_sem=rs.at[slot],
            device_id={"dp": peer}, device_id_type=MESH,
        )

    def others(step):
        def one(i, carry):
            step(lax.rem(me + i, DP))
            return carry

        lax.fori_loop(1, DP, one, 0)

    def others_back(step):
        def one(i, carry):
            step(lax.rem(me + DP - i, DP))
            return carry

        lax.fori_loop(1, DP, one, 0)

    def swap_start(snd, rcv, ss, rs):
        others(lambda peer: dp_copy(snd.at[peer], rcv.at[me], ss, rs, peer, me).start())
        rcv[me] = snd[me]

    def swap_recv(snd, rcv, ss, rs):
        others_back(lambda src: dp_copy(snd.at[src], rcv.at[src], ss, rs, src, src).wait_recv())

    def swap_sent(snd, rcv, ss, rs):
        others(lambda peer: dp_copy(snd.at[peer], rcv.at[me], ss, rs, peer, me).wait_send())

    def spread(buf, ss, rs):
        others(lambda peer: dp_copy(buf.at[me], buf.at[me], ss, rs, peer, me).start())

    def spread_recv(buf, ss, rs):
        others_back(lambda src: dp_copy(buf.at[src], buf.at[src], ss, rs, src, src).wait_recv())

    def spread_sent(buf, ss, rs):
        others(lambda peer: dp_copy(buf.at[me], buf.at[me], ss, rs, peer, me).wait_send())

    def hand(b, t, ss, rs, src, dst):
        return pltpu.make_async_remote_copy(
            src_ref=src.at[b, t], dst_ref=dst.at[b, t], send_sem=ss.at[b, t],
            recv_sem=rs.at[b, t], device_id={"section": 1 - sec}, device_id_type=MESH,
        )

    def both(sems, b):
        return sems[0].at[b], sems[1].at[b]

    c_sem, b_sem, d_sem = (c_ss, c_rs), (b_ss, b_rs), (d_ss, d_rs)
    ro, ao = (ro_ss, ro_rs), (ao_ss, ao_rs)
    ry, ay, rh = (ry_ss, ry_rs), (ay_ss, ay_rs), (rh_ss, rh_rs)
    ah, ra, aa = (ah_ss, ah_rs), (ra_ss, ra_rs), (aa_ss, aa_rs)
    dn, df = (dn_ss, dn_rs), (df_ss, df_rs)

    row = iota((BLOCK, BLOCK), 0)
    col = iota((BLOCK, BLOCK), 1)
    eye = row == col
    earlier = (row > col).astype(f32).astype(bf16)
    every = jnp.ones((BLOCK, BLOCK), bf16)
    lane = iota((BLOCK, SMALL), 1)
    slot_lane = iota((BLOCK, SLOTS), 1)
    slot_sub = iota((SLOTS, BLOCK), 0)

    def to_col(values):
        return jnp.sum(jnp.where(eye, values, 0.0), axis=1, keepdims=True)

    def to_row(values):
        return jnp.sum(jnp.where(eye, values, 0.0), axis=0, keepdims=True)

    rpad[...] = jnp.zeros((SMALL, D), bf16)
    rpad[0:32, :] = router[0]
    for b in range(2):
        named = routes[0, :, b * BLOCK : (b + 1) * BLOCK].astype(f32)
        e0 = to_col(named[0:1, :]).astype(jnp.int32)
        e1 = to_col(named[1:2, :]).astype(jnp.int32)
        hit0 = (lane == e0).astype(f32)
        hit1 = (lane == e1).astype(f32)
        rank0 = jnp.sum(nn(earlier, hit0.astype(bf16)) * hit0, axis=1, keepdims=True)
        rank1 = jnp.sum(
            (nn(earlier, hit1.astype(bf16)) + nn(every, hit0.astype(bf16))) * hit1,
            axis=1, keepdims=True,
        )
        slot0 = (e0 % 2) * ER + (e0 // 2) * PAD + rank0.astype(jnp.int32)
        slot1 = (e1 % 2) * ER + (e1 // 2) * PAD + rank1.astype(jnp.int32)
        slots[b, :, 0:1] = slot0
        slots[b, :, 1:2] = slot1
        hits[b, 0] = hit0
        hits[b, 1] = hit1
        row0 = to_row(slot0.astype(f32)).astype(jnp.int32)
        row1 = to_row(slot1.astype(f32)).astype(jnp.int32)
        pick[b] = ((slot_sub == row0) | (slot_sub == row1)).astype(f32).astype(bf16)

    gain0 = gains[0, 0:1, :].astype(f32)
    gain1 = gains[0, 1:2, :].astype(f32)
    gap = row - col
    head_of = iota((BLOCK, HF), 1) // (HF // HEADS)

    @pl.when(first)
    def _():
        load_x.wait()

    @pl.when(second)
    def _():
        load_g.wait()

    load_qkv.wait()
    load_att.wait()
    load_in.start()
    load_out.start()

    @pl.when(second)
    def _():
        pl.semaphore_wait(barrier, DP + TZ - 1)
        pl.semaphore_wait(turn_sem, 1)
        gather_start(wall, w_ss, w_rs)

    for b in range(2):
        rows = slice(b * BLOCK, (b + 1) * BLOCK)

        @pl.when(second)
        def _():
            for t in range(TZ):
                hand(b, t, hand_ss, hand_rs, gact, xin).wait_recv()

        x = xin[b].reshape(BLOCK, D).astype(f32)
        normed[rows, :] = (x * rms_scale(x) * gain0).astype(bf16)
        for j in range(3):
            qkv[j, rows, :] = nt(normed[rows, :], w_qkv[j]).astype(bf16)
        seg_row = segments[b : b + 1, :].astype(f32)
        allowed = (gap >= 0) & (seg_row == to_col(seg_row))
        q = qkv[0, rows, :]
        k = qkv[1, rows, :]
        v = qkv[2, rows, :]
        context = jnp.zeros((BLOCK, HF), f32)
        for h in range(HEADS):
            bias = jnp.broadcast_to(bias_tab[0, h : h + 1, 0:1].astype(f32), (BLOCK, BLOCK))
            for n, edge in enumerate(bucket_edges):
                bias = jnp.where(
                    gap >= edge, bias_tab[0, h : h + 1, n + 1 : n + 2].astype(f32), bias
                )
            score = nt(jnp.where(head_of == h, q, jnp.zeros_like(q)), k) * 0.125 + bias
            score = jnp.where(allowed, score, masked_score)
            score = jnp.exp(score - jnp.max(score, axis=-1, keepdims=True))
            prob = score / jnp.sum(score, axis=-1, keepdims=True)
            probs[b * HEADS + h] = prob
            context = jnp.where(head_of == h, nn(prob.astype(bf16), v), context)
        call[b, mz] = context.astype(bf16)

        @pl.when(first)
        def _():
            if b == 0:
                pl.semaphore_wait(barrier, DP + TZ - 1)
            part_o[b] = nn(call[b, mz], wall[mz]).astype(bf16).reshape(TZ, OWN, D)
            scatter_start(part_o.at[b], rs_o.at[b], *both(ro, b))

        @pl.when(second)
        def _():
            gather_start(call.at[b], *both(c_sem, b))

    def dispatch(chosen, values, snd, rcv, sems, b):
        for e in range(2):
            out = nn(chosen[b, ER * e : ER * (e + 1), :], values).astype(bf16)
            snd[b, e] = out.reshape(DP, PAD, D)
            swap_start(snd.at[b, e], rcv.at[b, e], sems[0].at[b, e], sems[1].at[b, e])

    def dispatch_grad(b):
        dispatch(pick_g, gin[b].reshape(BLOCK, D), send_d, recv_d, d_sem, b)

    @pl.when(first)
    def _():
        for b in range(2):
            o_full[b, mz] = scatter_sum(part_o.at[b], rs_o.at[b], *both(ro, b)).astype(bf16)
            gather_start(o_full.at[b], *both(ao, b))

    for b in range(2):
        @pl.when(first)
        def _():
            for i in range(1, TZ):
                gather_recv(o_full.at[b], *both(ao, b), i)
            if b == 1:
                pl.semaphore_signal(
                    turn_sem, inc=1, device_id={"section": 1 - sec}, device_id_type=MESH
                )
            hidden[b] = xin[b].reshape(BLOCK, D).astype(f32) + o_full[b].reshape(BLOCK, D).astype(f32)

        @pl.when(second)
        def _():
            for i in range(1, TZ):
                gather_recv(call.at[b], *both(c_sem, b), i)
                if b == 0:
                    gather_recv(wall, w_ss, w_rs, i)
            total = xin[b].reshape(BLOCK, D).astype(f32)
            for t in range(TZ):
                total += nn(call[b, t], wall[t])
            hidden[b] = total

        h = hidden[b]
        scale = rms_scale(h)
        hid_scale[b] = scale
        normed2[b] = (h * scale * gain1).astype(bf16)
        dispatch(pick, normed2[b], send_b, recv_b, b_sem, b)

        z = nt(normed2[b], rpad[...])
        z0 = jnp.sum(z * hits[b, 0], axis=1, keepdims=True)
        z1 = jnp.sum(z * hits[b, 1], axis=1, keepdims=True)
        g0 = 1.0 / (1.0 + jnp.exp(z1 - z0))
        g1 = 1.0 / (1.0 + jnp.exp(z0 - z1))
        gate[b, :, 0:1] = g0
        gate[b, :, 1:2] = g1
        slot0 = slots[b, :, 0:1]
        slot1 = slots[b, :, 1:2]
        row0 = to_row(slot0.astype(f32)).astype(jnp.int32)
        row1 = to_row(slot1.astype(f32)).astype(jnp.int32)
        pick_g[b] = (
            jnp.where(slot_sub == row0, to_row(g0), 0.0)
            + jnp.where(slot_sub == row1, to_row(g1), 0.0)
        ).astype(bf16)

        @pl.when(second)
        def _():
            dispatch_grad(b)

        ptg[b] = (
            jnp.where(slot_lane == slot0, g0, 0.0) + jnp.where(slot_lane == slot1, g1, 0.0)
        ).astype(bf16)

    root = 0.7978845608028654
    saved = []

    def save(b, n, src, dst):
        copy = pltpu.make_async_copy(src.at[b], dst.at[b], out_sem.at[b, n])
        copy.start()
        saved.append(copy)

    def expert_forward(b, e):
        swap_recv(send_b.at[b, e], recv_b.at[b, e], b_ss.at[b, e], b_rs.at[b, e])
        x = recv_b[b, e].reshape(ER, D)
        for n in range(3):
            cols = slice(256 * n, 256 * (n + 1))
            pre = nn(x, w_in[e, :, cols])
            square = pre * pre
            wave = jnp.tanh(root * pre * (1.0 + 0.044715 * square))
            lift = 0.5 * (1.0 + wave)
            act[b, e, :, cols] = (pre * lift).astype(bf16)
            slope = lift + 0.5 * root * pre * (1.0 - wave * wave) * (1.0 + 0.134145 * square)
            dact[b, e, :, cols] = slope.astype(bf16)
        out = nn(act[b, e], w_out[e])
        send_e[b, e] = out.astype(bf16).reshape(DP, PAD, D)

    def return_rows(b, e):
        swap_start(send_e.at[b, e], recv_e.at[b, e], e_ss.at[b, e], e_rs.at[b, e])

    def expert_backward(b, e):
        swap_recv(send_d.at[b, e], recv_d.at[b, e], d_ss.at[b, e], d_rs.at[b, e])
        de = recv_d[b, e].reshape(ER, D)
        for n in range(3):
            cols = slice(256 * n, 256 * (n + 1))
            grad = nt(de, w_out[e, cols, :])
            dpre[b, e, :, cols] = (grad * dact[b, e, :, cols].astype(f32)).astype(bf16)
        out = nt(dpre[b, e], w_in[e])
        send_x[b, e, :, :, 0:D] = out.astype(bf16).reshape(DP, PAD, D)
        rows = send_e[b, e].reshape(ER, D).astype(f32)
        weight = jnp.sum(rows * de.astype(f32), axis=1, keepdims=True)
        coarse = weight.astype(bf16).astype(f32)
        place = iota((ER, 128), 1)
        pair = jnp.where(place == 0, coarse, jnp.where(place == 1, weight - coarse, 0.0))
        send_x[b, e, :, :, D:] = pair.astype(bf16).reshape(DP, PAD, 128)
        swap_start(send_x.at[b, e], recv_x.at[b, e], x_ss.at[b, e], x_rs.at[b, e])

    def each_expert(step):
        def one(e, carry):
            step(e)
            return carry

        lax.fori_loop(0, 2, one, 0)

    def each_part(step):
        def one(i, carry):
            step(i // 2, i % 2)
            return carry

        lax.fori_loop(0, 4, one, 0)

    def combine(b):
        for e in range(2):
            swap_recv(send_e.at[b, e], recv_e.at[b, e], e_ss.at[b, e], e_rs.at[b, e])
        out = nn(ptg[b], recv_e[b].reshape(SLOTS, D))
        part_y[b] = out.astype(bf16).reshape(TZ, OWN, D)
        scatter_start(part_y.at[b], rs_y.at[b], *both(ry, b))

    def settle(b):
        own = pl.ds(pl.multiple_of(mz * OWN, OWN), OWN)
        total = scatter_sum(part_y.at[b], rs_y.at[b], *both(ry, b)) + hidden[b, own, :]
        gact[b, mz] = total.astype(bf16)
        gather_start(gact.at[b], *both(ay, b))

    load_in.wait()
    load_out.wait()

    @pl.when(first)
    def _():
        def part(b, e):
            expert_forward(b, e)
            return_rows(b, e)

        each_part(part)

    @pl.when(second)
    def _():
        def block(b, carry):
            each_expert(lambda e: expert_forward(b, e))
            each_expert(lambda e: expert_backward(b, e))
            return carry

        lax.fori_loop(0, 2, block, 0)
        each_part(return_rows)

    for b in range(2):
        save(b, 0, recv_b, xe_out)

    @pl.when(first)
    def _():
        combine(0)
        combine(1)
        for b in range(2):
            settle(b)
            hand(b, mz, hand_ss, hand_rs, gact, xin).start()
        for b in range(2):
            for i in range(1, TZ):
                gather_recv(gact.at[b], *both(ay, b), i)
                hand(b, lax.rem(mz + i, TZ), hand_ss, hand_rs, gact, xin).start()
        for b in range(2):
            for t in range(TZ):
                hand(b, t, back_ss, back_rs, in_full, gin).wait_recv()
            dispatch_grad(b)
        each_part(expert_backward)

    for b in range(2):
        save(b, 1, recv_d, de_out)

    for b in range(2):
        pt0 = (slot_lane == slots[b, :, 0:1]).astype(f32).astype(bf16)
        pt1 = (slot_lane == slots[b, :, 1:2]).astype(f32).astype(bf16)
        for e in range(2):
            swap_recv(send_x.at[b, e], recv_x.at[b, e], x_ss.at[b, e], x_rs.at[b, e])
        if b == 1:
            @pl.when(first)
            def _():
                pl.semaphore_signal(
                    turn_sem, inc=1, device_id={"section": 1 - sec}, device_id_type=MESH
                )

        back = recv_x[b].reshape(SLOTS, WIDE)
        q0 = jnp.sum(nn(pt0, back[:, D:]), axis=1, keepdims=True)
        q1 = jnp.sum(nn(pt1, back[:, D:]), axis=1, keepdims=True)
        dc = gate[b, :, 1:2] * q0 - gate[b, :, 0:1] * q1
        dz = ((hits[b, 0] - hits[b, 1]) * dc).astype(bf16)
        db = nn(pt0 + pt1, back[:, 0:D]) + nn(dz, rpad[...])
        part_h[b] = db.astype(bf16).reshape(TZ, OWN, D)
        scatter_start(part_h.at[b], rs_h.at[b], *both(rh, b))
        unit = (lane == GAIN1).astype(f32).astype(bf16)
        small = tn(dz, normed2[b])
        small += tn(unit, (db * hidden[b] * hid_scale[b]).astype(bf16))
        if b == 0:
            small_acc[...] = small
        else:
            small_acc[...] += small

    for b in range(2):
        own = pl.ds(pl.multiple_of(mz * OWN, OWN), OWN)
        s_own = hid_scale[b, own, :]
        hat = hidden[b, own, :] * s_own
        lifted = scatter_sum(part_h.at[b], rs_h.at[b], *both(rh, b)) * gain1
        total = gin[b, mz].astype(f32) + s_own * (
            lifted - hat * jnp.mean(lifted * hat, axis=-1, keepdims=True)
        )
        dh_own[b] = total
        dh_full[b, mz] = total.astype(bf16)
        gather_start(dh_full.at[b], *both(ah, b))

    for b in range(2):
        rows = slice(b * BLOCK, (b + 1) * BLOCK)
        for i in range(1, TZ):
            gather_recv(dh_full.at[b], *both(ah, b), i)
        dc = nt(dh_full[b].reshape(BLOCK, D), wall[mz]).astype(bf16)
        q = qkv[0, rows, :]
        k = qkv[1, rows, :]
        v = qkv[2, rows, :]
        dq = jnp.zeros((BLOCK, HF), f32)
        dk = jnp.zeros((BLOCK, HF), f32)
        dv = jnp.zeros((BLOCK, HF), f32)
        for h in range(HEADS):
            mine = head_of == h
            prob = probs[b * HEADS + h]
            dp = nt(jnp.where(mine, dc, jnp.zeros_like(dc)), v)
            ds = (prob * (dp - jnp.sum(prob * dp, axis=-1, keepdims=True))).astype(bf16)
            if b == 0:
                score_sum[h] = ds.astype(f32)
            else:
                score_sum[h] += ds.astype(f32)
            dq = jnp.where(mine, nn(ds, k), dq)
            dk = jnp.where(mine, tn(ds, q), dk)
            dv = jnp.where(mine, tn(prob.astype(bf16), dc), dv)
        dq_all[0, rows, :] = (dq * 0.125).astype(bf16)
        dq_all[1, rows, :] = (dk * 0.125).astype(bf16)
        dq_all[2, rows, :] = dv.astype(bf16)
        da = nn(dq_all[0, rows, :], w_qkv[0])
        da += nn(dq_all[1, rows, :], w_qkv[1])
        da += nn(dq_all[2, rows, :], w_qkv[2])
        part_a[b] = da.astype(bf16).reshape(TZ, OWN, D)
        scatter_start(part_a.at[b], rs_a.at[b], *both(ra, b))

    def dense_part():
        own_context = jnp.concatenate([call[0, mz], call[1, mz]], axis=0)
        for n in range(2):
            cols = slice(HALF * n, HALF * (n + 1))
            for j in range(3):
                out = tn(dq_all[j], normed[:, cols]).astype(bf16)
                dense_s[n, 4 * j : 4 * j + 4] = out.reshape(4, CUT, HALF)
            grad = dh_full[:, :, :, cols].reshape(ROWS, HALF)
            dense_s[n, 12:16] = tn(own_context, grad).astype(bf16).reshape(4, CUT, HALF)
            swap_start(dense_s.at[n], dense_r.at[n], *both(dn, n))
        small = small_acc[...]
        unit = (lane == GAIN0).astype(f32).astype(bf16)
        for b in range(2):
            x = xin[b].reshape(BLOCK, D).astype(f32)
            da = part_a[b].reshape(BLOCK, D).astype(f32)
            small += tn(unit, (da * x * rms_scale(x)).astype(bf16))
        bias_rows = []
        for h in range(HEADS):
            for n in range(len(EDGES)):
                hit = gap >= EDGES[n]
                if n + 1 < len(EDGES):
                    hit = hit & (gap < EDGES[n + 1])
                bias_rows.append(jnp.sum(jnp.where(hit, score_sum[h], 0.0), axis=0, keepdims=True))
        bias_col = jnp.sum(jnp.concatenate(bias_rows, axis=0), axis=1, keepdims=True)
        diagonal = iota((SMALL, 128), 0) == iota((SMALL, 128), 1)
        bias_row = jnp.sum(jnp.where(diagonal, bias_col, 0.0), axis=0, keepdims=True)
        mine = iota((SMALL, 128), 0) == BIAS + mz
        for j in range(PARTS):
            piece = small[:, 128 * j : 128 * (j + 1)]
            if j == 0:
                piece += jnp.where(mine, bias_row, 0.0)
            small_s[j] = piece.astype(bf16)

            @pl.when(me != j)
            def _():
                dp_copy(small_s.at[j], small_r.at[me], sm_ss, sm_rs, j, me).start()

    dense_part()

    for b in range(2):
        x_own = xin[b, mz].astype(f32)
        r_own = rms_scale(x_own)
        hat = x_own * r_own
        lifted = scatter_sum(part_a.at[b], rs_a.at[b], *both(ra, b)) * gain0
        total = dh_own[b] + r_own * (lifted - hat * jnp.mean(lifted * hat, axis=-1, keepdims=True))
        in_full[b, mz] = total.astype(bf16)
        gather_start(in_full.at[b], *both(aa, b))

        @pl.when(second)
        def _():
            hand(b, mz, back_ss, back_rs, in_full, gin).start()

    for b in range(2):
        for i in range(1, TZ):
            gather_recv(in_full.at[b], *both(aa, b), i)

            @pl.when(second)
            def _():
                hand(b, lax.rem(mz + i, TZ), back_ss, back_rs, in_full, gin).start()

    save_grad = pltpu.make_async_copy(in_full, grad_out, end_sem.at[1])
    save_grad.start()

    @pl.when(second)
    def _():
        for b in range(2):
            combine(b)
        for b in range(2):
            settle(b)
        for b in range(2):
            for i in range(1, TZ):
                gather_recv(gact.at[b], *both(ay, b), i)

    save_act = pltpu.make_async_copy(gact, act_out, end_sem.at[0])
    save_act.start()

    holds = me < PARTS

    @pl.when(second)
    def _():
        pl.semaphore_wait(turn_sem, 1)

    for n in range(2):
        swap_recv(dense_s.at[n], dense_r.at[n], *both(dn, n))
        total = dense_r[n, 0].astype(f32)
        for p in range(1, DP):
            total += dense_r[n, p].astype(f32)
        dense_f[n, me] = total.astype(bf16)
        spread(dense_f.at[n], *both(df, n))

    @pl.when(holds)
    def _():
        small_r[me] = small_s[me]
        others_back(
            lambda src: dp_copy(small_s.at[src], small_r.at[src], sm_ss, sm_rs, src, src).wait_recv()
        )
        total = small_r[0].astype(f32)
        for p in range(1, DP):
            total += small_r[p].astype(f32)
        small_z[mz] = total.astype(bf16)
        gather_start(small_z, sz_ss, sz_rs)
        for i in range(1, TZ):
            gather_recv(small_z, sz_ss, sz_rs, i)
        total = small_z[0].astype(f32)
        for t in range(1, TZ):
            total += small_z[t].astype(f32)
        small_f[me] = total.astype(bf16)
        spread(small_f, sf_ss, sf_rs)

    @pl.when(second)
    def _():
        gather_sent(wall, w_ss, w_rs)

    for b in range(2):
        for e in range(2):
            swap_sent(send_b.at[b, e], recv_b.at[b, e], b_ss.at[b, e], b_rs.at[b, e])
            swap_sent(send_e.at[b, e], recv_e.at[b, e], e_ss.at[b, e], e_rs.at[b, e])
            swap_sent(send_d.at[b, e], recv_d.at[b, e], d_ss.at[b, e], d_rs.at[b, e])
            swap_sent(send_x.at[b, e], recv_x.at[b, e], x_ss.at[b, e], x_rs.at[b, e])
        scatter_sent(part_y.at[b], rs_y.at[b], *both(ry, b))
        gather_sent(gact.at[b], *both(ay, b))
        scatter_sent(part_h.at[b], rs_h.at[b], *both(rh, b))
        gather_sent(dh_full.at[b], *both(ah, b))
        scatter_sent(part_a.at[b], rs_a.at[b], *both(ra, b))
        gather_sent(in_full.at[b], *both(aa, b))

        @pl.when(first)
        def _():
            scatter_sent(part_o.at[b], rs_o.at[b], *both(ro, b))
            gather_sent(o_full.at[b], *both(ao, b))
            for t in range(TZ):
                hand(b, t, hand_ss, hand_rs, gact, xin).wait_send()

        @pl.when(second)
        def _():
            gather_sent(call.at[b], *both(c_sem, b))
            for t in range(TZ):
                hand(b, t, back_ss, back_rs, in_full, gin).wait_send()

    for n in range(2):
        swap_sent(dense_s.at[n], dense_r.at[n], *both(dn, n))
    for j in range(PARTS):
        @pl.when(me != j)
        def _():
            dp_copy(small_s.at[j], small_r.at[me], sm_ss, sm_rs, j, me).wait_send()

    @pl.when(holds)
    def _():
        gather_sent(small_z, sz_ss, sz_rs)
        spread_sent(small_f, sf_ss, sf_rs)

    for copy in saved:
        copy.wait()
    for n in range(2):
        spread_recv(dense_f.at[n], *both(df, n))
        pltpu.make_async_copy(dense_f.at[n], dense_out.at[n], end_sem.at[2 + n]).start()
    for j in range(PARTS):
        @pl.when(me != j)
        def _():
            dp_copy(small_f.at[j], small_f.at[j], sf_ss, sf_rs, j, j).wait_recv()

        small_out[:, 128 * j : 128 * (j + 1)] = small_f[j].astype(f32)
    held = small_f[0].astype(f32)
    mine = iota((SMALL, 128), 0) == BIAS + mz
    small_out[BIAS : BIAS + 1, 0:128] = jnp.sum(jnp.where(mine, held, 0.0), axis=0, keepdims=True)
    for n in range(2):
        spread_sent(dense_f.at[n], *both(df, n))
    save_act.wait()
    save_grad.wait()
    for n in range(2):
        pltpu.make_async_copy(dense_f.at[n], dense_out.at[n], end_sem.at[2 + n]).wait()


def last_outputs(
    xe, dpre, u, de, act, grads, dense, small,
    inner, outer, act_out, grads_out, qkv_out, attn_out, gain_out, router_out, bias_out,
    inner_v, outer_v, grads_f, dense_f, out_sem,
):
    sent = []

    def store(src, dst):
        copy = pltpu.make_async_copy(src, dst, out_sem.at[len(sent)])
        copy.start()
        sent.append(copy)

    store(act, act_out)
    grads_f[...] = grads[...].reshape(ROWS, D).astype(f32)
    store(grads_f, grads_out)
    for n in range(2):
        dense_f[:, HALF * n : HALF * (n + 1)] = dense[n].reshape(D, HALF).astype(f32)
    for j in range(3):
        store(dense_f.at[HF * j : HF * (j + 1)], qkv_out.at[j])
    store(dense_f.at[3 * HF : D], attn_out)
    for e in range(2):
        for one, two, total, out in ((xe, dpre, inner_v, inner), (u, de, outer_v, outer)):
            right = two[:, e].reshape(SLOTS, D)
            for i in range(3):
                cols = slice(256 * i, 256 * (i + 1))
                left = one[:, e, :, cols] if one is u else one[:, e, :, :, cols]
                total[e, cols, :] = tn(left.reshape(SLOTS, 256), right)
                store(total.at[e, cols], out.at[e, cols])
    router_out[...] = small[0:32, :]
    gain_out[...] = small[GAIN0 : GAIN1 + 1, :]
    for h in range(HEADS):
        bias_out[h] = small[BIAS : BIAS + 1, 16 * h : 16 * (h + 1)]
    for copy in sent:
        copy.wait()


def body(
    tokens, cotangent, norm_gains, w_qkv, w_attn_out, bias_table, router, w_in, w_out, routes, segments
):
    vmem = pl.BlockSpec(memory_space=pltpu.VMEM)
    hbm = pl.BlockSpec(memory_space=pl.ANY)
    dma = pltpu.SemaphoreType.DMA
    rows4 = pltpu.VMEM((2, TZ, OWN, D), bf16)
    messages = pltpu.VMEM((2, 2, DP, PAD, D), bf16)
    wide = pltpu.VMEM((2, 2, DP, PAD, WIDE), bf16)
    expert_rows = pltpu.VMEM((2, 2, ER, D), bf16)
    cuts = pltpu.VMEM((2, DP, CUT, HALF), bf16)
    pieces = pltpu.VMEM((DP, SMALL, 128), bf16)
    scratch = dict(
        xin=rows4,
        gin=rows4,
        w_qkv=pltpu.VMEM((3, HF, D), bf16),
        w_in=pltpu.VMEM((2, D, D), bf16),
        w_out=pltpu.VMEM((2, D, D), bf16),
        wall=pltpu.VMEM((TZ, HF, D), bf16),
        part_o=rows4, rs_o=rows4, o_full=rows4,
        call=pltpu.VMEM((2, TZ, BLOCK, HF), bf16),
        normed=pltpu.VMEM((ROWS, D), bf16),
        qkv=pltpu.VMEM((3, ROWS, HF), bf16),
        probs=pltpu.VMEM((2 * HEADS, BLOCK, BLOCK), f32),
        hidden=pltpu.VMEM((2, BLOCK, D), f32),
        hid_scale=pltpu.VMEM((2, BLOCK, 1), f32),
        normed2=pltpu.VMEM((2, BLOCK, D), bf16),
        rpad=pltpu.VMEM((SMALL, D), bf16),
        gate=pltpu.VMEM((2, BLOCK, 2), f32),
        slots=pltpu.VMEM((2, BLOCK, 2), jnp.int32),
        hits=pltpu.VMEM((2, 2, BLOCK, SMALL), f32),
        ptg=pltpu.VMEM((2, BLOCK, SLOTS), bf16),
        pick=pltpu.VMEM((2, SLOTS, BLOCK), bf16),
        pick_g=pltpu.VMEM((2, SLOTS, BLOCK), bf16),
        send_b=messages, recv_b=messages, send_e=messages, recv_e=messages,
        send_d=messages, recv_d=messages, send_x=wide, recv_x=wide,
        dact=expert_rows,
        part_y=rows4, rs_y=rows4, part_h=rows4, rs_h=rows4,
        dh_own=pltpu.VMEM((2, OWN, D), f32),
        dh_full=rows4, part_a=rows4, rs_a=rows4, in_full=rows4,
        dq_all=pltpu.VMEM((3, ROWS, HF), bf16),
        score_sum=pltpu.VMEM((HEADS, BLOCK, BLOCK), f32),
        gact=rows4,
        dense_s=cuts, dense_r=cuts, dense_f=cuts,
        small_acc=pltpu.VMEM((SMALL, D), f32),
        small_s=pieces, small_r=pieces,
        small_z=pltpu.VMEM((TZ, SMALL, 128), bf16),
        small_f=pieces,
        ld_sem=dma((5,)),
        out_sem=dma((2, 2)),
        end_sem=dma((4,)),
        w_ss=dma((TZ,)), w_rs=dma((TZ,)),
        c_ss=dma((2, TZ)), c_rs=dma((2, TZ)),
    )
    for name in ("b", "e", "d", "x"):
        scratch[name + "_ss"] = dma((2, 2, DP))
        scratch[name + "_rs"] = dma((2, 2, DP))
    for name in ("ro", "ao", "ry", "ay", "rh", "ah", "ra", "aa", "hand", "back"):
        scratch[name + "_ss"] = dma((2, TZ))
        scratch[name + "_rs"] = dma((2, TZ))
    for name in ("dn", "df"):
        scratch[name + "_ss"] = dma((2, DP))
        scratch[name + "_rs"] = dma((2, DP))
    for name, count in (("sm", DP), ("sz", TZ), ("sf", DP)):
        scratch[name + "_ss"] = dma((count,))
        scratch[name + "_rs"] = dma((count,))
    scratch["turn_sem"] = pltpu.SemaphoreType.REGULAR

    shape = jax.ShapeDtypeStruct
    near = pltpu.VMEM
    act, grads, dense, small, xe, u, dpre, de = pl.pallas_call(
        kernel,
        out_shape=(
            near((2, TZ, OWN, D), bf16),
            near((2, TZ, OWN, D), bf16),
            near((2, DP, CUT, HALF), bf16),
            near((SMALL, D), f32),
            near((2, 2, DP, PAD, D), bf16),
            near((2, 2, ER, D), bf16),
            near((2, 2, ER, D), bf16),
            near((2, 2, DP, PAD, D), bf16),
        ),
        in_specs=[hbm, hbm, vmem, hbm, hbm, vmem, vmem, hbm, hbm, vmem, vmem],
        out_specs=(vmem,) * 8,
        scratch_shapes=list(scratch.values()),
        compiler_params=pltpu.CompilerParams(
            collective_id=0, has_side_effects=True, vmem_limit_bytes=55 * 1024 * 1024
        ),
        name="layers",
    )(
        tokens.reshape(2, TZ, OWN, D), cotangent.reshape(2, TZ, OWN, D), norm_gains,
        w_qkv[0].swapaxes(1, 2), w_attn_out[0], bias_table.swapaxes(1, 2),
        router.swapaxes(1, 2), w_in[0], w_out[0], routes.swapaxes(1, 2), segments,
    )

    inner, outer, act, grads, qkv_grad, attn_grad, gain_grad, router_grad, bias_grad = pl.pallas_call(
        last_outputs,
        out_shape=(
            shape((2, D, D), f32),
            shape((2, D, D), f32),
            shape((2, TZ, OWN, D), bf16),
            shape((ROWS, D), f32),
            shape((3, HF, D), f32),
            shape((HF, D), f32),
            shape((2, D), f32),
            shape((32, D), f32),
            shape((HEADS, 1, 16), f32),
        ),
        in_specs=[vmem] * 8,
        out_specs=(hbm,) * 6 + (vmem,) * 3,
        scratch_shapes=[
            pltpu.VMEM((2, D, D), f32),
            pltpu.VMEM((2, D, D), f32),
            pltpu.VMEM((ROWS, D), f32),
            pltpu.VMEM((D, D), f32),
            dma((18,)),
        ],
        compiler_params=pltpu.CompilerParams(vmem_limit_bytes=20 * 1024 * 1024),
        name="last_outputs",
    )(xe, dpre, u, de, act, grads, dense, small)

    return (
        act.reshape(ROWS, D)[None],
        grads[None],
        gain_grad[None],
        qkv_grad.swapaxes(1, 2)[None],
        attn_grad[None],
        bias_grad.transpose(1, 2, 0),
        router_grad.T[None],
        inner[None],
        outer[None],
    )


def solution(mesh):
    in_specs = (
        P("dp", None),
        P("dp", None),
        P("section", None, None),
        P("section", None, None, "tensor"),
        P("section", "tensor", None),
        P("section", None, "tensor"),
        P("section", None, None),
        P("section", "dp", None, "tensor"),
        P("section", "dp", "tensor", None),
        P("section", "dp", None),
        P("dp", None),
    )
    out_specs = (
        P("section", "dp", None),
        P("section", "dp", None),
        P("section", None, None),
        P("section", None, None, "tensor"),
        P("section", "tensor", None),
        P("section", None, "tensor"),
        P("section", None, None),
        P("section", "dp", None, "tensor"),
        P("section", "dp", "tensor", None),
    )
    return jax.shard_map(body, mesh=mesh, in_specs=in_specs, out_specs=out_specs, check_vma=False)
```

```python
import jax
import jax.numpy as jnp
from jax import lax
from jax.experimental import pallas as pl
from jax.experimental.pallas import tpu as pltpu
from jax.sharding import PartitionSpec as P

epsilon = 1e-06
masked_score = -1000000000.0
bucket_edges = (1, 2, 3, 4, 5, 6, 7, 8, 10, 13, 16, 20, 25, 32, 40)
MESH = pl.DeviceIdType.MESH
f32 = jnp.float32
bf16 = jnp.bfloat16

DP = 16
TZ = 4
ROWS = 256
BLOCK = 128
OWN = BLOCK // TZ
D = 768
HF = 192
HEADS = 3
PAD = 16
ER = DP * PAD
SLOTS = 2 * ER
WIDE = D + 128
CUT = D // DP
SMALL = 48
GAIN0, GAIN1, BIAS = 32, 33, 34
HALF = D // 2
PARTS = D // 128
EDGES = (0,) + bucket_edges


def nn(a, b):
    return lax.dot_general(a, b, (((1,), (0,)), ((), ())), preferred_element_type=f32)


def nt(a, b):
    return lax.dot_general(a, b, (((1,), (1,)), ((), ())), preferred_element_type=f32)


def tn(a, b):
    return lax.dot_general(a, b, (((0,), (0,)), ((), ())), preferred_element_type=f32)


def iota(shape, dim):
    return lax.broadcasted_iota(jnp.int32, shape, dim)


def rms_scale(values):
    return lax.rsqrt(jnp.mean(values * values, axis=-1, keepdims=True) + epsilon)


def kernel(
    tokens, cotangent, gains, w_qkv_hbm, w_att, bias_tab, router, w_in_hbm, w_out_hbm, routes, segments,
    act_out, grad_out, dense_out, small_out, xe_out, act, dpre, de_out,
    xin, gin, w_qkv, w_in, w_out, wall, part_o, rs_o, o_full, call, normed, qkv, probs, hidden, hid_scale, normed2, rpad,
    gate, slots, hits, ptg, pick, pick_g, send_b, recv_b, send_e, recv_e, send_d, recv_d, send_x,
    recv_x, dact, part_y, rs_y, part_h, rs_h, dh_own, dh_full, part_a, rs_a, in_full,
    dq_all, score_sum, gact, dense_s, dense_r, dense_f, small_acc, small_s, small_r, small_z, small_f,
    ld_sem, out_sem, end_sem, w_ss, w_rs, c_ss, c_rs, b_ss, b_rs, e_ss, e_rs, d_ss, d_rs, x_ss, x_rs,
    ro_ss, ro_rs, ao_ss, ao_rs, ry_ss, ry_rs, ay_ss, ay_rs, rh_ss, rh_rs, ah_ss, ah_rs, ra_ss, ra_rs, aa_ss, aa_rs,
    hand_ss, hand_rs, back_ss, back_rs, dn_ss, dn_rs, df_ss, df_rs, sm_ss, sm_rs, sz_ss, sz_rs,
    sf_ss, sf_rs, turn_sem,
):
    sec = lax.axis_index("section")
    me = lax.axis_index("dp")
    mz = lax.axis_index("tensor")
    first = sec == 0
    second = sec == 1

    load_in = pltpu.make_async_copy(w_in_hbm, w_in, ld_sem.at[0])
    load_out = pltpu.make_async_copy(w_out_hbm, w_out, ld_sem.at[1])
    load_qkv = pltpu.make_async_copy(w_qkv_hbm, w_qkv, ld_sem.at[2])
    load_att = pltpu.make_async_copy(w_att, wall.at[mz], ld_sem.at[3])
    load_x = pltpu.make_async_copy(tokens, xin, ld_sem.at[4])
    load_g = pltpu.make_async_copy(cotangent, gin, ld_sem.at[4])

    @pl.when(first)
    def _():
        load_x.start()

    @pl.when(second)
    def _():
        load_g.start()

    load_qkv.start()
    load_att.start()

    barrier = pltpu.get_barrier_semaphore()

    def greet(i, carry):
        pl.semaphore_signal(
            barrier, inc=1, device_id={"dp": lax.rem(me + i, DP)}, device_id_type=MESH
        )
        return carry

    lax.fori_loop(1, DP, greet, 0)
    for i in range(1, TZ):
        pl.semaphore_signal(
            barrier, inc=1, device_id={"tensor": lax.rem(mz + i, TZ)}, device_id_type=MESH
        )
    pl.semaphore_signal(barrier, inc=1, device_id={"section": 1 - sec}, device_id_type=MESH)

    def z_copy(src, dst, ss, rs, peer):
        return pltpu.make_async_remote_copy(
            src_ref=src, dst_ref=dst, send_sem=ss, recv_sem=rs,
            device_id={"tensor": peer}, device_id_type=MESH,
        )

    def z_round(buf, ss, rs):
        part = buf.at[pl.ds(0, TZ - 1)]
        return z_copy(part, part, ss, rs, lax.rem(mz + 1, TZ))

    def gather_start(buf, ss, rs):
        for i in range(1, TZ):
            z_copy(buf.at[mz], buf.at[mz], ss, rs, lax.rem(mz + i, TZ)).start()

    def gather_recv(buf, ss, rs):
        z_round(buf, ss, rs).wait_recv()

    def gather_sent(buf, ss, rs):
        z_round(buf, ss, rs).wait_send()

    def scatter_start(part, rcv, ss, rs):
        for i in range(1, TZ):
            peer = lax.rem(mz + i, TZ)
            z_copy(part.at[peer], rcv.at[mz], ss, rs, peer).start()

    def scatter_sum(part, rcv, ss, rs):
        z_round(rcv, ss, rs).wait_recv()
        total = part[mz].astype(f32)
        for i in range(1, TZ):
            total += rcv[lax.rem(mz + i, TZ)].astype(f32)
        return total

    def scatter_sent(part, rcv, ss, rs):
        z_round(part, ss, rs).wait_send()

    def dp_copy(src, dst, ss, rs, peer):
        return pltpu.make_async_remote_copy(
            src_ref=src, dst_ref=dst, send_sem=ss, recv_sem=rs,
            device_id={"dp": peer}, device_id_type=MESH,
        )

    def dp_round(buf, ss, rs, count=DP - 1):
        part = buf.at[pl.ds(0, count)]
        return dp_copy(part, part, ss, rs, lax.rem(me + 1, DP))

    def others(step):
        def one(i, carry):
            step(lax.rem(me + i, DP))
            return carry

        lax.fori_loop(1, DP, one, 0)

    def swap_start(snd, rcv, ss, rs):
        others(lambda peer: dp_copy(snd.at[peer], rcv.at[me], ss, rs, peer).start())
        rcv[me] = snd[me]

    def swap_recv(snd, rcv, ss, rs):
        dp_round(rcv, ss, rs).wait_recv()

    def swap_sent(snd, rcv, ss, rs):
        dp_round(snd, ss, rs).wait_send()

    def spread(buf, ss, rs):
        others(lambda peer: dp_copy(buf.at[me], buf.at[me], ss, rs, peer).start())

    def spread_recv(buf, ss, rs):
        dp_round(buf, ss, rs).wait_recv()

    def spread_sent(buf, ss, rs):
        dp_round(buf, ss, rs).wait_send()

    def hand(b, t, ss, rs, src, dst):
        return pltpu.make_async_remote_copy(
            src_ref=src.at[b, t], dst_ref=dst.at[b, t], send_sem=ss.at[b],
            recv_sem=rs.at[b], device_id={"section": 1 - sec}, device_id_type=MESH,
        )

    def hand_all(b, ss, rs, src, dst):
        return pltpu.make_async_remote_copy(
            src_ref=src.at[b], dst_ref=dst.at[b], send_sem=ss.at[b],
            recv_sem=rs.at[b], device_id={"section": 1 - sec}, device_id_type=MESH,
        )

    def both(sems, b):
        return sems[0].at[b], sems[1].at[b]

    c_sem, b_sem, d_sem = (c_ss, c_rs), (b_ss, b_rs), (d_ss, d_rs)
    ro, ao = (ro_ss, ro_rs), (ao_ss, ao_rs)
    ry, ay, rh = (ry_ss, ry_rs), (ay_ss, ay_rs), (rh_ss, rh_rs)
    ah, ra, aa = (ah_ss, ah_rs), (ra_ss, ra_rs), (aa_ss, aa_rs)
    dn, df = (dn_ss, dn_rs), (df_ss, df_rs)

    row = iota((BLOCK, BLOCK), 0)
    col = iota((BLOCK, BLOCK), 1)
    eye = row == col
    earlier = (row > col).astype(f32).astype(bf16)
    every = jnp.ones((BLOCK, BLOCK), bf16)
    lane = iota((BLOCK, SMALL), 1)
    slot_lane = iota((BLOCK, SLOTS), 1)
    slot_sub = iota((SLOTS, BLOCK), 0)

    def to_col(values):
        return jnp.sum(jnp.where(eye, values, 0.0), axis=1, keepdims=True)

    def to_row(values):
        return jnp.sum(jnp.where(eye, values, 0.0), axis=0, keepdims=True)

    rpad[...] = jnp.zeros((SMALL, D), bf16)
    rpad[0:32, :] = router[0]
    for b in range(2):
        named = routes[0, :, b * BLOCK : (b + 1) * BLOCK].astype(f32)
        e0 = to_col(named[0:1, :]).astype(jnp.int32)
        e1 = to_col(named[1:2, :]).astype(jnp.int32)
        hit0 = (lane == e0).astype(f32)
        hit1 = (lane == e1).astype(f32)
        rank0 = jnp.sum(nn(earlier, hit0.astype(bf16)) * hit0, axis=1, keepdims=True)
        rank1 = jnp.sum(
            (nn(earlier, hit1.astype(bf16)) + nn(every, hit0.astype(bf16))) * hit1,
            axis=1, keepdims=True,
        )
        slot0 = (e0 % 2) * ER + (e0 // 2) * PAD + rank0.astype(jnp.int32)
        slot1 = (e1 % 2) * ER + (e1 // 2) * PAD + rank1.astype(jnp.int32)
        slots[b, :, 0:1] = slot0
        slots[b, :, 1:2] = slot1
        hits[b, 0] = hit0
        hits[b, 1] = hit1
        row0 = to_row(slot0.astype(f32)).astype(jnp.int32)
        row1 = to_row(slot1.astype(f32)).astype(jnp.int32)
        pick[b] = ((slot_sub == row0) | (slot_sub == row1)).astype(f32).astype(bf16)

    gain0 = gains[0, 0:1, :].astype(f32)
    gain1 = gains[0, 1:2, :].astype(f32)
    gap = row - col
    head_of = iota((BLOCK, HF), 1) // (HF // HEADS)

    @pl.when(first)
    def _():
        load_x.wait()

    @pl.when(second)
    def _():
        load_g.wait()

    load_qkv.wait()
    load_att.wait()
    load_in.start()
    load_out.start()

    @pl.when(second)
    def _():
        pl.semaphore_wait(barrier, DP + TZ - 1)
        pl.semaphore_wait(turn_sem, 1)
        gather_start(wall, w_ss.at[0], w_rs.at[0])

    for b in range(2):
        rows = slice(b * BLOCK, (b + 1) * BLOCK)

        @pl.when(second)
        def _():
            hand_all(b, hand_ss, hand_rs, gact, xin).wait_recv()

        x = xin[b].reshape(BLOCK, D).astype(f32)
        normed[rows, :] = (x * rms_scale(x) * gain0).astype(bf16)
        for j in range(3):
            qkv[j, rows, :] = nt(normed[rows, :], w_qkv[j]).astype(bf16)
        seg_row = segments[b : b + 1, :].astype(f32)
        allowed = (gap >= 0) & (seg_row == to_col(seg_row))
        q = qkv[0, rows, :]
        k = qkv[1, rows, :]
        v = qkv[2, rows, :]
        context = jnp.zeros((BLOCK, HF), f32)
        for h in range(HEADS):
            bias = jnp.broadcast_to(bias_tab[0, h : h + 1, 0:1].astype(f32), (BLOCK, BLOCK))
            for n, edge in enumerate(bucket_edges):
                bias = jnp.where(
                    gap >= edge, bias_tab[0, h : h + 1, n + 1 : n + 2].astype(f32), bias
                )
            score = nt(jnp.where(head_of == h, q, jnp.zeros_like(q)), k) * 0.125 + bias
            score = jnp.where(allowed, score, masked_score)
            score = jnp.exp(score - jnp.max(score, axis=-1, keepdims=True))
            prob = score / jnp.sum(score, axis=-1, keepdims=True)
            probs[b * HEADS + h] = prob
            context = jnp.where(head_of == h, nn(prob.astype(bf16), v), context)
        call[b, mz] = context.astype(bf16)

        @pl.when(first)
        def _():
            if b == 0:
                pl.semaphore_wait(barrier, DP + TZ - 1)
            part_o[b] = nn(call[b, mz], wall[mz]).astype(bf16).reshape(TZ, OWN, D)
            scatter_start(part_o.at[b], rs_o.at[b], *both(ro, b))

        @pl.when(second)
        def _():
            gather_start(call.at[b], *both(c_sem, b))

    def dispatch(chosen, values, snd, rcv, sems, b):
        for e in range(2):
            out = nn(chosen[b, ER * e : ER * (e + 1), :], values).astype(bf16)
            snd[b, e] = out.reshape(DP, PAD, D)
            swap_start(snd.at[b, e], rcv.at[b, e], sems[0].at[b, e], sems[1].at[b, e])

    def dispatch_grad(b):
        dispatch(pick_g, gin[b].reshape(BLOCK, D), send_d, recv_d, d_sem, b)

    @pl.when(first)
    def _():
        for b in range(2):
            o_full[b, mz] = scatter_sum(part_o.at[b], rs_o.at[b], *both(ro, b)).astype(bf16)
            gather_start(o_full.at[b], *both(ao, b))

    for b in range(2):
        @pl.when(first)
        def _():
            gather_recv(o_full.at[b], *both(ao, b))
            if b == 1:
                pl.semaphore_signal(
                    turn_sem, inc=1, device_id={"section": 1 - sec}, device_id_type=MESH
                )
            hidden[b] = xin[b].reshape(BLOCK, D).astype(f32) + o_full[b].reshape(BLOCK, D).astype(f32)

        @pl.when(second)
        def _():
            gather_recv(call.at[b], *both(c_sem, b))
            if b == 0:
                gather_recv(wall, w_ss.at[0], w_rs.at[0])
            total = xin[b].reshape(BLOCK, D).astype(f32)
            for t in range(TZ):
                total += nn(call[b, t], wall[t])
            hidden[b] = total

        h = hidden[b]
        scale = rms_scale(h)
        hid_scale[b] = scale
        normed2[b] = (h * scale * gain1).astype(bf16)
        dispatch(pick, normed2[b], send_b, recv_b, b_sem, b)

        z = nt(normed2[b], rpad[...])
        z0 = jnp.sum(z * hits[b, 0], axis=1, keepdims=True)
        z1 = jnp.sum(z * hits[b, 1], axis=1, keepdims=True)
        g0 = 1.0 / (1.0 + jnp.exp(z1 - z0))
        g1 = 1.0 / (1.0 + jnp.exp(z0 - z1))
        gate[b, :, 0:1] = g0
        gate[b, :, 1:2] = g1
        slot0 = slots[b, :, 0:1]
        slot1 = slots[b, :, 1:2]
        row0 = to_row(slot0.astype(f32)).astype(jnp.int32)
        row1 = to_row(slot1.astype(f32)).astype(jnp.int32)
        pick_g[b] = (
            jnp.where(slot_sub == row0, to_row(g0), 0.0)
            + jnp.where(slot_sub == row1, to_row(g1), 0.0)
        ).astype(bf16)

        @pl.when(second)
        def _():
            dispatch_grad(b)

        ptg[b] = (
            jnp.where(slot_lane == slot0, g0, 0.0) + jnp.where(slot_lane == slot1, g1, 0.0)
        ).astype(bf16)

    root = 0.7978845608028654
    saved = []

    def save(b, n, src, dst):
        copy = pltpu.make_async_copy(src.at[b], dst.at[b], out_sem.at[b, n])
        copy.start()
        saved.append(copy)

    def expert_forward(b, e):
        swap_recv(send_b.at[b, e], recv_b.at[b, e], b_ss.at[b, e], b_rs.at[b, e])
        x = recv_b[b, e].reshape(ER, D)
        for n in range(3):
            cols = slice(256 * n, 256 * (n + 1))
            pre = nn(x, w_in[e, :, cols])
            square = pre * pre
            wave = jnp.tanh(root * pre * (1.0 + 0.044715 * square))
            lift = 0.5 * (1.0 + wave)
            act[b, e, :, cols] = (pre * lift).astype(bf16)
            slope = lift + 0.5 * root * pre * (1.0 - wave * wave) * (1.0 + 0.134145 * square)
            dact[b, e, :, cols] = slope.astype(bf16)
        out = nn(act[b, e], w_out[e])
        send_e[b, e] = out.astype(bf16).reshape(DP, PAD, D)

    def return_rows(b, e):
        swap_start(send_e.at[b, e], recv_e.at[b, e], e_ss.at[b, e], e_rs.at[b, e])

    def expert_backward(b, e):
        swap_recv(send_d.at[b, e], recv_d.at[b, e], d_ss.at[b, e], d_rs.at[b, e])
        de = recv_d[b, e].reshape(ER, D)
        for n in range(3):
            cols = slice(256 * n, 256 * (n + 1))
            grad = nt(de, w_out[e, cols, :])
            dpre[b, e, :, cols] = (grad * dact[b, e, :, cols].astype(f32)).astype(bf16)
        out = nt(dpre[b, e], w_in[e])
        send_x[b, e, :, :, 0:D] = out.astype(bf16).reshape(DP, PAD, D)
        rows = send_e[b, e].reshape(ER, D).astype(f32)
        weight = jnp.sum(rows * de.astype(f32), axis=1, keepdims=True)
        coarse = weight.astype(bf16).astype(f32)
        place = iota((ER, 128), 1)
        pair = jnp.where(place == 0, coarse, jnp.where(place == 1, weight - coarse, 0.0))
        send_x[b, e, :, :, D:] = pair.astype(bf16).reshape(DP, PAD, 128)
        swap_start(send_x.at[b, e], recv_x.at[b, e], x_ss.at[b, e], x_rs.at[b, e])

    def each_expert(step):
        def one(e, carry):
            step(e)
            return carry

        lax.fori_loop(0, 2, one, 0)

    def each_part(step):
        def one(i, carry):
            step(i // 2, i % 2)
            return carry

        lax.fori_loop(0, 4, one, 0)

    def combine(b):
        for e in range(2):
            swap_recv(send_e.at[b, e], recv_e.at[b, e], e_ss.at[b, e], e_rs.at[b, e])
        out = nn(ptg[b], recv_e[b].reshape(SLOTS, D))
        part_y[b] = out.astype(bf16).reshape(TZ, OWN, D)
        scatter_start(part_y.at[b], rs_y.at[b], *both(ry, b))

    def settle(b):
        own = pl.ds(pl.multiple_of(mz * OWN, OWN), OWN)
        total = scatter_sum(part_y.at[b], rs_y.at[b], *both(ry, b)) + hidden[b, own, :]
        gact[b, mz] = total.astype(bf16)
        gather_start(gact.at[b], *both(ay, b))

    load_in.wait()
    load_out.wait()

    @pl.when(first)
    def _():
        def part(b, e):
            expert_forward(b, e)
            return_rows(b, e)

        each_part(part)

    @pl.when(second)
    def _():
        def block(b, carry):
            each_expert(lambda e: expert_forward(b, e))
            each_expert(lambda e: expert_backward(b, e))
            return carry

        lax.fori_loop(0, 2, block, 0)
        each_part(return_rows)

    for b in range(2):
        save(b, 0, recv_b, xe_out)

    @pl.when(first)
    def _():
        combine(0)
        combine(1)
        for b in range(2):
            settle(b)
            hand(b, mz, hand_ss, hand_rs, gact, xin).start()
        for b in range(2):
            gather_recv(gact.at[b], *both(ay, b))
            for i in range(1, TZ):
                hand(b, lax.rem(mz + i, TZ), hand_ss, hand_rs, gact, xin).start()
        for b in range(2):
            hand_all(b, back_ss, back_rs, in_full, gin).wait_recv()
            dispatch_grad(b)
        each_part(expert_backward)

    for b in range(2):
        save(b, 1, recv_d, de_out)

    for b in range(2):
        pt0 = (slot_lane == slots[b, :, 0:1]).astype(f32).astype(bf16)
        pt1 = (slot_lane == slots[b, :, 1:2]).astype(f32).astype(bf16)
        for e in range(2):
            swap_recv(send_x.at[b, e], recv_x.at[b, e], x_ss.at[b, e], x_rs.at[b, e])
        if b == 1:
            @pl.when(first)
            def _():
                pl.semaphore_signal(
                    turn_sem, inc=1, device_id={"section": 1 - sec}, device_id_type=MESH
                )

        back = recv_x[b].reshape(SLOTS, WIDE)
        q0 = jnp.sum(nn(pt0, back[:, D:]), axis=1, keepdims=True)
        q1 = jnp.sum(nn(pt1, back[:, D:]), axis=1, keepdims=True)
        dc = gate[b, :, 1:2] * q0 - gate[b, :, 0:1] * q1
        dz = ((hits[b, 0] - hits[b, 1]) * dc).astype(bf16)
        db = nn(pt0 + pt1, back[:, 0:D]) + nn(dz, rpad[...])
        part_h[b] = db.astype(bf16).reshape(TZ, OWN, D)
        scatter_start(part_h.at[b], rs_h.at[b], *both(rh, b))
        unit = (lane == GAIN1).astype(f32).astype(bf16)
        small = tn(dz, normed2[b])
        small += tn(unit, (db * hidden[b] * hid_scale[b]).astype(bf16))
        if b == 0:
            small_acc[...] = small
        else:
            small_acc[...] += small

    for b in range(2):
        own = pl.ds(pl.multiple_of(mz * OWN, OWN), OWN)
        s_own = hid_scale[b, own, :]
        hat = hidden[b, own, :] * s_own
        lifted = scatter_sum(part_h.at[b], rs_h.at[b], *both(rh, b)) * gain1
        total = gin[b, mz].astype(f32) + s_own * (
            lifted - hat * jnp.mean(lifted * hat, axis=-1, keepdims=True)
        )
        dh_own[b] = total
        dh_full[b, mz] = total.astype(bf16)
        gather_start(dh_full.at[b], *both(ah, b))

    for b in range(2):
        rows = slice(b * BLOCK, (b + 1) * BLOCK)
        gather_recv(dh_full.at[b], *both(ah, b))
        dc = nt(dh_full[b].reshape(BLOCK, D), wall[mz]).astype(bf16)
        q = qkv[0, rows, :]
        k = qkv[1, rows, :]
        v = qkv[2, rows, :]
        dq = jnp.zeros((BLOCK, HF), f32)
        dk = jnp.zeros((BLOCK, HF), f32)
        dv = jnp.zeros((BLOCK, HF), f32)
        for h in range(HEADS):
            mine = head_of == h
            prob = probs[b * HEADS + h]
            dp = nt(jnp.where(mine, dc, jnp.zeros_like(dc)), v)
            ds = (prob * (dp - jnp.sum(prob * dp, axis=-1, keepdims=True))).astype(bf16)
            if b == 0:
                score_sum[h] = ds.astype(f32)
            else:
                score_sum[h] += ds.astype(f32)
            dq = jnp.where(mine, nn(ds, k), dq)
            dk = jnp.where(mine, tn(ds, q), dk)
            dv = jnp.where(mine, tn(prob.astype(bf16), dc), dv)
        dq_all[0, rows, :] = (dq * 0.125).astype(bf16)
        dq_all[1, rows, :] = (dk * 0.125).astype(bf16)
        dq_all[2, rows, :] = dv.astype(bf16)
        da = nn(dq_all[0, rows, :], w_qkv[0])
        da += nn(dq_all[1, rows, :], w_qkv[1])
        da += nn(dq_all[2, rows, :], w_qkv[2])
        part_a[b] = da.astype(bf16).reshape(TZ, OWN, D)
        scatter_start(part_a.at[b], rs_a.at[b], *both(ra, b))

    def dense_part():
        own_context = jnp.concatenate([call[0, mz], call[1, mz]], axis=0)
        for n in range(2):
            cols = slice(HALF * n, HALF * (n + 1))
            for j in range(3):
                out = tn(dq_all[j], normed[:, cols]).astype(bf16)
                dense_s[n, 4 * j : 4 * j + 4] = out.reshape(4, CUT, HALF)
            grad = dh_full[:, :, :, cols].reshape(ROWS, HALF)
            dense_s[n, 12:16] = tn(own_context, grad).astype(bf16).reshape(4, CUT, HALF)
            swap_start(dense_s.at[n], dense_r.at[n], *both(dn, n))
        small = small_acc[...]
        unit = (lane == GAIN0).astype(f32).astype(bf16)
        for b in range(2):
            x = xin[b].reshape(BLOCK, D).astype(f32)
            da = part_a[b].reshape(BLOCK, D).astype(f32)
            small += tn(unit, (da * x * rms_scale(x)).astype(bf16))
        bias_rows = []
        for h in range(HEADS):
            for n in range(len(EDGES)):
                hit = gap >= EDGES[n]
                if n + 1 < len(EDGES):
                    hit = hit & (gap < EDGES[n + 1])
                bias_rows.append(jnp.sum(jnp.where(hit, score_sum[h], 0.0), axis=0, keepdims=True))
        bias_col = jnp.sum(jnp.concatenate(bias_rows, axis=0), axis=1, keepdims=True)
        diagonal = iota((SMALL, 128), 0) == iota((SMALL, 128), 1)
        bias_row = jnp.sum(jnp.where(diagonal, bias_col, 0.0), axis=0, keepdims=True)
        mine = iota((SMALL, 128), 0) == BIAS + mz
        for j in range(PARTS):
            piece = small[:, 128 * j : 128 * (j + 1)]
            if j == 0:
                piece += jnp.where(mine, bias_row, 0.0)
            small_s[j] = piece.astype(bf16)

            @pl.when(me != j)
            def _():
                dp_copy(small_s.at[j], small_r.at[me], sm_ss.at[0], sm_rs.at[0], j).start()

    dense_part()

    for b in range(2):
        x_own = xin[b, mz].astype(f32)
        r_own = rms_scale(x_own)
        hat = x_own * r_own
        lifted = scatter_sum(part_a.at[b], rs_a.at[b], *both(ra, b)) * gain0
        total = dh_own[b] + r_own * (lifted - hat * jnp.mean(lifted * hat, axis=-1, keepdims=True))
        in_full[b, mz] = total.astype(bf16)
        gather_start(in_full.at[b], *both(aa, b))

        @pl.when(second)
        def _():
            hand(b, mz, back_ss, back_rs, in_full, gin).start()

    for b in range(2):
        gather_recv(in_full.at[b], *both(aa, b))

        @pl.when(second)
        def _():
            for i in range(1, TZ):
                hand(b, lax.rem(mz + i, TZ), back_ss, back_rs, in_full, gin).start()

    save_grad = pltpu.make_async_copy(in_full, grad_out, end_sem.at[1])
    save_grad.start()

    @pl.when(second)
    def _():
        for b in range(2):
            combine(b)
        for b in range(2):
            settle(b)
        for b in range(2):
            gather_recv(gact.at[b], *both(ay, b))

    save_act = pltpu.make_async_copy(gact, act_out, end_sem.at[0])
    save_act.start()

    holds = me < PARTS

    @pl.when(second)
    def _():
        pl.semaphore_wait(turn_sem, 1)

    for n in range(2):
        swap_recv(dense_s.at[n], dense_r.at[n], *both(dn, n))
        total = dense_r[n, 0].astype(f32)
        for p in range(1, DP):
            total += dense_r[n, p].astype(f32)
        dense_f[n, me] = total.astype(bf16)
        spread(dense_f.at[n], *both(df, n))

    @pl.when(holds)
    def _():
        small_r[me] = small_s[me]
        dp_round(small_r, sm_ss.at[0], sm_rs.at[0]).wait_recv()
        total = small_r[0].astype(f32)
        for p in range(1, DP):
            total += small_r[p].astype(f32)
        small_z[mz] = total.astype(bf16)
        gather_start(small_z, sz_ss.at[0], sz_rs.at[0])
        gather_recv(small_z, sz_ss.at[0], sz_rs.at[0])
        total = small_z[0].astype(f32)
        for t in range(1, TZ):
            total += small_z[t].astype(f32)
        small_f[me] = total.astype(bf16)
        spread(small_f, sf_ss.at[0], sf_rs.at[0])

    @pl.when(second)
    def _():
        gather_sent(wall, w_ss.at[0], w_rs.at[0])

    for b in range(2):
        for e in range(2):
            swap_sent(send_b.at[b, e], recv_b.at[b, e], b_ss.at[b, e], b_rs.at[b, e])
            swap_sent(send_e.at[b, e], recv_e.at[b, e], e_ss.at[b, e], e_rs.at[b, e])
            swap_sent(send_d.at[b, e], recv_d.at[b, e], d_ss.at[b, e], d_rs.at[b, e])
            swap_sent(send_x.at[b, e], recv_x.at[b, e], x_ss.at[b, e], x_rs.at[b, e])
        scatter_sent(part_y.at[b], rs_y.at[b], *both(ry, b))
        gather_sent(gact.at[b], *both(ay, b))
        scatter_sent(part_h.at[b], rs_h.at[b], *both(rh, b))
        gather_sent(dh_full.at[b], *both(ah, b))
        scatter_sent(part_a.at[b], rs_a.at[b], *both(ra, b))
        gather_sent(in_full.at[b], *both(aa, b))

        @pl.when(first)
        def _():
            scatter_sent(part_o.at[b], rs_o.at[b], *both(ro, b))
            gather_sent(o_full.at[b], *both(ao, b))
            hand_all(b, hand_ss, hand_rs, gact, xin).wait_send()

        @pl.when(second)
        def _():
            gather_sent(call.at[b], *both(c_sem, b))
            hand_all(b, back_ss, back_rs, in_full, gin).wait_send()

    for n in range(2):
        swap_sent(dense_s.at[n], dense_r.at[n], *both(dn, n))

    @pl.when(holds)
    def _():
        dp_round(small_s, sm_ss.at[0], sm_rs.at[0], PARTS - 1).wait_send()
        gather_sent(small_z, sz_ss.at[0], sz_rs.at[0])
        spread_sent(small_f, sf_ss.at[0], sf_rs.at[0])

    @pl.when(jnp.logical_not(holds))
    def _():
        dp_round(small_s, sm_ss.at[0], sm_rs.at[0], PARTS).wait_send()

    for copy in saved:
        copy.wait()
    for n in range(2):
        spread_recv(dense_f.at[n], *both(df, n))
        pltpu.make_async_copy(dense_f.at[n], dense_out.at[n], end_sem.at[2 + n]).start()

    @pl.when(holds)
    def _():
        dp_round(small_f, sf_ss.at[0], sf_rs.at[0], PARTS - 1).wait_recv()

    @pl.when(jnp.logical_not(holds))
    def _():
        dp_round(small_f, sf_ss.at[0], sf_rs.at[0], PARTS).wait_recv()

    for j in range(PARTS):
        small_out[:, 128 * j : 128 * (j + 1)] = small_f[j].astype(f32)
    held = small_f[0].astype(f32)
    mine = iota((SMALL, 128), 0) == BIAS + mz
    small_out[BIAS : BIAS + 1, 0:128] = jnp.sum(jnp.where(mine, held, 0.0), axis=0, keepdims=True)
    for n in range(2):
        spread_sent(dense_f.at[n], *both(df, n))
    save_act.wait()
    save_grad.wait()
    for n in range(2):
        pltpu.make_async_copy(dense_f.at[n], dense_out.at[n], end_sem.at[2 + n]).wait()


def last_outputs(
    xe, dpre, u, de, act, grads, dense, small,
    inner, outer, act_out, grads_out, qkv_out, attn_out, gain_out, router_out, bias_out,
    inner_v, outer_v, grads_f, dense_f, out_sem,
):
    sent = []

    def store(src, dst):
        copy = pltpu.make_async_copy(src, dst, out_sem.at[len(sent)])
        copy.start()
        sent.append(copy)

    store(act, act_out)
    grads_f[...] = grads[...].reshape(ROWS, D).astype(f32)
    store(grads_f, grads_out)
    for n in range(2):
        dense_f[:, HALF * n : HALF * (n + 1)] = dense[n].reshape(D, HALF).astype(f32)
    for j in range(3):
        store(dense_f.at[HF * j : HF * (j + 1)], qkv_out.at[j])
    store(dense_f.at[3 * HF : D], attn_out)
    for e in range(2):
        for one, two, total, out in ((xe, dpre, inner_v, inner), (u, de, outer_v, outer)):
            right = two[:, e].reshape(SLOTS, D)
            for i in range(3):
                cols = slice(256 * i, 256 * (i + 1))
                left = one[:, e, :, cols] if one is u else one[:, e, :, :, cols]
                total[e, cols, :] = tn(left.reshape(SLOTS, 256), right)
                store(total.at[e, cols], out.at[e, cols])
    router_out[...] = small[0:32, :]
    gain_out[...] = small[GAIN0 : GAIN1 + 1, :]
    for h in range(HEADS):
        bias_out[h] = small[BIAS : BIAS + 1, 16 * h : 16 * (h + 1)]
    for copy in sent:
        copy.wait()


def body(
    tokens, cotangent, norm_gains, w_qkv, w_attn_out, bias_table, router, w_in, w_out, routes, segments
):
    vmem = pl.BlockSpec(memory_space=pltpu.VMEM)
    hbm = pl.BlockSpec(memory_space=pl.ANY)
    dma = pltpu.SemaphoreType.DMA
    rows4 = pltpu.VMEM((2, TZ, OWN, D), bf16)
    messages = pltpu.VMEM((2, 2, DP, PAD, D), bf16)
    wide = pltpu.VMEM((2, 2, DP, PAD, WIDE), bf16)
    expert_rows = pltpu.VMEM((2, 2, ER, D), bf16)
    cuts = pltpu.VMEM((2, DP, CUT, HALF), bf16)
    pieces = pltpu.VMEM((DP, SMALL, 128), bf16)
    scratch = dict(
        xin=rows4,
        gin=rows4,
        w_qkv=pltpu.VMEM((3, HF, D), bf16),
        w_in=pltpu.VMEM((2, D, D), bf16),
        w_out=pltpu.VMEM((2, D, D), bf16),
        wall=pltpu.VMEM((TZ, HF, D), bf16),
        part_o=rows4, rs_o=rows4, o_full=rows4,
        call=pltpu.VMEM((2, TZ, BLOCK, HF), bf16),
        normed=pltpu.VMEM((ROWS, D), bf16),
        qkv=pltpu.VMEM((3, ROWS, HF), bf16),
        probs=pltpu.VMEM((2 * HEADS, BLOCK, BLOCK), f32),
        hidden=pltpu.VMEM((2, BLOCK, D), f32),
        hid_scale=pltpu.VMEM((2, BLOCK, 1), f32),
        normed2=pltpu.VMEM((2, BLOCK, D), bf16),
        rpad=pltpu.VMEM((SMALL, D), bf16),
        gate=pltpu.VMEM((2, BLOCK, 2), f32),
        slots=pltpu.VMEM((2, BLOCK, 2), jnp.int32),
        hits=pltpu.VMEM((2, 2, BLOCK, SMALL), f32),
        ptg=pltpu.VMEM((2, BLOCK, SLOTS), bf16),
        pick=pltpu.VMEM((2, SLOTS, BLOCK), bf16),
        pick_g=pltpu.VMEM((2, SLOTS, BLOCK), bf16),
        send_b=messages, recv_b=messages, send_e=messages, recv_e=messages,
        send_d=messages, recv_d=messages, send_x=wide, recv_x=wide,
        dact=expert_rows,
        part_y=rows4, rs_y=rows4, part_h=rows4, rs_h=rows4,
        dh_own=pltpu.VMEM((2, OWN, D), f32),
        dh_full=rows4, part_a=rows4, rs_a=rows4, in_full=rows4,
        dq_all=pltpu.VMEM((3, ROWS, HF), bf16),
        score_sum=pltpu.VMEM((HEADS, BLOCK, BLOCK), f32),
        gact=rows4,
        dense_s=cuts, dense_r=cuts, dense_f=cuts,
        small_acc=pltpu.VMEM((SMALL, D), f32),
        small_s=pieces, small_r=pieces,
        small_z=pltpu.VMEM((TZ, SMALL, 128), bf16),
        small_f=pieces,
        ld_sem=dma((5,)),
        out_sem=dma((2, 2)),
        end_sem=dma((4,)),
        w_ss=dma((1,)), w_rs=dma((1,)),
        c_ss=dma((2,)), c_rs=dma((2,)),
    )
    for name in ("b", "e", "d", "x"):
        scratch[name + "_ss"] = dma((2, 2))
        scratch[name + "_rs"] = dma((2, 2))
    for name in ("ro", "ao", "ry", "ay", "rh", "ah", "ra", "aa", "hand", "back", "dn", "df"):
        scratch[name + "_ss"] = dma((2,))
        scratch[name + "_rs"] = dma((2,))
    for name in ("sm", "sz", "sf"):
        scratch[name + "_ss"] = dma((1,))
        scratch[name + "_rs"] = dma((1,))
    scratch["turn_sem"] = pltpu.SemaphoreType.REGULAR

    shape = jax.ShapeDtypeStruct
    near = pltpu.VMEM
    act, grads, dense, small, xe, u, dpre, de = pl.pallas_call(
        kernel,
        out_shape=(
            near((2, TZ, OWN, D), bf16),
            near((2, TZ, OWN, D), bf16),
            near((2, DP, CUT, HALF), bf16),
            near((SMALL, D), f32),
            near((2, 2, DP, PAD, D), bf16),
            near((2, 2, ER, D), bf16),
            near((2, 2, ER, D), bf16),
            near((2, 2, DP, PAD, D), bf16),
        ),
        in_specs=[hbm, hbm, vmem, hbm, hbm, vmem, vmem, hbm, hbm, vmem, vmem],
        out_specs=(vmem,) * 8,
        scratch_shapes=list(scratch.values()),
        compiler_params=pltpu.CompilerParams(
            collective_id=0, has_side_effects=True, vmem_limit_bytes=55 * 1024 * 1024
        ),
        name="layers",
    )(
        tokens.reshape(2, TZ, OWN, D), cotangent.reshape(2, TZ, OWN, D), norm_gains,
        w_qkv[0].swapaxes(1, 2), w_attn_out[0], bias_table.swapaxes(1, 2),
        router.swapaxes(1, 2), w_in[0], w_out[0], routes.swapaxes(1, 2), segments,
    )

    inner, outer, act, grads, qkv_grad, attn_grad, gain_grad, router_grad, bias_grad = pl.pallas_call(
        last_outputs,
        out_shape=(
            shape((2, D, D), f32),
            shape((2, D, D), f32),
            shape((2, TZ, OWN, D), bf16),
            shape((ROWS, D), f32),
            shape((3, HF, D), f32),
            shape((HF, D), f32),
            shape((2, D), f32),
            shape((32, D), f32),
            shape((HEADS, 1, 16), f32),
        ),
        in_specs=[vmem] * 8,
        out_specs=(hbm,) * 6 + (vmem,) * 3,
        scratch_shapes=[
            pltpu.VMEM((2, D, D), f32),
            pltpu.VMEM((2, D, D), f32),
            pltpu.VMEM((ROWS, D), f32),
            pltpu.VMEM((D, D), f32),
            dma((18,)),
        ],
        compiler_params=pltpu.CompilerParams(vmem_limit_bytes=20 * 1024 * 1024),
        name="last_outputs",
    )(xe, dpre, u, de, act, grads, dense, small)

    return (
        act.reshape(ROWS, D)[None],
        grads[None],
        gain_grad[None],
        qkv_grad.swapaxes(1, 2)[None],
        attn_grad[None],
        bias_grad.transpose(1, 2, 0),
        router_grad.T[None],
        inner[None],
        outer[None],
    )


def solution(mesh):
    in_specs = (
        P("dp", None),
        P("dp", None),
        P("section", None, None),
        P("section", None, None, "tensor"),
        P("section", "tensor", None),
        P("section", None, "tensor"),
        P("section", None, None),
        P("section", "dp", None, "tensor"),
        P("section", "dp", "tensor", None),
        P("section", "dp", None),
        P("dp", None),
    )
    out_specs = (
        P("section", "dp", None),
        P("section", "dp", None),
        P("section", None, None),
        P("section", None, None, "tensor"),
        P("section", "tensor", None),
        P("section", None, "tensor"),
        P("section", None, None),
        P("section", "dp", None, "tensor"),
        P("section", "dp", "tensor", None),
    )
    return jax.shard_map(body, mesh=mesh, in_specs=in_specs, out_specs=out_specs, check_vma=False)
```

```python
import jax
import jax.numpy as jnp
from jax import lax
from jax.experimental import pallas as pl
from jax.experimental.pallas import tpu as pltpu
from jax.sharding import PartitionSpec as P

epsilon = 1e-06
masked_score = -1000000000.0
bucket_edges = (1, 2, 3, 4, 5, 6, 7, 8, 10, 13, 16, 20, 25, 32, 40)
MESH = pl.DeviceIdType.MESH
f32 = jnp.float32
bf16 = jnp.bfloat16

DP = 16
TZ = 4
ROWS = 256
BLOCK = 128
OWN = BLOCK // TZ
D = 768
HF = 192
HEADS = 3
PAD = 16
ER = DP * PAD
SLOTS = 2 * ER
GATE_ROW = 12
CUT = D // DP
SMALL = 48
GAIN0, GAIN1, BIAS = 32, 33, 34
HALF = D // 2
PARTS = D // 128
EDGES = (0,) + bucket_edges
FAR_FIRST = (2, 1, 3)


def nn(a, b):
    return lax.dot_general(a, b, (((1,), (0,)), ((), ())), preferred_element_type=f32)


def nt(a, b):
    return lax.dot_general(a, b, (((1,), (1,)), ((), ())), preferred_element_type=f32)


def tn(a, b):
    return lax.dot_general(a, b, (((0,), (0,)), ((), ())), preferred_element_type=f32)


def iota(shape, dim):
    return lax.broadcasted_iota(jnp.int32, shape, dim)


def rms_scale(values):
    return lax.rsqrt(jnp.mean(values * values, axis=-1, keepdims=True) + epsilon)


def kernel(
    tokens, cotangent, gains, w_qkv_hbm, w_att, bias_tab, router, w_in_hbm, w_out_hbm, routes, segments,
    act_out, grad_out, dense_out, small_out, xe_out, act, dpre, de_out,
    xin, gin, w_qkv, w_in, w_out, wall, part_o, rs_o, o_full, call, normed, qkv, probs, hidden, hid_scale, normed2, rpad,
    gate, slots, hits, ptg, pick, pick_g, send_b, recv_b, send_e, recv_e, send_d, recv_d, send_x,
    recv_x, dact, part_y, rs_y, part_h, rs_h, dh_own, dh_full, part_a, rs_a, in_full,
    dq_all, score_sum, gact, dense_s, dense_r, dense_f, small_acc, small_s, small_r, small_z, small_f,
    ld_sem, out_sem, end_sem, w_ss, w_rs, c_ss, c_rs, b_ss, b_rs, e_ss, e_rs, d_ss, d_rs, x_ss, x_rs,
    ro_ss, ro_rs, ao_ss, ao_rs, ry_ss, ry_rs, ay_ss, ay_rs, rh_ss, rh_rs, ah_ss, ah_rs, ra_ss, ra_rs, aa_ss, aa_rs,
    hand_ss, hand_rs, back_ss, back_rs, dn_ss, dn_rs, df_ss, df_rs, sm_ss, sm_rs, sz_ss, sz_rs,
    sf_ss, sf_rs, turn_sem,
):
    sec = lax.axis_index("section")
    me = lax.axis_index("dp")
    mz = lax.axis_index("tensor")
    first = sec == 0
    second = sec == 1

    load_in = pltpu.make_async_copy(w_in_hbm, w_in, ld_sem.at[0])
    load_out = pltpu.make_async_copy(w_out_hbm, w_out, ld_sem.at[1])
    load_qkv = pltpu.make_async_copy(w_qkv_hbm, w_qkv, ld_sem.at[2])
    load_att = pltpu.make_async_copy(w_att, wall.at[mz], ld_sem.at[3])
    load_x = pltpu.make_async_copy(tokens, xin, ld_sem.at[4])
    load_g = pltpu.make_async_copy(cotangent, gin, ld_sem.at[4])

    @pl.when(first)
    def _():
        load_x.start()

    @pl.when(second)
    def _():
        load_g.start()

    load_qkv.start()
    load_att.start()

    barrier = pltpu.get_barrier_semaphore()

    def greet(i, carry):
        pl.semaphore_signal(
            barrier, inc=1, device_id={"dp": lax.rem(me + i, DP)}, device_id_type=MESH
        )
        return carry

    lax.fori_loop(1, DP, greet, 0)
    for i in range(1, TZ):
        pl.semaphore_signal(
            barrier, inc=1, device_id={"tensor": lax.rem(mz + i, TZ)}, device_id_type=MESH
        )
    pl.semaphore_signal(barrier, inc=1, device_id={"section": 1 - sec}, device_id_type=MESH)

    def z_copy(src, dst, ss, rs, peer):
        return pltpu.make_async_remote_copy(
            src_ref=src, dst_ref=dst, send_sem=ss, recv_sem=rs,
            device_id={"tensor": peer}, device_id_type=MESH,
        )

    def z_round(buf, ss, rs):
        part = buf.at[pl.ds(0, TZ - 1)]
        return z_copy(part, part, ss, rs, lax.rem(mz + 1, TZ))

    def gather_start(buf, ss, rs):
        for i in FAR_FIRST:
            z_copy(buf.at[mz], buf.at[mz], ss, rs, lax.rem(mz + i, TZ)).start()

    def gather_recv(buf, ss, rs):
        z_round(buf, ss, rs).wait_recv()

    def gather_sent(buf, ss, rs):
        z_round(buf, ss, rs).wait_send()

    def scatter_start(part, rcv, ss, rs):
        for i in FAR_FIRST:
            peer = lax.rem(mz + i, TZ)
            z_copy(part.at[peer], rcv.at[mz], ss, rs, peer).start()

    def scatter_sum(part, rcv, ss, rs):
        z_round(rcv, ss, rs).wait_recv()
        total = part[mz].astype(f32)
        for i in range(1, TZ):
            total += rcv[lax.rem(mz + i, TZ)].astype(f32)
        return total

    def scatter_sent(part, rcv, ss, rs):
        z_round(part, ss, rs).wait_send()

    def dp_copy(src, dst, ss, rs, peer):
        return pltpu.make_async_remote_copy(
            src_ref=src, dst_ref=dst, send_sem=ss, recv_sem=rs,
            device_id={"dp": peer}, device_id_type=MESH,
        )

    def dp_round(buf, ss, rs, count=DP - 1):
        part = buf.at[pl.ds(0, count)]
        return dp_copy(part, part, ss, rs, lax.rem(me + 1, DP))

    me_x, me_y = me // 4, me % 4

    def away(i):
        return 2 + ((i + 1) // 2) * (1 - 2 * (i % 2))

    def others(step):
        def one(i, carry):
            step(((me_x + away(i // 4)) % 4) * 4 + (me_y + away(i % 4)) % 4)
            return carry

        lax.fori_loop(0, DP - 1, one, 0)

    def swap_start(snd, rcv, ss, rs):
        others(lambda peer: dp_copy(snd.at[peer], rcv.at[me], ss, rs, peer).start())
        rcv[me] = snd[me]

    def swap_recv(snd, rcv, ss, rs):
        dp_round(rcv, ss, rs).wait_recv()

    def swap_sent(snd, rcv, ss, rs):
        dp_round(snd, ss, rs).wait_send()

    def spread(buf, ss, rs):
        others(lambda peer: dp_copy(buf.at[me], buf.at[me], ss, rs, peer).start())

    def spread_recv(buf, ss, rs):
        dp_round(buf, ss, rs).wait_recv()

    def spread_sent(buf, ss, rs):
        dp_round(buf, ss, rs).wait_send()

    def hand(b, t, ss, rs, src, dst):
        return pltpu.make_async_remote_copy(
            src_ref=src.at[b, t], dst_ref=dst.at[b, t], send_sem=ss.at[b],
            recv_sem=rs.at[b], device_id={"section": 1 - sec}, device_id_type=MESH,
        )

    def hand_all(b, ss, rs, src, dst):
        return pltpu.make_async_remote_copy(
            src_ref=src.at[b], dst_ref=dst.at[b], send_sem=ss.at[b],
            recv_sem=rs.at[b], device_id={"section": 1 - sec}, device_id_type=MESH,
        )

    def both(sems, b):
        return sems[0].at[b], sems[1].at[b]

    c_sem, b_sem, d_sem = (c_ss, c_rs), (b_ss, b_rs), (d_ss, d_rs)
    ro, ao = (ro_ss, ro_rs), (ao_ss, ao_rs)
    ry, ay, rh = (ry_ss, ry_rs), (ay_ss, ay_rs), (rh_ss, rh_rs)
    ah, ra, aa = (ah_ss, ah_rs), (ra_ss, ra_rs), (aa_ss, aa_rs)
    dn, df = (dn_ss, dn_rs), (df_ss, df_rs)

    row = iota((BLOCK, BLOCK), 0)
    col = iota((BLOCK, BLOCK), 1)
    eye = row == col
    earlier = (row > col).astype(f32).astype(bf16)
    every = jnp.ones((BLOCK, BLOCK), bf16)
    lane = iota((BLOCK, SMALL), 1)
    slot_lane = iota((BLOCK, SLOTS), 1)
    slot_sub = iota((SLOTS, BLOCK), 0)

    def to_col(values):
        return jnp.sum(jnp.where(eye, values, 0.0), axis=1, keepdims=True)

    def to_row(values):
        return jnp.sum(jnp.where(eye, values, 0.0), axis=0, keepdims=True)

    rpad[...] = jnp.zeros((SMALL, D), bf16)
    rpad[0:32, :] = router[0]
    for b in range(2):
        named = routes[0, :, b * BLOCK : (b + 1) * BLOCK].astype(f32)
        e0 = to_col(named[0:1, :]).astype(jnp.int32)
        e1 = to_col(named[1:2, :]).astype(jnp.int32)
        hit0 = (lane == e0).astype(f32)
        hit1 = (lane == e1).astype(f32)
        rank0 = jnp.sum(nn(earlier, hit0.astype(bf16)) * hit0, axis=1, keepdims=True)
        rank1 = jnp.sum(
            (nn(earlier, hit1.astype(bf16)) + nn(every, hit0.astype(bf16))) * hit1,
            axis=1, keepdims=True,
        )
        slot0 = (e0 % 2) * ER + (e0 // 2) * PAD + rank0.astype(jnp.int32)
        slot1 = (e1 % 2) * ER + (e1 // 2) * PAD + rank1.astype(jnp.int32)
        slots[b, :, 0:1] = slot0
        slots[b, :, 1:2] = slot1
        hits[b, 0] = hit0
        hits[b, 1] = hit1
        row0 = to_row(slot0.astype(f32)).astype(jnp.int32)
        row1 = to_row(slot1.astype(f32)).astype(jnp.int32)
        pick[b] = ((slot_sub == row0) | (slot_sub == row1)).astype(f32).astype(bf16)

    gain0 = gains[0, 0:1, :].astype(f32)
    gain1 = gains[0, 1:2, :].astype(f32)
    gap = row - col
    head_of = iota((BLOCK, HF), 1) // (HF // HEADS)

    @pl.when(first)
    def _():
        load_x.wait()

    @pl.when(second)
    def _():
        load_g.wait()

    load_qkv.wait()
    load_att.wait()
    load_in.start()
    load_out.start()

    @pl.when(second)
    def _():
        pl.semaphore_wait(barrier, DP + TZ - 1)
        pl.semaphore_wait(turn_sem, 1)
        gather_start(wall, w_ss.at[0], w_rs.at[0])

    for b in range(2):
        rows = slice(b * BLOCK, (b + 1) * BLOCK)

        @pl.when(second)
        def _():
            hand_all(b, hand_ss, hand_rs, gact, xin).wait_recv()

        x = xin[b].reshape(BLOCK, D).astype(f32)
        normed[rows, :] = (x * rms_scale(x) * gain0).astype(bf16)
        for j in range(3):
            qkv[j, rows, :] = nt(normed[rows, :], w_qkv[j]).astype(bf16)
        seg_row = segments[b : b + 1, :].astype(f32)
        allowed = (gap >= 0) & (seg_row == to_col(seg_row))
        q = qkv[0, rows, :]
        k = qkv[1, rows, :]
        v = qkv[2, rows, :]
        context = jnp.zeros((BLOCK, HF), f32)
        for h in range(HEADS):
            bias = jnp.broadcast_to(bias_tab[0, h : h + 1, 0:1].astype(f32), (BLOCK, BLOCK))
            for n, edge in enumerate(bucket_edges):
                bias = jnp.where(
                    gap >= edge, bias_tab[0, h : h + 1, n + 1 : n + 2].astype(f32), bias
                )
            score = nt(jnp.where(head_of == h, q, jnp.zeros_like(q)), k) * 0.125 + bias
            score = jnp.where(allowed, score, masked_score)
            score = jnp.exp(score - jnp.max(score, axis=-1, keepdims=True))
            prob = score / jnp.sum(score, axis=-1, keepdims=True)
            probs[b * HEADS + h] = prob
            context = jnp.where(head_of == h, nn(prob.astype(bf16), v), context)
        call[b, mz] = context.astype(bf16)

        @pl.when(first)
        def _():
            if b == 0:
                pl.semaphore_wait(barrier, DP + TZ - 1)
            part_o[b] = nn(call[b, mz], wall[mz]).astype(bf16).reshape(TZ, OWN, D)
            scatter_start(part_o.at[b], rs_o.at[b], *both(ro, b))

        @pl.when(second)
        def _():
            gather_start(call.at[b], *both(c_sem, b))

    def dispatch(chosen, values, snd, rcv, sems, b):
        for e in range(2):
            out = nn(chosen[b, ER * e : ER * (e + 1), :], values).astype(bf16)
            snd[b, e] = out.reshape(DP, PAD, D)
            swap_start(snd.at[b, e], rcv.at[b, e], sems[0].at[b, e], sems[1].at[b, e])

    def dispatch_grad(b):
        dispatch(pick_g, gin[b].reshape(BLOCK, D), send_d, recv_d, d_sem, b)

    @pl.when(first)
    def _():
        for b in range(2):
            o_full[b, mz] = scatter_sum(part_o.at[b], rs_o.at[b], *both(ro, b)).astype(bf16)
            gather_start(o_full.at[b], *both(ao, b))

    for b in range(2):
        @pl.when(first)
        def _():
            gather_recv(o_full.at[b], *both(ao, b))
            if b == 1:
                pl.semaphore_signal(
                    turn_sem, inc=1, device_id={"section": 1 - sec}, device_id_type=MESH
                )
            hidden[b] = xin[b].reshape(BLOCK, D).astype(f32) + o_full[b].reshape(BLOCK, D).astype(f32)

        @pl.when(second)
        def _():
            gather_recv(call.at[b], *both(c_sem, b))
            if b == 0:
                gather_recv(wall, w_ss.at[0], w_rs.at[0])
            total = xin[b].reshape(BLOCK, D).astype(f32)
            for t in range(TZ):
                total += nn(call[b, t], wall[t])
            hidden[b] = total

        h = hidden[b]
        scale = rms_scale(h)
        hid_scale[b] = scale
        normed2[b] = (h * scale * gain1).astype(bf16)
        dispatch(pick, normed2[b], send_b, recv_b, b_sem, b)

        z = nt(normed2[b], rpad[...])
        z0 = jnp.sum(z * hits[b, 0], axis=1, keepdims=True)
        z1 = jnp.sum(z * hits[b, 1], axis=1, keepdims=True)
        g0 = 1.0 / (1.0 + jnp.exp(z1 - z0))
        g1 = 1.0 / (1.0 + jnp.exp(z0 - z1))
        gate[b, :, 0:1] = g0
        gate[b, :, 1:2] = g1
        slot0 = slots[b, :, 0:1]
        slot1 = slots[b, :, 1:2]
        row0 = to_row(slot0.astype(f32)).astype(jnp.int32)
        row1 = to_row(slot1.astype(f32)).astype(jnp.int32)
        pick_g[b] = (
            jnp.where(slot_sub == row0, to_row(g0), 0.0)
            + jnp.where(slot_sub == row1, to_row(g1), 0.0)
        ).astype(bf16)

        @pl.when(second)
        def _():
            dispatch_grad(b)

        ptg[b] = (
            jnp.where(slot_lane == slot0, g0, 0.0) + jnp.where(slot_lane == slot1, g1, 0.0)
        ).astype(bf16)

    root = 0.7978845608028654
    saved = []

    def save(b, n, src, dst):
        copy = pltpu.make_async_copy(src.at[b], dst.at[b], out_sem.at[b, n])
        copy.start()
        saved.append(copy)

    def expert_forward(b, e):
        swap_recv(send_b.at[b, e], recv_b.at[b, e], b_ss.at[b, e], b_rs.at[b, e])
        x = recv_b[b, e].reshape(ER, D)
        for n in range(3):
            cols = slice(256 * n, 256 * (n + 1))
            pre = nn(x, w_in[e, :, cols])
            square = pre * pre
            wave = jnp.tanh(root * pre * (1.0 + 0.044715 * square))
            lift = 0.5 * (1.0 + wave)
            act[b, e, :, cols] = (pre * lift).astype(bf16)
            slope = lift + 0.5 * root * pre * (1.0 - wave * wave) * (1.0 + 0.134145 * square)
            dact[b, e, :, cols] = slope.astype(bf16)
        out = nn(act[b, e], w_out[e])
        send_e[b, e] = out.astype(bf16).reshape(DP, PAD, D)

    def return_rows(b, e):
        swap_start(send_e.at[b, e], recv_e.at[b, e], e_ss.at[b, e], e_rs.at[b, e])

    def expert_backward(b, e):
        swap_recv(send_d.at[b, e], recv_d.at[b, e], d_ss.at[b, e], d_rs.at[b, e])
        de = recv_d[b, e].reshape(ER, D)
        for n in range(3):
            cols = slice(256 * n, 256 * (n + 1))
            grad = nt(de, w_out[e, cols, :])
            dpre[b, e, :, cols] = (grad * dact[b, e, :, cols].astype(f32)).astype(bf16)
        out = nt(dpre[b, e], w_in[e])
        send_x[b, e] = out.astype(bf16).reshape(DP, PAD, D)
        rows = send_e[b, e].reshape(ER, D).astype(f32)
        weight = jnp.sum(rows * de.astype(f32), axis=1, keepdims=True)
        slot = iota((ER, 128), 0) % PAD
        spread_out = jnp.where(iota((ER, 128), 1) == slot, weight, 0.0).reshape(DP, PAD, 128)
        line = jnp.sum(spread_out, axis=1, keepdims=True)
        coarse = line.astype(bf16).astype(f32)
        place = iota((DP, PAD, 128), 1)
        extra = jnp.where(place == GATE_ROW, coarse, 0.0)
        extra += jnp.where(place == GATE_ROW + 1, line - coarse, 0.0)
        near = out[:, 0:128].reshape(DP, PAD, 128) + extra
        send_x[b, e, :, :, 0:128] = near.astype(bf16)
        swap_start(send_x.at[b, e], recv_x.at[b, e], x_ss.at[b, e], x_rs.at[b, e])

    def each_expert(step):
        def one(e, carry):
            step(e)
            return carry

        lax.fori_loop(0, 2, one, 0)

    def each_part(step):
        def one(i, carry):
            step(i // 2, i % 2)
            return carry

        lax.fori_loop(0, 4, one, 0)

    def combine(b):
        for e in range(2):
            swap_recv(send_e.at[b, e], recv_e.at[b, e], e_ss.at[b, e], e_rs.at[b, e])
        out = nn(ptg[b], recv_e[b].reshape(SLOTS, D))
        part_y[b] = out.astype(bf16).reshape(TZ, OWN, D)
        scatter_start(part_y.at[b], rs_y.at[b], *both(ry, b))

    def settle(b):
        own = pl.ds(pl.multiple_of(mz * OWN, OWN), OWN)
        total = scatter_sum(part_y.at[b], rs_y.at[b], *both(ry, b)) + hidden[b, own, :]
        gact[b, mz] = total.astype(bf16)
        gather_start(gact.at[b], *both(ay, b))

    load_in.wait()
    load_out.wait()

    @pl.when(first)
    def _():
        def part(b, e):
            expert_forward(b, e)
            return_rows(b, e)

        each_part(part)

    @pl.when(second)
    def _():
        def block(b, carry):
            each_expert(lambda e: expert_forward(b, e))
            each_expert(lambda e: expert_backward(b, e))
            return carry

        lax.fori_loop(0, 2, block, 0)
        each_part(return_rows)

    for b in range(2):
        save(b, 0, recv_b, xe_out)

    @pl.when(first)
    def _():
        combine(0)
        combine(1)
        for b in range(2):
            settle(b)
            hand(b, mz, hand_ss, hand_rs, gact, xin).start()
        for b in range(2):
            gather_recv(gact.at[b], *both(ay, b))
            for i in range(1, TZ):
                hand(b, lax.rem(mz + i, TZ), hand_ss, hand_rs, gact, xin).start()
        for b in range(2):
            hand_all(b, back_ss, back_rs, in_full, gin).wait_recv()
            dispatch_grad(b)
        each_part(expert_backward)

    for b in range(2):
        save(b, 1, recv_d, de_out)

    for b in range(2):
        pt0 = (slot_lane == slots[b, :, 0:1]).astype(f32).astype(bf16)
        pt1 = (slot_lane == slots[b, :, 1:2]).astype(f32).astype(bf16)
        for e in range(2):
            swap_recv(send_x.at[b, e], recv_x.at[b, e], x_ss.at[b, e], x_rs.at[b, e])
        if b == 1:
            @pl.when(first)
            def _():
                pl.semaphore_signal(
                    turn_sem, inc=1, device_id={"section": 1 - sec}, device_id_type=MESH
                )

        back = recv_x[b].reshape(SLOTS, D)

        def gate_product(slot):
            line = slot - slot % PAD + GATE_ROW
            both_rows = ((slot_lane == line) | (slot_lane == line + 1)).astype(f32).astype(bf16)
            found = nn(both_rows, back[:, 0:128])
            mine = iota((BLOCK, 128), 1) == slot % PAD
            return jnp.sum(jnp.where(mine, found, 0.0), axis=1, keepdims=True)

        q0 = gate_product(slots[b, :, 0:1])
        q1 = gate_product(slots[b, :, 1:2])
        dc = gate[b, :, 1:2] * q0 - gate[b, :, 0:1] * q1
        dz = ((hits[b, 0] - hits[b, 1]) * dc).astype(bf16)
        db = nn(pt0 + pt1, back) + nn(dz, rpad[...])
        part_h[b] = db.astype(bf16).reshape(TZ, OWN, D)
        scatter_start(part_h.at[b], rs_h.at[b], *both(rh, b))
        unit = (lane == GAIN1).astype(f32).astype(bf16)
        small = tn(dz, normed2[b])
        small += tn(unit, (db * hidden[b] * hid_scale[b]).astype(bf16))
        if b == 0:
            small_acc[...] = small
        else:
            small_acc[...] += small

    for b in range(2):
        own = pl.ds(pl.multiple_of(mz * OWN, OWN), OWN)
        s_own = hid_scale[b, own, :]
        hat = hidden[b, own, :] * s_own
        lifted = scatter_sum(part_h.at[b], rs_h.at[b], *both(rh, b)) * gain1
        total = gin[b, mz].astype(f32) + s_own * (
            lifted - hat * jnp.mean(lifted * hat, axis=-1, keepdims=True)
        )
        dh_own[b] = total
        dh_full[b, mz] = total.astype(bf16)
        gather_start(dh_full.at[b], *both(ah, b))

    for b in range(2):
        rows = slice(b * BLOCK, (b + 1) * BLOCK)
        gather_recv(dh_full.at[b], *both(ah, b))
        dc = nt(dh_full[b].reshape(BLOCK, D), wall[mz]).astype(bf16)
        q = qkv[0, rows, :]
        k = qkv[1, rows, :]
        v = qkv[2, rows, :]
        dq = jnp.zeros((BLOCK, HF), f32)
        dk = jnp.zeros((BLOCK, HF), f32)
        dv = jnp.zeros((BLOCK, HF), f32)
        for h in range(HEADS):
            mine = head_of == h
            prob = probs[b * HEADS + h]
            dp = nt(jnp.where(mine, dc, jnp.zeros_like(dc)), v)
            ds = (prob * (dp - jnp.sum(prob * dp, axis=-1, keepdims=True))).astype(bf16)
            if b == 0:
                score_sum[h] = ds.astype(f32)
            else:
                score_sum[h] += ds.astype(f32)
            dq = jnp.where(mine, nn(ds, k), dq)
            dk = jnp.where(mine, tn(ds, q), dk)
            dv = jnp.where(mine, tn(prob.astype(bf16), dc), dv)
        dq_all[0, rows, :] = (dq * 0.125).astype(bf16)
        dq_all[1, rows, :] = (dk * 0.125).astype(bf16)
        dq_all[2, rows, :] = dv.astype(bf16)
        da = nn(dq_all[0, rows, :], w_qkv[0])
        da += nn(dq_all[1, rows, :], w_qkv[1])
        da += nn(dq_all[2, rows, :], w_qkv[2])
        part_a[b] = da.astype(bf16).reshape(TZ, OWN, D)
        scatter_start(part_a.at[b], rs_a.at[b], *both(ra, b))

    def dense_part():
        own_context = jnp.concatenate([call[0, mz], call[1, mz]], axis=0)
        for n in range(2):
            cols = slice(HALF * n, HALF * (n + 1))
            for j in range(3):
                out = tn(dq_all[j], normed[:, cols]).astype(bf16)
                dense_s[n, 4 * j : 4 * j + 4] = out.reshape(4, CUT, HALF)
            grad = dh_full[:, :, :, cols].reshape(ROWS, HALF)
            dense_s[n, 12:16] = tn(own_context, grad).astype(bf16).reshape(4, CUT, HALF)
            swap_start(dense_s.at[n], dense_r.at[n], *both(dn, n))
        small = small_acc[...]
        unit = (lane == GAIN0).astype(f32).astype(bf16)
        for b in range(2):
            x = xin[b].reshape(BLOCK, D).astype(f32)
            da = part_a[b].reshape(BLOCK, D).astype(f32)
            small += tn(unit, (da * x * rms_scale(x)).astype(bf16))
        bias_rows = []
        for h in range(HEADS):
            for n in range(len(EDGES)):
                hit = gap >= EDGES[n]
                if n + 1 < len(EDGES):
                    hit = hit & (gap < EDGES[n + 1])
                bias_rows.append(jnp.sum(jnp.where(hit, score_sum[h], 0.0), axis=0, keepdims=True))
        bias_col = jnp.sum(jnp.concatenate(bias_rows, axis=0), axis=1, keepdims=True)
        diagonal = iota((SMALL, 128), 0) == iota((SMALL, 128), 1)
        bias_row = jnp.sum(jnp.where(diagonal, bias_col, 0.0), axis=0, keepdims=True)
        mine = iota((SMALL, 128), 0) == BIAS + mz
        for j in range(PARTS):
            piece = small[:, 128 * j : 128 * (j + 1)]
            if j == 0:
                piece += jnp.where(mine, bias_row, 0.0)
            small_s[j] = piece.astype(bf16)

            @pl.when(me != j)
            def _():
                dp_copy(small_s.at[j], small_r.at[me], sm_ss.at[0], sm_rs.at[0], j).start()

    dense_part()

    for b in range(2):
        x_own = xin[b, mz].astype(f32)
        r_own = rms_scale(x_own)
        hat = x_own * r_own
        lifted = scatter_sum(part_a.at[b], rs_a.at[b], *both(ra, b)) * gain0
        total = dh_own[b] + r_own * (lifted - hat * jnp.mean(lifted * hat, axis=-1, keepdims=True))
        in_full[b, mz] = total.astype(bf16)
        gather_start(in_full.at[b], *both(aa, b))

        @pl.when(second)
        def _():
            hand(b, mz, back_ss, back_rs, in_full, gin).start()

    for b in range(2):
        gather_recv(in_full.at[b], *both(aa, b))

        @pl.when(second)
        def _():
            for i in range(1, TZ):
                hand(b, lax.rem(mz + i, TZ), back_ss, back_rs, in_full, gin).start()

    save_grad = pltpu.make_async_copy(in_full, grad_out, end_sem.at[1])
    save_grad.start()

    @pl.when(second)
    def _():
        for b in range(2):
            combine(b)
        for b in range(2):
            settle(b)
        for b in range(2):
            gather_recv(gact.at[b], *both(ay, b))

    save_act = pltpu.make_async_copy(gact, act_out, end_sem.at[0])
    save_act.start()

    holds = me < PARTS

    @pl.when(second)
    def _():
        pl.semaphore_wait(turn_sem, 1)

    for n in range(2):
        swap_recv(dense_s.at[n], dense_r.at[n], *both(dn, n))
        total = dense_r[n, 0].astype(f32)
        for p in range(1, DP):
            total += dense_r[n, p].astype(f32)
        dense_f[n, me] = total.astype(bf16)
        spread(dense_f.at[n], *both(df, n))

    @pl.when(holds)
    def _():
        small_r[me] = small_s[me]
        dp_round(small_r, sm_ss.at[0], sm_rs.at[0]).wait_recv()
        total = small_r[0].astype(f32)
        for p in range(1, DP):
            total += small_r[p].astype(f32)
        small_z[mz] = total.astype(bf16)
        gather_start(small_z, sz_ss.at[0], sz_rs.at[0])
        gather_recv(small_z, sz_ss.at[0], sz_rs.at[0])
        total = small_z[0].astype(f32)
        for t in range(1, TZ):
            total += small_z[t].astype(f32)
        small_f[me] = total.astype(bf16)
        spread(small_f, sf_ss.at[0], sf_rs.at[0])

    @pl.when(second)
    def _():
        gather_sent(wall, w_ss.at[0], w_rs.at[0])

    for b in range(2):
        for e in range(2):
            swap_sent(send_b.at[b, e], recv_b.at[b, e], b_ss.at[b, e], b_rs.at[b, e])
            swap_sent(send_e.at[b, e], recv_e.at[b, e], e_ss.at[b, e], e_rs.at[b, e])
            swap_sent(send_d.at[b, e], recv_d.at[b, e], d_ss.at[b, e], d_rs.at[b, e])
            swap_sent(send_x.at[b, e], recv_x.at[b, e], x_ss.at[b, e], x_rs.at[b, e])
        scatter_sent(part_y.at[b], rs_y.at[b], *both(ry, b))
        gather_sent(gact.at[b], *both(ay, b))
        scatter_sent(part_h.at[b], rs_h.at[b], *both(rh, b))
        gather_sent(dh_full.at[b], *both(ah, b))
        scatter_sent(part_a.at[b], rs_a.at[b], *both(ra, b))
        gather_sent(in_full.at[b], *both(aa, b))

        @pl.when(first)
        def _():
            scatter_sent(part_o.at[b], rs_o.at[b], *both(ro, b))
            gather_sent(o_full.at[b], *both(ao, b))
            hand_all(b, hand_ss, hand_rs, gact, xin).wait_send()

        @pl.when(second)
        def _():
            gather_sent(call.at[b], *both(c_sem, b))
            hand_all(b, back_ss, back_rs, in_full, gin).wait_send()

    for n in range(2):
        swap_sent(dense_s.at[n], dense_r.at[n], *both(dn, n))

    @pl.when(holds)
    def _():
        dp_round(small_s, sm_ss.at[0], sm_rs.at[0], PARTS - 1).wait_send()
        gather_sent(small_z, sz_ss.at[0], sz_rs.at[0])
        spread_sent(small_f, sf_ss.at[0], sf_rs.at[0])

    @pl.when(jnp.logical_not(holds))
    def _():
        dp_round(small_s, sm_ss.at[0], sm_rs.at[0], PARTS).wait_send()

    for copy in saved:
        copy.wait()
    for n in range(2):
        spread_recv(dense_f.at[n], *both(df, n))
        pltpu.make_async_copy(dense_f.at[n], dense_out.at[n], end_sem.at[2 + n]).start()

    @pl.when(holds)
    def _():
        dp_round(small_f, sf_ss.at[0], sf_rs.at[0], PARTS - 1).wait_recv()

    @pl.when(jnp.logical_not(holds))
    def _():
        dp_round(small_f, sf_ss.at[0], sf_rs.at[0], PARTS).wait_recv()

    for j in range(PARTS):
        small_out[:, 128 * j : 128 * (j + 1)] = small_f[j].astype(f32)
    held = small_f[0].astype(f32)
    mine = iota((SMALL, 128), 0) == BIAS + mz
    small_out[BIAS : BIAS + 1, 0:128] = jnp.sum(jnp.where(mine, held, 0.0), axis=0, keepdims=True)
    for n in range(2):
        spread_sent(dense_f.at[n], *both(df, n))
    save_act.wait()
    save_grad.wait()
    for n in range(2):
        pltpu.make_async_copy(dense_f.at[n], dense_out.at[n], end_sem.at[2 + n]).wait()


def last_outputs(
    xe, dpre, u, de, act, grads, dense, small,
    inner, outer, act_out, grads_out, qkv_out, attn_out, gain_out, router_out, bias_out,
    inner_v, outer_v, grads_f, dense_f, out_sem,
):
    sent = []

    def store(src, dst):
        copy = pltpu.make_async_copy(src, dst, out_sem.at[len(sent)])
        copy.start()
        sent.append(copy)

    store(act, act_out)
    grads_f[...] = grads[...].reshape(ROWS, D).astype(f32)
    store(grads_f, grads_out)
    for n in range(2):
        dense_f[:, HALF * n : HALF * (n + 1)] = dense[n].reshape(D, HALF).astype(f32)
    for j in range(3):
        store(dense_f.at[HF * j : HF * (j + 1)], qkv_out.at[j])
    store(dense_f.at[3 * HF : D], attn_out)
    for e in range(2):
        for one, two, total, out in ((xe, dpre, inner_v, inner), (u, de, outer_v, outer)):
            right = two[:, e].reshape(SLOTS, D)
            for i in range(3):
                cols = slice(256 * i, 256 * (i + 1))
                left = one[:, e, :, cols] if one is u else one[:, e, :, :, cols]
                total[e, cols, :] = tn(left.reshape(SLOTS, 256), right)
                store(total.at[e, cols], out.at[e, cols])
    router_out[...] = small[0:32, :]
    gain_out[...] = small[GAIN0 : GAIN1 + 1, :]
    for h in range(HEADS):
        bias_out[h] = small[BIAS : BIAS + 1, 16 * h : 16 * (h + 1)]
    for copy in sent:
        copy.wait()


def body(
    tokens, cotangent, norm_gains, w_qkv, w_attn_out, bias_table, router, w_in, w_out, routes, segments
):
    vmem = pl.BlockSpec(memory_space=pltpu.VMEM)
    hbm = pl.BlockSpec(memory_space=pl.ANY)
    dma = pltpu.SemaphoreType.DMA
    rows4 = pltpu.VMEM((2, TZ, OWN, D), bf16)
    messages = pltpu.VMEM((2, 2, DP, PAD, D), bf16)
    expert_rows = pltpu.VMEM((2, 2, ER, D), bf16)
    cuts = pltpu.VMEM((2, DP, CUT, HALF), bf16)
    pieces = pltpu.VMEM((DP, SMALL, 128), bf16)
    scratch = dict(
        xin=rows4,
        gin=rows4,
        w_qkv=pltpu.VMEM((3, HF, D), bf16),
        w_in=pltpu.VMEM((2, D, D), bf16),
        w_out=pltpu.VMEM((2, D, D), bf16),
        wall=pltpu.VMEM((TZ, HF, D), bf16),
        part_o=rows4, rs_o=rows4, o_full=rows4,
        call=pltpu.VMEM((2, TZ, BLOCK, HF), bf16),
        normed=pltpu.VMEM((ROWS, D), bf16),
        qkv=pltpu.VMEM((3, ROWS, HF), bf16),
        probs=pltpu.VMEM((2 * HEADS, BLOCK, BLOCK), f32),
        hidden=pltpu.VMEM((2, BLOCK, D), f32),
        hid_scale=pltpu.VMEM((2, BLOCK, 1), f32),
        normed2=pltpu.VMEM((2, BLOCK, D), bf16),
        rpad=pltpu.VMEM((SMALL, D), bf16),
        gate=pltpu.VMEM((2, BLOCK, 2), f32),
        slots=pltpu.VMEM((2, BLOCK, 2), jnp.int32),
        hits=pltpu.VMEM((2, 2, BLOCK, SMALL), f32),
        ptg=pltpu.VMEM((2, BLOCK, SLOTS), bf16),
        pick=pltpu.VMEM((2, SLOTS, BLOCK), bf16),
        pick_g=pltpu.VMEM((2, SLOTS, BLOCK), bf16),
        send_b=messages, recv_b=messages, send_e=messages, recv_e=messages,
        send_d=messages, recv_d=messages, send_x=messages, recv_x=messages,
        dact=expert_rows,
        part_y=rows4, rs_y=rows4, part_h=rows4, rs_h=rows4,
        dh_own=pltpu.VMEM((2, OWN, D), f32),
        dh_full=rows4, part_a=rows4, rs_a=rows4, in_full=rows4,
        dq_all=pltpu.VMEM((3, ROWS, HF), bf16),
        score_sum=pltpu.VMEM((HEADS, BLOCK, BLOCK), f32),
        gact=rows4,
        dense_s=cuts, dense_r=cuts, dense_f=cuts,
        small_acc=pltpu.VMEM((SMALL, D), f32),
        small_s=pieces, small_r=pieces,
        small_z=pltpu.VMEM((TZ, SMALL, 128), bf16),
        small_f=pieces,
        ld_sem=dma((5,)),
        out_sem=dma((2, 2)),
        end_sem=dma((4,)),
        w_ss=dma((1,)), w_rs=dma((1,)),
        c_ss=dma((2,)), c_rs=dma((2,)),
    )
    for name in ("b", "e", "d", "x"):
        scratch[name + "_ss"] = dma((2, 2))
        scratch[name + "_rs"] = dma((2, 2))
    for name in ("ro", "ao", "ry", "ay", "rh", "ah", "ra", "aa", "hand", "back", "dn", "df"):
        scratch[name + "_ss"] = dma((2,))
        scratch[name + "_rs"] = dma((2,))
    for name in ("sm", "sz", "sf"):
        scratch[name + "_ss"] = dma((1,))
        scratch[name + "_rs"] = dma((1,))
    scratch["turn_sem"] = pltpu.SemaphoreType.REGULAR

    shape = jax.ShapeDtypeStruct
    near = pltpu.VMEM
    act, grads, dense, small, xe, u, dpre, de = pl.pallas_call(
        kernel,
        out_shape=(
            near((2, TZ, OWN, D), bf16),
            near((2, TZ, OWN, D), bf16),
            near((2, DP, CUT, HALF), bf16),
            near((SMALL, D), f32),
            near((2, 2, DP, PAD, D), bf16),
            near((2, 2, ER, D), bf16),
            near((2, 2, ER, D), bf16),
            near((2, 2, DP, PAD, D), bf16),
        ),
        in_specs=[hbm, hbm, vmem, hbm, hbm, vmem, vmem, hbm, hbm, vmem, vmem],
        out_specs=(vmem,) * 8,
        scratch_shapes=list(scratch.values()),
        compiler_params=pltpu.CompilerParams(
            collective_id=0, has_side_effects=True, vmem_limit_bytes=55 * 1024 * 1024
        ),
        name="layers",
    )(
        tokens.reshape(2, TZ, OWN, D), cotangent.reshape(2, TZ, OWN, D), norm_gains,
        w_qkv[0].swapaxes(1, 2), w_attn_out[0], bias_table.swapaxes(1, 2),
        router.swapaxes(1, 2), w_in[0], w_out[0], routes.swapaxes(1, 2), segments,
    )

    inner, outer, act, grads, qkv_grad, attn_grad, gain_grad, router_grad, bias_grad = pl.pallas_call(
        last_outputs,
        out_shape=(
            shape((2, D, D), f32),
            shape((2, D, D), f32),
            shape((2, TZ, OWN, D), bf16),
            shape((ROWS, D), f32),
            shape((3, HF, D), f32),
            shape((HF, D), f32),
            shape((2, D), f32),
            shape((32, D), f32),
            shape((HEADS, 1, 16), f32),
        ),
        in_specs=[vmem] * 8,
        out_specs=(hbm,) * 6 + (vmem,) * 3,
        scratch_shapes=[
            pltpu.VMEM((2, D, D), f32),
            pltpu.VMEM((2, D, D), f32),
            pltpu.VMEM((ROWS, D), f32),
            pltpu.VMEM((D, D), f32),
            dma((18,)),
        ],
        compiler_params=pltpu.CompilerParams(vmem_limit_bytes=20 * 1024 * 1024),
        name="last_outputs",
    )(xe, dpre, u, de, act, grads, dense, small)

    return (
        act.reshape(ROWS, D)[None],
        grads[None],
        gain_grad[None],
        qkv_grad.swapaxes(1, 2)[None],
        attn_grad[None],
        bias_grad.transpose(1, 2, 0),
        router_grad.T[None],
        inner[None],
        outer[None],
    )


def solution(mesh):
    in_specs = (
        P("dp", None),
        P("dp", None),
        P("section", None, None),
        P("section", None, None, "tensor"),
        P("section", "tensor", None),
        P("section", None, "tensor"),
        P("section", None, None),
        P("section", "dp", None, "tensor"),
        P("section", "dp", "tensor", None),
        P("section", "dp", None),
        P("dp", None),
    )
    out_specs = (
        P("section", "dp", None),
        P("section", "dp", None),
        P("section", None, None),
        P("section", None, None, "tensor"),
        P("section", "tensor", None),
        P("section", None, "tensor"),
        P("section", None, None),
        P("section", "dp", None, "tensor"),
        P("section", "dp", "tensor", None),
    )
    return jax.shard_map(body, mesh=mesh, in_specs=in_specs, out_specs=out_specs, check_vma=False)
```

```python
import jax
import jax.numpy as jnp
from jax import lax
from jax.experimental import pallas as pl
from jax.experimental.pallas import tpu as pltpu
from jax.sharding import PartitionSpec as P

epsilon = 1e-06
masked_score = -1000000000.0
bucket_edges = (1, 2, 3, 4, 5, 6, 7, 8, 10, 13, 16, 20, 25, 32, 40)
MESH = pl.DeviceIdType.MESH
f32 = jnp.float32
bf16 = jnp.bfloat16

DP = 16
TZ = 4
ROWS = 256
BLOCK = 128
OWN = BLOCK // TZ
D = 768
HF = 192
HEADS = 3
PAD = 16
ER = DP * PAD
SLOTS = 2 * ER
GATE_ROW = 12
CUT = D // DP
SMALL = 48
GAIN0, GAIN1, BIAS = 32, 33, 34
HALF = D // 2
PARTS = D // 128
EDGES = (0,) + bucket_edges
FAR_FIRST = (2, 1, 3)


def nn(a, b):
    return lax.dot_general(a, b, (((1,), (0,)), ((), ())), preferred_element_type=f32)


def nt(a, b):
    return lax.dot_general(a, b, (((1,), (1,)), ((), ())), preferred_element_type=f32)


def tn(a, b):
    return lax.dot_general(a, b, (((0,), (0,)), ((), ())), preferred_element_type=f32)


def iota(shape, dim):
    return lax.broadcasted_iota(jnp.int32, shape, dim)


def rms_scale(values):
    return lax.rsqrt(jnp.mean(values * values, axis=-1, keepdims=True) + epsilon)


def kernel(
    tokens, cotangent, gains, w_qkv_hbm, w_att, bias_tab, router, w_in_hbm, w_out_hbm, routes, segments,
    act_out, grad_out, dense_out, small_out, xe_out, act, dpre, de_out,
    xin, gin, w_qkv, w_in, w_out, wall, part_o, rs_o, o_full, call, normed, qkv, probs, hidden, hid_scale, normed2, rpad,
    gate, slots, hits, ptg, pick, pick_g, send_b, recv_b, send_e, recv_e, send_d, recv_d, send_x,
    recv_x, dact, part_y, rs_y, part_h, rs_h, dh_own, dh_full, part_a, rs_a, in_full,
    dq_all, score_sum, gact, dense_s, dense_r, dense_f, small_acc, small_s, small_r, small_z, small_f,
    ld_sem, out_sem, end_sem, w_ss, w_rs, c_ss, c_rs, b_ss, b_rs, e_ss, e_rs, d_ss, d_rs, x_ss, x_rs,
    ro_ss, ro_rs, ao_ss, ao_rs, ry_ss, ry_rs, ay_ss, ay_rs, rh_ss, rh_rs, ah_ss, ah_rs, ra_ss, ra_rs, aa_ss, aa_rs,
    hand_ss, hand_rs, back_ss, back_rs, dn_ss, dn_rs, df_ss, df_rs, sm_ss, sm_rs, sz_ss, sz_rs,
    sf_ss, sf_rs, turn_sem,
):
    sec = lax.axis_index("section")
    me = lax.axis_index("dp")
    mz = lax.axis_index("tensor")
    first = sec == 0
    second = sec == 1

    load_in = pltpu.make_async_copy(w_in_hbm, w_in, ld_sem.at[0])
    load_out = pltpu.make_async_copy(w_out_hbm, w_out, ld_sem.at[1])
    load_qkv = pltpu.make_async_copy(w_qkv_hbm, w_qkv, ld_sem.at[2])
    load_att = pltpu.make_async_copy(w_att, wall.at[mz], ld_sem.at[3])
    load_x = pltpu.make_async_copy(tokens, xin, ld_sem.at[4])
    load_g = pltpu.make_async_copy(cotangent, gin, ld_sem.at[4])

    @pl.when(first)
    def _():
        load_x.start()

    @pl.when(second)
    def _():
        load_g.start()

    load_qkv.start()
    load_att.start()

    barrier = pltpu.get_barrier_semaphore()

    def greet(i, carry):
        pl.semaphore_signal(
            barrier, inc=1, device_id={"dp": lax.rem(me + i, DP)}, device_id_type=MESH
        )
        return carry

    lax.fori_loop(1, DP, greet, 0)
    for i in range(1, TZ):
        pl.semaphore_signal(
            barrier, inc=1, device_id={"tensor": lax.rem(mz + i, TZ)}, device_id_type=MESH
        )
    pl.semaphore_signal(barrier, inc=1, device_id={"section": 1 - sec}, device_id_type=MESH)

    def z_copy(src, dst, ss, rs, peer):
        return pltpu.make_async_remote_copy(
            src_ref=src, dst_ref=dst, send_sem=ss, recv_sem=rs,
            device_id={"tensor": peer}, device_id_type=MESH,
        )

    def z_round(buf, ss, rs):
        part = buf.at[pl.ds(0, TZ - 1)]
        return z_copy(part, part, ss, rs, lax.rem(mz + 1, TZ))

    def gather_start(buf, ss, rs):
        for i in FAR_FIRST:
            z_copy(buf.at[mz], buf.at[mz], ss, rs, lax.rem(mz + i, TZ)).start()

    def gather_recv(buf, ss, rs):
        z_round(buf, ss, rs).wait_recv()

    def gather_sent(buf, ss, rs):
        z_round(buf, ss, rs).wait_send()

    def scatter_start(part, rcv, ss, rs):
        for i in FAR_FIRST:
            peer = lax.rem(mz + i, TZ)
            z_copy(part.at[peer], rcv.at[mz], ss, rs, peer).start()

    def scatter_sum(part, rcv, ss, rs):
        z_round(rcv, ss, rs).wait_recv()
        total = part[mz].astype(f32)
        for i in range(1, TZ):
            total += rcv[lax.rem(mz + i, TZ)].astype(f32)
        return total

    def scatter_sent(part, rcv, ss, rs):
        z_round(part, ss, rs).wait_send()

    def dp_copy(src, dst, ss, rs, peer):
        return pltpu.make_async_remote_copy(
            src_ref=src, dst_ref=dst, send_sem=ss, recv_sem=rs,
            device_id={"dp": peer}, device_id_type=MESH,
        )

    def dp_round(buf, ss, rs, count=DP - 1):
        part = buf.at[pl.ds(0, count)]
        return dp_copy(part, part, ss, rs, lax.rem(me + 1, DP))

    me_x, me_y = me // 4, me % 4

    def away(i):
        return 2 + ((i + 1) // 2) * (1 - 2 * (i % 2))

    def others(step):
        def one(i, j):
            step(((me_x + away(i)) % 4) * 4 + (me_y + away(j)) % 4)

        def pair(n, carry):
            j = 1 + (n + 1) // 2 - n // 5
            i = n - j * (j - 1) // 2
            one(i, j)
            one(j, i)
            return carry

        one(0, 0)
        lax.fori_loop(0, 2, pair, 0)
        one(1, 1)
        one(2, 2)
        lax.fori_loop(2, 6, pair, 0)

    def swap_start(snd, rcv, ss, rs):
        others(lambda peer: dp_copy(snd.at[peer], rcv.at[me], ss, rs, peer).start())
        rcv[me] = snd[me]

    def swap_recv(snd, rcv, ss, rs):
        dp_round(rcv, ss, rs).wait_recv()

    def swap_sent(snd, rcv, ss, rs):
        dp_round(snd, ss, rs).wait_send()

    def spread(buf, ss, rs):
        others(lambda peer: dp_copy(buf.at[me], buf.at[me], ss, rs, peer).start())

    def spread_recv(buf, ss, rs):
        dp_round(buf, ss, rs).wait_recv()

    def spread_sent(buf, ss, rs):
        dp_round(buf, ss, rs).wait_send()

    def hand(b, t, ss, rs, src, dst):
        return pltpu.make_async_remote_copy(
            src_ref=src.at[b, t], dst_ref=dst.at[b, t], send_sem=ss.at[b],
            recv_sem=rs.at[b], device_id={"section": 1 - sec}, device_id_type=MESH,
        )

    def hand_all(b, ss, rs, src, dst):
        return pltpu.make_async_remote_copy(
            src_ref=src.at[b], dst_ref=dst.at[b], send_sem=ss.at[b],
            recv_sem=rs.at[b], device_id={"section": 1 - sec}, device_id_type=MESH,
        )

    def both(sems, b):
        return sems[0].at[b], sems[1].at[b]

    c_sem, b_sem, d_sem = (c_ss, c_rs), (b_ss, b_rs), (d_ss, d_rs)
    ro, ao = (ro_ss, ro_rs), (ao_ss, ao_rs)
    ry, ay, rh = (ry_ss, ry_rs), (ay_ss, ay_rs), (rh_ss, rh_rs)
    ah, ra, aa = (ah_ss, ah_rs), (ra_ss, ra_rs), (aa_ss, aa_rs)
    dn, df = (dn_ss, dn_rs), (df_ss, df_rs)

    row = iota((BLOCK, BLOCK), 0)
    col = iota((BLOCK, BLOCK), 1)
    eye = row == col
    earlier = (row > col).astype(f32).astype(bf16)
    every = jnp.ones((BLOCK, BLOCK), bf16)
    lane = iota((BLOCK, SMALL), 1)
    slot_lane = iota((BLOCK, SLOTS), 1)
    slot_sub = iota((SLOTS, BLOCK), 0)

    def to_col(values):
        return jnp.sum(jnp.where(eye, values, 0.0), axis=1, keepdims=True)

    def to_row(values):
        return jnp.sum(jnp.where(eye, values, 0.0), axis=0, keepdims=True)

    rpad[...] = jnp.zeros((SMALL, D), bf16)
    rpad[0:32, :] = router[0]
    for b in range(2):
        named = routes[0, :, b * BLOCK : (b + 1) * BLOCK].astype(f32)
        e0 = to_col(named[0:1, :]).astype(jnp.int32)
        e1 = to_col(named[1:2, :]).astype(jnp.int32)
        hit0 = (lane == e0).astype(f32)
        hit1 = (lane == e1).astype(f32)
        rank0 = jnp.sum(nn(earlier, hit0.astype(bf16)) * hit0, axis=1, keepdims=True)
        rank1 = jnp.sum(
            (nn(earlier, hit1.astype(bf16)) + nn(every, hit0.astype(bf16))) * hit1,
            axis=1, keepdims=True,
        )
        slot0 = (e0 % 2) * ER + (e0 // 2) * PAD + rank0.astype(jnp.int32)
        slot1 = (e1 % 2) * ER + (e1 // 2) * PAD + rank1.astype(jnp.int32)
        slots[b, :, 0:1] = slot0
        slots[b, :, 1:2] = slot1
        hits[b, 0] = hit0
        hits[b, 1] = hit1
        row0 = to_row(slot0.astype(f32)).astype(jnp.int32)
        row1 = to_row(slot1.astype(f32)).astype(jnp.int32)
        pick[b] = ((slot_sub == row0) | (slot_sub == row1)).astype(f32).astype(bf16)

    gain0 = gains[0, 0:1, :].astype(f32)
    gain1 = gains[0, 1:2, :].astype(f32)
    gap = row - col
    head_of = iota((BLOCK, HF), 1) // (HF // HEADS)

    @pl.when(first)
    def _():
        load_x.wait()

    @pl.when(second)
    def _():
        load_g.wait()

    load_qkv.wait()
    load_att.wait()
    load_in.start()
    load_out.start()

    @pl.when(second)
    def _():
        pl.semaphore_wait(barrier, DP + TZ - 1)
        pl.semaphore_wait(turn_sem, 1)
        gather_start(wall, w_ss.at[0], w_rs.at[0])

    for b in range(2):
        rows = slice(b * BLOCK, (b + 1) * BLOCK)

        @pl.when(second)
        def _():
            hand_all(b, hand_ss, hand_rs, gact, xin).wait_recv()

        x = xin[b].reshape(BLOCK, D).astype(f32)
        normed[rows, :] = (x * rms_scale(x) * gain0).astype(bf16)
        for j in range(3):
            qkv[j, rows, :] = nt(normed[rows, :], w_qkv[j]).astype(bf16)
        seg_row = segments[b : b + 1, :].astype(f32)
        allowed = (gap >= 0) & (seg_row == to_col(seg_row))
        q = qkv[0, rows, :]
        k = qkv[1, rows, :]
        v = qkv[2, rows, :]
        context = jnp.zeros((BLOCK, HF), f32)
        for h in range(HEADS):
            bias = jnp.broadcast_to(bias_tab[0, h : h + 1, 0:1].astype(f32), (BLOCK, BLOCK))
            for n, edge in enumerate(bucket_edges):
                bias = jnp.where(
                    gap >= edge, bias_tab[0, h : h + 1, n + 1 : n + 2].astype(f32), bias
                )
            score = nt(jnp.where(head_of == h, q, jnp.zeros_like(q)), k) * 0.125 + bias
            score = jnp.where(allowed, score, masked_score)
            score = jnp.exp(score - jnp.max(score, axis=-1, keepdims=True))
            prob = score / jnp.sum(score, axis=-1, keepdims=True)
            probs[b * HEADS + h] = prob
            context = jnp.where(head_of == h, nn(prob.astype(bf16), v), context)
        call[b, mz] = context.astype(bf16)

        @pl.when(first)
        def _():
            if b == 0:
                pl.semaphore_wait(barrier, DP + TZ - 1)
            part_o[b] = nn(call[b, mz], wall[mz]).astype(bf16).reshape(TZ, OWN, D)
            scatter_start(part_o.at[b], rs_o.at[b], *both(ro, b))

        @pl.when(second)
        def _():
            gather_start(call.at[b], *both(c_sem, b))

    def dispatch(chosen, values, snd, rcv, sems, b):
        for e in range(2):
            out = nn(chosen[b, ER * e : ER * (e + 1), :], values).astype(bf16)
            snd[b, e] = out.reshape(DP, PAD, D)
            swap_start(snd.at[b, e], rcv.at[b, e], sems[0].at[b, e], sems[1].at[b, e])

    def dispatch_grad(b):
        dispatch(pick_g, gin[b].reshape(BLOCK, D), send_d, recv_d, d_sem, b)

    @pl.when(first)
    def _():
        for b in range(2):
            o_full[b, mz] = scatter_sum(part_o.at[b], rs_o.at[b], *both(ro, b)).astype(bf16)
            gather_start(o_full.at[b], *both(ao, b))

    for b in range(2):
        @pl.when(first)
        def _():
            gather_recv(o_full.at[b], *both(ao, b))
            if b == 1:
                pl.semaphore_signal(
                    turn_sem, inc=1, device_id={"section": 1 - sec}, device_id_type=MESH
                )
            hidden[b] = xin[b].reshape(BLOCK, D).astype(f32) + o_full[b].reshape(BLOCK, D).astype(f32)

        @pl.when(second)
        def _():
            gather_recv(call.at[b], *both(c_sem, b))
            if b == 0:
                gather_recv(wall, w_ss.at[0], w_rs.at[0])
            total = xin[b].reshape(BLOCK, D).astype(f32)
            for t in range(TZ):
                total += nn(call[b, t], wall[t])
            hidden[b] = total

        h = hidden[b]
        scale = rms_scale(h)
        hid_scale[b] = scale
        normed2[b] = (h * scale * gain1).astype(bf16)
        dispatch(pick, normed2[b], send_b, recv_b, b_sem, b)

        z = nt(normed2[b], rpad[...])
        z0 = jnp.sum(z * hits[b, 0], axis=1, keepdims=True)
        z1 = jnp.sum(z * hits[b, 1], axis=1, keepdims=True)
        g0 = 1.0 / (1.0 + jnp.exp(z1 - z0))
        g1 = 1.0 / (1.0 + jnp.exp(z0 - z1))
        gate[b, :, 0:1] = g0
        gate[b, :, 1:2] = g1
        slot0 = slots[b, :, 0:1]
        slot1 = slots[b, :, 1:2]
        row0 = to_row(slot0.astype(f32)).astype(jnp.int32)
        row1 = to_row(slot1.astype(f32)).astype(jnp.int32)
        pick_g[b] = (
            jnp.where(slot_sub == row0, to_row(g0), 0.0)
            + jnp.where(slot_sub == row1, to_row(g1), 0.0)
        ).astype(bf16)

        @pl.when(second)
        def _():
            dispatch_grad(b)

        ptg[b] = (
            jnp.where(slot_lane == slot0, g0, 0.0) + jnp.where(slot_lane == slot1, g1, 0.0)
        ).astype(bf16)

    root = 0.7978845608028654
    saved = []

    def save(b, n, src, dst):
        copy = pltpu.make_async_copy(src.at[b], dst.at[b], out_sem.at[b, n])
        copy.start()
        saved.append(copy)

    def expert_forward(b, e):
        swap_recv(send_b.at[b, e], recv_b.at[b, e], b_ss.at[b, e], b_rs.at[b, e])
        x = recv_b[b, e].reshape(ER, D)
        for n in range(3):
            cols = slice(256 * n, 256 * (n + 1))
            pre = nn(x, w_in[e, :, cols])
            square = pre * pre
            wave = jnp.tanh(root * pre * (1.0 + 0.044715 * square))
            lift = 0.5 * (1.0 + wave)
            act[b, e, :, cols] = (pre * lift).astype(bf16)
            slope = lift + 0.5 * root * pre * (1.0 - wave * wave) * (1.0 + 0.134145 * square)
            dact[b, e, :, cols] = slope.astype(bf16)
        out = nn(act[b, e], w_out[e])
        send_e[b, e] = out.astype(bf16).reshape(DP, PAD, D)

    def return_rows(b, e):
        swap_start(send_e.at[b, e], recv_e.at[b, e], e_ss.at[b, e], e_rs.at[b, e])

    def expert_backward(b, e):
        swap_recv(send_d.at[b, e], recv_d.at[b, e], d_ss.at[b, e], d_rs.at[b, e])
        de = recv_d[b, e].reshape(ER, D)
        for n in range(3):
            cols = slice(256 * n, 256 * (n + 1))
            grad = nt(de, w_out[e, cols, :])
            dpre[b, e, :, cols] = (grad * dact[b, e, :, cols].astype(f32)).astype(bf16)
        out = nt(dpre[b, e], w_in[e])
        send_x[b, e] = out.astype(bf16).reshape(DP, PAD, D)
        rows = send_e[b, e].reshape(ER, D).astype(f32)
        weight = jnp.sum(rows * de.astype(f32), axis=1, keepdims=True)
        slot = iota((ER, 128), 0) % PAD
        spread_out = jnp.where(iota((ER, 128), 1) == slot, weight, 0.0).reshape(DP, PAD, 128)
        line = jnp.sum(spread_out, axis=1, keepdims=True)
        coarse = line.astype(bf16).astype(f32)
        place = iota((DP, PAD, 128), 1)
        extra = jnp.where(place == GATE_ROW, coarse, 0.0)
        extra += jnp.where(place == GATE_ROW + 1, line - coarse, 0.0)
        near = out[:, 0:128].reshape(DP, PAD, 128) + extra
        send_x[b, e, :, :, 0:128] = near.astype(bf16)
        swap_start(send_x.at[b, e], recv_x.at[b, e], x_ss.at[b, e], x_rs.at[b, e])

    def each_expert(step):
        def one(e, carry):
            step(e)
            return carry

        lax.fori_loop(0, 2, one, 0)

    def each_part(step):
        def one(i, carry):
            step(i // 2, i % 2)
            return carry

        lax.fori_loop(0, 4, one, 0)

    def combine(b):
        for e in range(2):
            swap_recv(send_e.at[b, e], recv_e.at[b, e], e_ss.at[b, e], e_rs.at[b, e])
        out = nn(ptg[b], recv_e[b].reshape(SLOTS, D))
        part_y[b] = out.astype(bf16).reshape(TZ, OWN, D)
        scatter_start(part_y.at[b], rs_y.at[b], *both(ry, b))

    def settle(b):
        own = pl.ds(pl.multiple_of(mz * OWN, OWN), OWN)
        total = scatter_sum(part_y.at[b], rs_y.at[b], *both(ry, b)) + hidden[b, own, :]
        gact[b, mz] = total.astype(bf16)
        gather_start(gact.at[b], *both(ay, b))

    load_in.wait()
    load_out.wait()

    @pl.when(first)
    def _():
        def part(b, e):
            expert_forward(b, e)
            return_rows(b, e)

        each_part(part)

    @pl.when(second)
    def _():
        def block(b, carry):
            each_expert(lambda e: expert_forward(b, e))
            each_expert(lambda e: expert_backward(b, e))
            return carry

        lax.fori_loop(0, 2, block, 0)
        each_part(return_rows)

    for b in range(2):
        save(b, 0, recv_b, xe_out)

    @pl.when(first)
    def _():
        combine(0)
        combine(1)
        for b in range(2):
            settle(b)
            hand(b, mz, hand_ss, hand_rs, gact, xin).start()
        for b in range(2):
            gather_recv(gact.at[b], *both(ay, b))
            for i in range(1, TZ):
                hand(b, lax.rem(mz + i, TZ), hand_ss, hand_rs, gact, xin).start()
        for b in range(2):
            hand_all(b, back_ss, back_rs, in_full, gin).wait_recv()
            dispatch_grad(b)
        each_part(expert_backward)

    for b in range(2):
        save(b, 1, recv_d, de_out)

    for b in range(2):
        pt0 = (slot_lane == slots[b, :, 0:1]).astype(f32).astype(bf16)
        pt1 = (slot_lane == slots[b, :, 1:2]).astype(f32).astype(bf16)
        for e in range(2):
            swap_recv(send_x.at[b, e], recv_x.at[b, e], x_ss.at[b, e], x_rs.at[b, e])
        if b == 1:
            @pl.when(first)
            def _():
                pl.semaphore_signal(
                    turn_sem, inc=1, device_id={"section": 1 - sec}, device_id_type=MESH
                )

        back = recv_x[b].reshape(SLOTS, D)

        def gate_product(slot):
            line = slot - slot % PAD + GATE_ROW
            both_rows = ((slot_lane == line) | (slot_lane == line + 1)).astype(f32).astype(bf16)
            found = nn(both_rows, back[:, 0:128])
            mine = iota((BLOCK, 128), 1) == slot % PAD
            return jnp.sum(jnp.where(mine, found, 0.0), axis=1, keepdims=True)

        q0 = gate_product(slots[b, :, 0:1])
        q1 = gate_product(slots[b, :, 1:2])
        dc = gate[b, :, 1:2] * q0 - gate[b, :, 0:1] * q1
        dz = ((hits[b, 0] - hits[b, 1]) * dc).astype(bf16)
        db = nn(pt0 + pt1, back) + nn(dz, rpad[...])
        part_h[b] = db.astype(bf16).reshape(TZ, OWN, D)
        scatter_start(part_h.at[b], rs_h.at[b], *both(rh, b))
        unit = (lane == GAIN1).astype(f32).astype(bf16)
        small = tn(dz, normed2[b])
        small += tn(unit, (db * hidden[b] * hid_scale[b]).astype(bf16))
        if b == 0:
            small_acc[...] = small
        else:
            small_acc[...] += small

    for b in range(2):
        own = pl.ds(pl.multiple_of(mz * OWN, OWN), OWN)
        s_own = hid_scale[b, own, :]
        hat = hidden[b, own, :] * s_own
        lifted = scatter_sum(part_h.at[b], rs_h.at[b], *both(rh, b)) * gain1
        total = gin[b, mz].astype(f32) + s_own * (
            lifted - hat * jnp.mean(lifted * hat, axis=-1, keepdims=True)
        )
        dh_own[b] = total
        dh_full[b, mz] = total.astype(bf16)
        gather_start(dh_full.at[b], *both(ah, b))

    for b in range(2):
        rows = slice(b * BLOCK, (b + 1) * BLOCK)
        gather_recv(dh_full.at[b], *both(ah, b))
        dc = nt(dh_full[b].reshape(BLOCK, D), wall[mz]).astype(bf16)
        q = qkv[0, rows, :]
        k = qkv[1, rows, :]
        v = qkv[2, rows, :]
        dq = jnp.zeros((BLOCK, HF), f32)
        dk = jnp.zeros((BLOCK, HF), f32)
        dv = jnp.zeros((BLOCK, HF), f32)
        for h in range(HEADS):
            mine = head_of == h
            prob = probs[b * HEADS + h]
            dp = nt(jnp.where(mine, dc, jnp.zeros_like(dc)), v)
            ds = (prob * (dp - jnp.sum(prob * dp, axis=-1, keepdims=True))).astype(bf16)
            if b == 0:
                score_sum[h] = ds.astype(f32)
            else:
                score_sum[h] += ds.astype(f32)
            dq = jnp.where(mine, nn(ds, k), dq)
            dk = jnp.where(mine, tn(ds, q), dk)
            dv = jnp.where(mine, tn(prob.astype(bf16), dc), dv)
        dq_all[0, rows, :] = (dq * 0.125).astype(bf16)
        dq_all[1, rows, :] = (dk * 0.125).astype(bf16)
        dq_all[2, rows, :] = dv.astype(bf16)
        da = nn(dq_all[0, rows, :], w_qkv[0])
        da += nn(dq_all[1, rows, :], w_qkv[1])
        da += nn(dq_all[2, rows, :], w_qkv[2])
        part_a[b] = da.astype(bf16).reshape(TZ, OWN, D)
        scatter_start(part_a.at[b], rs_a.at[b], *both(ra, b))

    def dense_part():
        own_context = jnp.concatenate([call[0, mz], call[1, mz]], axis=0)
        for n in range(2):
            cols = slice(HALF * n, HALF * (n + 1))
            for j in range(3):
                out = tn(dq_all[j], normed[:, cols]).astype(bf16)
                dense_s[n, 4 * j : 4 * j + 4] = out.reshape(4, CUT, HALF)
            grad = dh_full[:, :, :, cols].reshape(ROWS, HALF)
            dense_s[n, 12:16] = tn(own_context, grad).astype(bf16).reshape(4, CUT, HALF)
            swap_start(dense_s.at[n], dense_r.at[n], *both(dn, n))
        small = small_acc[...]
        unit = (lane == GAIN0).astype(f32).astype(bf16)
        for b in range(2):
            x = xin[b].reshape(BLOCK, D).astype(f32)
            da = part_a[b].reshape(BLOCK, D).astype(f32)
            small += tn(unit, (da * x * rms_scale(x)).astype(bf16))
        bias_rows = []
        for h in range(HEADS):
            for n in range(len(EDGES)):
                hit = gap >= EDGES[n]
                if n + 1 < len(EDGES):
                    hit = hit & (gap < EDGES[n + 1])
                bias_rows.append(jnp.sum(jnp.where(hit, score_sum[h], 0.0), axis=0, keepdims=True))
        bias_col = jnp.sum(jnp.concatenate(bias_rows, axis=0), axis=1, keepdims=True)
        diagonal = iota((SMALL, 128), 0) == iota((SMALL, 128), 1)
        bias_row = jnp.sum(jnp.where(diagonal, bias_col, 0.0), axis=0, keepdims=True)
        mine = iota((SMALL, 128), 0) == BIAS + mz
        for j in range(PARTS):
            piece = small[:, 128 * j : 128 * (j + 1)]
            if j == 0:
                piece += jnp.where(mine, bias_row, 0.0)
            small_s[j] = piece.astype(bf16)

            @pl.when(me != j)
            def _():
                dp_copy(small_s.at[j], small_r.at[me], sm_ss.at[0], sm_rs.at[0], j).start()

    dense_part()

    for b in range(2):
        x_own = xin[b, mz].astype(f32)
        r_own = rms_scale(x_own)
        hat = x_own * r_own
        lifted = scatter_sum(part_a.at[b], rs_a.at[b], *both(ra, b)) * gain0
        total = dh_own[b] + r_own * (lifted - hat * jnp.mean(lifted * hat, axis=-1, keepdims=True))
        in_full[b, mz] = total.astype(bf16)
        gather_start(in_full.at[b], *both(aa, b))

        @pl.when(second)
        def _():
            hand(b, mz, back_ss, back_rs, in_full, gin).start()

    for b in range(2):
        gather_recv(in_full.at[b], *both(aa, b))

        @pl.when(second)
        def _():
            for i in range(1, TZ):
                hand(b, lax.rem(mz + i, TZ), back_ss, back_rs, in_full, gin).start()

    save_grad = pltpu.make_async_copy(in_full, grad_out, end_sem.at[1])
    save_grad.start()

    @pl.when(second)
    def _():
        for b in range(2):
            combine(b)
        for b in range(2):
            settle(b)
        for b in range(2):
            gather_recv(gact.at[b], *both(ay, b))

    save_act = pltpu.make_async_copy(gact, act_out, end_sem.at[0])
    save_act.start()

    holds = me < PARTS

    @pl.when(second)
    def _():
        pl.semaphore_wait(turn_sem, 1)

    for n in range(2):
        swap_recv(dense_s.at[n], dense_r.at[n], *both(dn, n))
        total = dense_r[n, 0].astype(f32)
        for p in range(1, DP):
            total += dense_r[n, p].astype(f32)
        dense_f[n, me] = total.astype(bf16)
        spread(dense_f.at[n], *both(df, n))

    @pl.when(holds)
    def _():
        small_r[me] = small_s[me]
        dp_round(small_r, sm_ss.at[0], sm_rs.at[0]).wait_recv()
        total = small_r[0].astype(f32)
        for p in range(1, DP):
            total += small_r[p].astype(f32)
        small_z[mz] = total.astype(bf16)
        gather_start(small_z, sz_ss.at[0], sz_rs.at[0])
        gather_recv(small_z, sz_ss.at[0], sz_rs.at[0])
        total = small_z[0].astype(f32)
        for t in range(1, TZ):
            total += small_z[t].astype(f32)
        small_f[me] = total.astype(bf16)
        spread(small_f, sf_ss.at[0], sf_rs.at[0])

    @pl.when(second)
    def _():
        gather_sent(wall, w_ss.at[0], w_rs.at[0])

    for b in range(2):
        for e in range(2):
            swap_sent(send_b.at[b, e], recv_b.at[b, e], b_ss.at[b, e], b_rs.at[b, e])
            swap_sent(send_e.at[b, e], recv_e.at[b, e], e_ss.at[b, e], e_rs.at[b, e])
            swap_sent(send_d.at[b, e], recv_d.at[b, e], d_ss.at[b, e], d_rs.at[b, e])
            swap_sent(send_x.at[b, e], recv_x.at[b, e], x_ss.at[b, e], x_rs.at[b, e])
        scatter_sent(part_y.at[b], rs_y.at[b], *both(ry, b))
        gather_sent(gact.at[b], *both(ay, b))
        scatter_sent(part_h.at[b], rs_h.at[b], *both(rh, b))
        gather_sent(dh_full.at[b], *both(ah, b))
        scatter_sent(part_a.at[b], rs_a.at[b], *both(ra, b))
        gather_sent(in_full.at[b], *both(aa, b))

        @pl.when(first)
        def _():
            scatter_sent(part_o.at[b], rs_o.at[b], *both(ro, b))
            gather_sent(o_full.at[b], *both(ao, b))
            hand_all(b, hand_ss, hand_rs, gact, xin).wait_send()

        @pl.when(second)
        def _():
            gather_sent(call.at[b], *both(c_sem, b))
            hand_all(b, back_ss, back_rs, in_full, gin).wait_send()

    for n in range(2):
        swap_sent(dense_s.at[n], dense_r.at[n], *both(dn, n))

    @pl.when(holds)
    def _():
        dp_round(small_s, sm_ss.at[0], sm_rs.at[0], PARTS - 1).wait_send()
        gather_sent(small_z, sz_ss.at[0], sz_rs.at[0])
        spread_sent(small_f, sf_ss.at[0], sf_rs.at[0])

    @pl.when(jnp.logical_not(holds))
    def _():
        dp_round(small_s, sm_ss.at[0], sm_rs.at[0], PARTS).wait_send()

    for copy in saved:
        copy.wait()
    for n in range(2):
        spread_recv(dense_f.at[n], *both(df, n))
        pltpu.make_async_copy(dense_f.at[n], dense_out.at[n], end_sem.at[2 + n]).start()

    @pl.when(holds)
    def _():
        dp_round(small_f, sf_ss.at[0], sf_rs.at[0], PARTS - 1).wait_recv()

    @pl.when(jnp.logical_not(holds))
    def _():
        dp_round(small_f, sf_ss.at[0], sf_rs.at[0], PARTS).wait_recv()

    for j in range(PARTS):
        small_out[:, 128 * j : 128 * (j + 1)] = small_f[j].astype(f32)
    held = small_f[0].astype(f32)
    mine = iota((SMALL, 128), 0) == BIAS + mz
    small_out[BIAS : BIAS + 1, 0:128] = jnp.sum(jnp.where(mine, held, 0.0), axis=0, keepdims=True)
    for n in range(2):
        spread_sent(dense_f.at[n], *both(df, n))
    save_act.wait()
    save_grad.wait()
    for n in range(2):
        pltpu.make_async_copy(dense_f.at[n], dense_out.at[n], end_sem.at[2 + n]).wait()


def last_outputs(
    xe, dpre, u, de, act, grads, dense, small,
    inner, outer, act_out, grads_out, qkv_out, attn_out, gain_out, router_out, bias_out,
    inner_v, outer_v, grads_f, dense_f, out_sem,
):
    sent = []

    def store(src, dst):
        copy = pltpu.make_async_copy(src, dst, out_sem.at[len(sent)])
        copy.start()
        sent.append(copy)

    store(act, act_out)
    grads_f[...] = grads[...].reshape(ROWS, D).astype(f32)
    store(grads_f, grads_out)
    for n in range(2):
        dense_f[:, HALF * n : HALF * (n + 1)] = dense[n].reshape(D, HALF).astype(f32)
    for j in range(3):
        store(dense_f.at[HF * j : HF * (j + 1)], qkv_out.at[j])
    store(dense_f.at[3 * HF : D], attn_out)
    for e in range(2):
        for one, two, total, out in ((xe, dpre, inner_v, inner), (u, de, outer_v, outer)):
            right = two[:, e].reshape(SLOTS, D)
            for i in range(3):
                cols = slice(256 * i, 256 * (i + 1))
                left = one[:, e, :, cols] if one is u else one[:, e, :, :, cols]
                total[e, cols, :] = tn(left.reshape(SLOTS, 256), right)
                store(total.at[e, cols], out.at[e, cols])
    router_out[...] = small[0:32, :]
    gain_out[...] = small[GAIN0 : GAIN1 + 1, :]
    for h in range(HEADS):
        bias_out[h] = small[BIAS : BIAS + 1, 16 * h : 16 * (h + 1)]
    for copy in sent:
        copy.wait()


def body(
    tokens, cotangent, norm_gains, w_qkv, w_attn_out, bias_table, router, w_in, w_out, routes, segments
):
    vmem = pl.BlockSpec(memory_space=pltpu.VMEM)
    hbm = pl.BlockSpec(memory_space=pl.ANY)
    dma = pltpu.SemaphoreType.DMA
    rows4 = pltpu.VMEM((2, TZ, OWN, D), bf16)
    messages = pltpu.VMEM((2, 2, DP, PAD, D), bf16)
    expert_rows = pltpu.VMEM((2, 2, ER, D), bf16)
    cuts = pltpu.VMEM((2, DP, CUT, HALF), bf16)
    pieces = pltpu.VMEM((DP, SMALL, 128), bf16)
    scratch = dict(
        xin=rows4,
        gin=rows4,
        w_qkv=pltpu.VMEM((3, HF, D), bf16),
        w_in=pltpu.VMEM((2, D, D), bf16),
        w_out=pltpu.VMEM((2, D, D), bf16),
        wall=pltpu.VMEM((TZ, HF, D), bf16),
        part_o=rows4, rs_o=rows4, o_full=rows4,
        call=pltpu.VMEM((2, TZ, BLOCK, HF), bf16),
        normed=pltpu.VMEM((ROWS, D), bf16),
        qkv=pltpu.VMEM((3, ROWS, HF), bf16),
        probs=pltpu.VMEM((2 * HEADS, BLOCK, BLOCK), f32),
        hidden=pltpu.VMEM((2, BLOCK, D), f32),
        hid_scale=pltpu.VMEM((2, BLOCK, 1), f32),
        normed2=pltpu.VMEM((2, BLOCK, D), bf16),
        rpad=pltpu.VMEM((SMALL, D), bf16),
        gate=pltpu.VMEM((2, BLOCK, 2), f32),
        slots=pltpu.VMEM((2, BLOCK, 2), jnp.int32),
        hits=pltpu.VMEM((2, 2, BLOCK, SMALL), f32),
        ptg=pltpu.VMEM((2, BLOCK, SLOTS), bf16),
        pick=pltpu.VMEM((2, SLOTS, BLOCK), bf16),
        pick_g=pltpu.VMEM((2, SLOTS, BLOCK), bf16),
        send_b=messages, recv_b=messages, send_e=messages, recv_e=messages,
        send_d=messages, recv_d=messages, send_x=messages, recv_x=messages,
        dact=expert_rows,
        part_y=rows4, rs_y=rows4, part_h=rows4, rs_h=rows4,
        dh_own=pltpu.VMEM((2, OWN, D), f32),
        dh_full=rows4, part_a=rows4, rs_a=rows4, in_full=rows4,
        dq_all=pltpu.VMEM((3, ROWS, HF), bf16),
        score_sum=pltpu.VMEM((HEADS, BLOCK, BLOCK), f32),
        gact=rows4,
        dense_s=cuts, dense_r=cuts, dense_f=cuts,
        small_acc=pltpu.VMEM((SMALL, D), f32),
        small_s=pieces, small_r=pieces,
        small_z=pltpu.VMEM((TZ, SMALL, 128), bf16),
        small_f=pieces,
        ld_sem=dma((5,)),
        out_sem=dma((2, 2)),
        end_sem=dma((4,)),
        w_ss=dma((1,)), w_rs=dma((1,)),
        c_ss=dma((2,)), c_rs=dma((2,)),
    )
    for name in ("b", "e", "d", "x"):
        scratch[name + "_ss"] = dma((2, 2))
        scratch[name + "_rs"] = dma((2, 2))
    for name in ("ro", "ao", "ry", "ay", "rh", "ah", "ra", "aa", "hand", "back", "dn", "df"):
        scratch[name + "_ss"] = dma((2,))
        scratch[name + "_rs"] = dma((2,))
    for name in ("sm", "sz", "sf"):
        scratch[name + "_ss"] = dma((1,))
        scratch[name + "_rs"] = dma((1,))
    scratch["turn_sem"] = pltpu.SemaphoreType.REGULAR

    shape = jax.ShapeDtypeStruct
    near = pltpu.VMEM
    act, grads, dense, small, xe, u, dpre, de = pl.pallas_call(
        kernel,
        out_shape=(
            near((2, TZ, OWN, D), bf16),
            near((2, TZ, OWN, D), bf16),
            near((2, DP, CUT, HALF), bf16),
            near((SMALL, D), f32),
            near((2, 2, DP, PAD, D), bf16),
            near((2, 2, ER, D), bf16),
            near((2, 2, ER, D), bf16),
            near((2, 2, DP, PAD, D), bf16),
        ),
        in_specs=[hbm, hbm, vmem, hbm, hbm, vmem, vmem, hbm, hbm, vmem, vmem],
        out_specs=(vmem,) * 8,
        scratch_shapes=list(scratch.values()),
        compiler_params=pltpu.CompilerParams(
            collective_id=0, has_side_effects=True, vmem_limit_bytes=55 * 1024 * 1024
        ),
        name="layers",
    )(
        tokens.reshape(2, TZ, OWN, D), cotangent.reshape(2, TZ, OWN, D), norm_gains,
        w_qkv[0].swapaxes(1, 2), w_attn_out[0], bias_table.swapaxes(1, 2),
        router.swapaxes(1, 2), w_in[0], w_out[0], routes.swapaxes(1, 2), segments,
    )

    inner, outer, act, grads, qkv_grad, attn_grad, gain_grad, router_grad, bias_grad = pl.pallas_call(
        last_outputs,
        out_shape=(
            shape((2, D, D), f32),
            shape((2, D, D), f32),
            shape((2, TZ, OWN, D), bf16),
            shape((ROWS, D), f32),
            shape((3, HF, D), f32),
            shape((HF, D), f32),
            shape((2, D), f32),
            shape((32, D), f32),
            shape((HEADS, 1, 16), f32),
        ),
        in_specs=[vmem] * 8,
        out_specs=(hbm,) * 6 + (vmem,) * 3,
        scratch_shapes=[
            pltpu.VMEM((2, D, D), f32),
            pltpu.VMEM((2, D, D), f32),
            pltpu.VMEM((ROWS, D), f32),
            pltpu.VMEM((D, D), f32),
            dma((18,)),
        ],
        compiler_params=pltpu.CompilerParams(vmem_limit_bytes=20 * 1024 * 1024),
        name="last_outputs",
    )(xe, dpre, u, de, act, grads, dense, small)

    return (
        act.reshape(ROWS, D)[None],
        grads[None],
        gain_grad[None],
        qkv_grad.swapaxes(1, 2)[None],
        attn_grad[None],
        bias_grad.transpose(1, 2, 0),
        router_grad.T[None],
        inner[None],
        outer[None],
    )


def solution(mesh):
    in_specs = (
        P("dp", None),
        P("dp", None),
        P("section", None, None),
        P("section", None, None, "tensor"),
        P("section", "tensor", None),
        P("section", None, "tensor"),
        P("section", None, None),
        P("section", "dp", None, "tensor"),
        P("section", "dp", "tensor", None),
        P("section", "dp", None),
        P("dp", None),
    )
    out_specs = (
        P("section", "dp", None),
        P("section", "dp", None),
        P("section", None, None),
        P("section", None, None, "tensor"),
        P("section", "tensor", None),
        P("section", None, "tensor"),
        P("section", None, None),
        P("section", "dp", None, "tensor"),
        P("section", "dp", "tensor", None),
    )
    return jax.shard_map(body, mesh=mesh, in_specs=in_specs, out_specs=out_specs, check_vma=False)
```
